32 devices in a mesh: replica: 8 (over z, core), tensor: 4 (over y, x).
Axes of the slice: x: 2, y: 2, z: 4, core: 2. Of those that a mesh axis runs over, the one named last changes fastest.
Arguments:
- tokens: bfloat16 [4096, 1024], P('replica'), may hold values from -6 to 6
- targets: bfloat16 [4096, 1024], P('replica'), may hold values from -6 to 6
- row_ids: int32 [8, 3, 512], P('replica'), may hold values from 0 to 511
- anchor: float32 [2, 1024, 4096], P(None, None, 'tensor'), may hold values from -0.1875 to 0.1875
- momentum: float32 [8, 2, 1024, 4096], P('replica', None, None, 'tensor'), may hold values from -4 to 4
- slow: float32 [2, 1024, 4096], P(None, None, 'tensor'), may hold values from -6 to 6
Outputs:
- anchor_new: float32 [2, 1024, 4096], P(None, None, 'tensor')
- slow_new: float32 [2, 1024, 4096], P(None, None, 'tensor')
- momentum_new: float32 [8, 2, 1024, 4096], P('replica', None, None, 'tensor')
The draws below stay inside these ranges and needn't reach their ends.
Inputs may be any that keep to these rules, and one draw needn't show every extreme that they name: `row_ids`: each id names a row within its replica's own block of 512 rows; rows may repeat.
All inputs are finite; a program needn't handle non-finite values.
Results may differ from the reference program's by a relative error of at most 0.008.
Values may be sent and summed in bfloat16 or wider, within the bound.
No kernel may reach another device: no remote copies, remote signals or barrier semaphores. Data moves between devices by JAX's collectives and lax.ppermute only.
A program may use at most 128 MiB of HBM per device.

```python
import jax
import jax.numpy as jnp
from jax import lax

D = 1024
FF = 4096
ROWS = 512
INNER = 3
REPLICAS = 8
TOKENS = 4096
N_REPLICA = 8


def with_ends(array, rng, least, top_value):
    longest = array.shape.index(max(array.shape))
    spots = []
    for shift in (0, 1):
        where = [jax.random.randint(jax.random.fold_in(rng, axis), (), 0, length) for axis, length in enumerate(array.shape)]
        where[longest] = (where[longest] + shift) % array.shape[longest]
        spots.append(tuple(where))
    return array.at[spots[0]].set(least).at[spots[1]].set(top_value)


def steps_of(own_key, dims, shards, least, largest):
    def one(position, shards_of):
        draws = jax.random.uniform(jax.random.fold_in(jax.random.fold_in(own_key, 6), position), (shards_of,), jnp.float32, least / len(shards), largest / len(shards))
        return jnp.repeat(jnp.exp(draws), dims[position] // shards_of).reshape((-1,) + (1,) * (len(dims) - position - 1))

    loudness = one(*shards[0])
    for cut in shards[1:]:
        loudness = loudness * one(*cut)
    return loudness


def bell_draw(key, shape, scale, limit, shards=(), kind=jnp.bfloat16):
    values = scale * jax.random.normal(key, shape, jnp.float32)
    if shards:
        values = values * steps_of(key, shape, shards, -0.22, 0.18)
    return jnp.clip(values, -limit, limit).astype(kind)


def setup_inputs(seed: int = 0) -> dict:
    splits = jax.random.split(jax.random.key(seed), 7)
    tokens = bell_draw(splits[0], (TOKENS, D), 1.0, 6.0, ((0, 8),))
    targets = bell_draw(splits[1], (TOKENS, D), 1.0, 6.0, ((0, 8),))
    row_ids = with_ends(jax.random.randint(splits[2], (REPLICAS, INNER, ROWS), 0, ROWS), jax.random.fold_in(splits[2], 1), 0, ROWS - 1).astype(jnp.int32)
    anchor = bell_draw(splits[3], (2, D, FF), D ** -0.5, 0.1875, ((2, 4),), jnp.float32)
    momentum = bell_draw(splits[4], (REPLICAS, 2, D, FF), 0.5, 4.0, ((0, 8), (3, 4)), jnp.float32)
    slow = bell_draw(splits[5], (2, D, FF), 1.0, 6.0, ((2, 4),), jnp.float32)
    return dict(tokens=tokens, targets=targets, row_ids=row_ids, anchor=anchor, momentum=momentum, slow=slow)


learn_rate = 0.02
inner_beta = 0.9
slow_beta = 0.5

def gelu_pair(pre):
    coeff = 0.7978845608028654
    inner = coeff * (pre + 0.044715 * pre * pre * pre)
    tanh_val = jnp.tanh(inner)
    value = 0.5 * pre * (1.0 + tanh_val)
    slope = 0.5 * (1.0 + tanh_val) + 0.5 * pre * (1.0 - tanh_val * tanh_val) * coeff * (1.0 + 3.0 * 0.044715 * pre * pre)
    return (value, slope)

def replica_grad(args):
    weights_bf, inputs, wanted = args
    pre = jnp.dot(inputs, weights_bf[0], preferred_element_type=jnp.float32)
    value, slope = gelu_pair(pre)
    hidden = value.astype(jnp.bfloat16)
    out = lax.dot_general(hidden, weights_bf[1], (((1,), (1,)), ((), ())), preferred_element_type=jnp.float32)
    error = ((out - wanted.astype(jnp.float32)) * (1.0 / ROWS)).astype(jnp.bfloat16)
    back = (jnp.dot(error, weights_bf[1], preferred_element_type=jnp.float32) * slope).astype(jnp.bfloat16)
    grad_in = lax.dot_general(inputs, back, (((0,), (0,)), ((), ())), preferred_element_type=jnp.float32)
    grad_out = lax.dot_general(error, hidden, (((0,), (0,)), ((), ())), preferred_element_type=jnp.float32)
    return jnp.stack([grad_in, grad_out])

def reference(tokens, targets, row_ids, anchor, momentum, slow):
    blocks_in = tokens.reshape(REPLICAS, ROWS, D)
    blocks_out = targets.reshape(REPLICAS, ROWS, D)
    weights = jnp.broadcast_to(anchor[None], (REPLICAS,) + anchor.shape).astype(jnp.float32)
    moment = momentum
    for step in range(INNER):
        if step > 0:
            incoming = jnp.roll(weights.astype(jnp.bfloat16), 2 ** (step - 1), axis=0)
            weights = 0.5 * (weights + incoming.astype(jnp.float32))
        picks = row_ids[:, step, :][:, :, None]
        inputs = jnp.take_along_axis(blocks_in, picks, axis=1)
        wanted = jnp.take_along_axis(blocks_out, picks, axis=1)
        weights_bf = weights.astype(jnp.bfloat16)
        grads = lax.map(replica_grad, (weights_bf, inputs, wanted))
        moment = inner_beta * moment + grads
        weights = weights - learn_rate * moment
    mean = lax.optimization_barrier(jnp.sum(weights, axis=0)) / N_REPLICA
    slow_new = slow_beta * slow + (anchor - mean) / learn_rate
    anchor_new = anchor - learn_rate * slow_new
    return (anchor_new, slow_new, moment)
```

```python
import jax
import jax.numpy as jnp
from jax import lax
from jax.sharding import PartitionSpec as P

INNER = 3


learn_rate = 0.02
inner_beta = 0.9
slow_beta = 0.5
chunks = 4


def passed_along(block, axis, distance):
    devices = range(lax.axis_size(axis))
    route = [((i - distance) % len(devices), i) for i in devices]
    return lax.ppermute(block, axis, route)


def swapped(block, axis, mask):
    return lax.ppermute(block, axis, [(i, i ^ mask) for i in range(lax.axis_size(axis))])


def gelu_pair(pre):
    coeff = 0.7978845608028654
    inner = coeff * (pre + 0.044715 * pre * pre * pre)
    tanh_val = jnp.tanh(inner)
    value = 0.5 * pre * (1.0 + tanh_val)
    slope = 0.5 * (1.0 + tanh_val) + 0.5 * pre * (1.0 - tanh_val * tanh_val) * coeff * (
        1.0 + 3.0 * 0.044715 * pre * pre
    )
    return (value, slope)


def rounded(value):
    return lax.reduce_precision(value, 8, 7).astype(jnp.bfloat16)


def added(left, right):
    return rounded(left.astype(jnp.float32) + right.astype(jnp.float32))


def line_sum(block, axis):
    cores = 2
    length = lax.axis_size(axis) // cores
    chip = lax.axis_index(axis) // cores

    def moved(part, hops):
        return lax.ppermute(part, axis, [(cores * a + c, cores * b + c) for a, b in hops for c in range(cores)])

    half = length // 2
    for s in range(half - 1):
        block = added(block, moved(block, [(s, s + 1), (length - 1 - s, length - 2 - s)]))
    if half:
        block = added(block, moved(block, [(half - 1, half), (half, half - 1)]))
    for s in reversed(range(half - 1)):
        arrived = moved(block, [(s + 1, s), (length - 2 - s, length - 1 - s)])
        block = jnp.where((chip == s) | (chip == length - 1 - s), arrived, block)
    return block


def replica_sum(total):
    core = lax.axis_index("replica") % 2
    mine = lax.dynamic_index_in_dim(total, core, 0, keepdims=False)
    other = lax.dynamic_index_in_dim(total, 1 - core, 0, keepdims=False)
    size = mine.shape[0] // chunks
    sums = []
    for c in range(chunks):
        part = slice(c * size, (c + 1) * size)
        pair = added(mine[part], swapped(rounded(other[part]), "replica", 1))
        own = line_sum(pair, "replica")
        theirs = swapped(own, "replica", 1)
        sums.append(jnp.stack([jnp.where(core == 0, own, theirs), jnp.where(core == 0, theirs, own)]))
    return jnp.concatenate(sums, axis=1)


def body(tokens, targets, row_ids, anchor, momentum, slow):
    row_count = tokens.shape[0]
    scale = 1.0 / row_count
    tensors = lax.axis_size("tensor")
    share_rows = row_count // tensors
    order = lax.axis_index("tensor") ^ jnp.arange(tensors)
    picks_all = row_ids[0].reshape(INNER, tensors, share_rows)[:, order].reshape(INNER, row_count)
    weights = anchor
    moment = momentum[0]
    total = 0.0
    for step in range(INNER):
        if step > 0:
            incoming = passed_along(weights.astype(jnp.bfloat16), "replica", 2 ** (step - 1))
            weights = 0.5 * (weights + incoming.astype(jnp.float32))
        picks = picks_all[step]
        inputs = tokens.at[picks].get(mode="promise_in_bounds")
        wanted = targets.at[picks[:share_rows]].get(mode="promise_in_bounds")
        weights_bf = weights.astype(jnp.bfloat16)
        pre = jnp.dot(inputs, weights_bf[0], preferred_element_type=jnp.float32)
        value, slope = gelu_pair(pre)
        hidden = value.astype(jnp.bfloat16)
        partial_out = lax.dot_general(
            hidden, weights_bf[1], (((1,), (1,)), ((), ())), preferred_element_type=jnp.float32
        )
        share = partial_out[:share_rows]
        for m in range(1, tensors):
            piece = partial_out[m * share_rows : (m + 1) * share_rows].astype(jnp.bfloat16)
            share = share + swapped(piece, "tensor", m).astype(jnp.float32)
        error_share = ((share - wanted.astype(jnp.float32)) * scale).astype(jnp.bfloat16)
        error = jnp.concatenate([error_share] + [swapped(error_share, "tensor", m) for m in range(1, tensors)])
        back = (jnp.dot(error, weights_bf[1], preferred_element_type=jnp.float32) * slope).astype(
            jnp.bfloat16
        )
        grad_in = lax.dot_general(
            inputs, back, (((0,), (0,)), ((), ())), preferred_element_type=jnp.float32
        )
        grad_out = lax.dot_general(
            error, hidden, (((0,), (0,)), ((), ())), preferred_element_type=jnp.float32
        )
        moment = inner_beta * moment + jnp.stack([grad_in, grad_out])
        weights = weights - learn_rate * moment
        total = total + moment
    replicas = lax.axis_size("replica")
    mean_total = replica_sum(total).astype(jnp.float32) / replicas
    slow_new = slow_beta * slow + mean_total
    anchor_new = anchor - learn_rate * slow_new
    return (anchor_new, slow_new, moment[None])


def solution(mesh):
    return jax.shard_map(
        body,
        mesh=mesh,
        in_specs=(
            P("replica", None),
            P("replica", None),
            P("replica", None, None),
            P(None, None, "tensor"),
            P("replica", None, None, "tensor"),
            P(None, None, "tensor"),
        ),
        out_specs=(
            P(None, None, "tensor"),
            P(None, None, "tensor"),
            P("replica", None, None, "tensor"),
        ),
        check_vma=False,
    )
```

```python
import functools

import jax
import jax.numpy as jnp
from jax import lax
from jax.experimental import pallas as pl
from jax.experimental.pallas import tpu as pltpu
from jax.sharding import PartitionSpec as P

INNER = 3


learn_rate = 0.02
inner_beta = 0.9
slow_beta = 0.5
chunks = 8
bf16, f32 = jnp.bfloat16, jnp.float32


def passed_along(block, axis, distance):
    devices = range(lax.axis_size(axis))
    route = [((i - distance) % len(devices), i) for i in devices]
    return lax.ppermute(block, axis, route)


def swapped(block, axis, mask):
    return lax.ppermute(block, axis, [(i, i ^ mask) for i in range(lax.axis_size(axis))])


def gelu_pair(pre):
    coeff = 0.7978845608028654
    square = pre * pre
    tanh_val = jnp.tanh(coeff * (pre + 0.044715 * square * pre))
    half = 0.5 * (1.0 + tanh_val)
    slope = half + 0.5 * pre * (1.0 - tanh_val * tanh_val) * coeff * (1.0 + 3.0 * 0.044715 * square)
    return (pre * half, slope)


def whole(shape):
    return pl.BlockSpec(shape, lambda j: (0,) * len(shape))


def forward_kernel(mixes, inputs, weights, *refs):
    if mixes:
        incoming, hidden, slope, partial, mixed, total = refs
        block = (0.5 * (weights[...].astype(f32) + incoming[...].astype(f32))).astype(bf16)
        mixed[...] = block
    else:
        hidden, slope, partial, total = refs
        block = weights[...].astype(bf16)
    j = pl.program_id(0)
    value, slope_val = gelu_pair(jnp.dot(inputs[...], block[0], preferred_element_type=f32))
    value = value.astype(bf16)
    hidden[...] = value
    slope[...] = slope_val.astype(bf16)
    out = lax.dot_general(value, block[1], (((1,), (1,)), ((), ())), preferred_element_type=f32)

    @pl.when(j == 0)
    def _():
        total[...] = out

    @pl.when(j > 0)
    def _():
        total[...] += out

    @pl.when(j == pl.num_programs(0) - 1)
    def _():
        partial[...] = total[...].astype(bf16)


def forward(inputs, weights, incoming=None):
    rows, width = inputs.shape
    units = weights.shape[2]
    block = min(units, 512)
    mixes = incoming is not None
    weight_spec = pl.BlockSpec((2, width, block), lambda j: (0, 0, j))
    unit_spec = pl.BlockSpec((rows, block), lambda j: (0, j))
    shapes = [((rows, units), unit_spec), ((rows, units), unit_spec), ((rows, width), whole((rows, width)))]
    if mixes:
        shapes.append((weights.shape, weight_spec))
    return pl.pallas_call(
        functools.partial(forward_kernel, mixes),
        grid=(units // block,),
        in_specs=[whole((rows, width)), weight_spec] + [weight_spec] * mixes,
        out_specs=[spec for _, spec in shapes],
        out_shape=[jax.ShapeDtypeStruct(shape, bf16) for shape, _ in shapes],
        scratch_shapes=[pltpu.VMEM((rows, width), f32)],
        compiler_params=pltpu.CompilerParams(vmem_limit_bytes=40 << 20),
        cost_estimate=pl.CostEstimate(
            flops=4 * rows * width * units, bytes_accessed=8 * width * units, transcendentals=rows * units
        ),
    )(inputs, weights, *([incoming] if mixes else []))


def backward_kernel(update, taken, error, weights, slope, hidden, inputs_t, *refs):
    states, results, error_t = refs[:taken], refs[taken:-1], refs[-1]

    @pl.when(pl.program_id(0) == 0)
    def _():
        error_t[...] = error[...].T

    back = jnp.dot(error[...], weights[0].astype(bf16), preferred_element_type=f32) * slope[...].astype(f32)
    for k, (left, right) in enumerate(((inputs_t[...], back.astype(bf16)), (error_t[...], hidden[...]))):
        grad = jnp.dot(left, right, preferred_element_type=f32)
        values = update(grad, *[state[k].astype(f32) for state in states])
        for result, value in zip(results, values):
            result[k] = value.astype(result.dtype)


def backward(error, weights, slope, hidden, inputs_t, states, update, kinds):
    rows, width = error.shape
    units = weights.shape[2]
    block = min(units, 512)
    both = pl.BlockSpec((2, width, block), lambda j: (0, 0, j))
    out_only = pl.BlockSpec((1, width, block), lambda j: (1, 0, j))
    unit_spec = pl.BlockSpec((rows, block), lambda j: (0, j))
    return pl.pallas_call(
        functools.partial(backward_kernel, update, len(states)),
        grid=(units // block,),
        in_specs=[whole((rows, width)), out_only, unit_spec, unit_spec, whole((width, rows))] + [both] * len(states),
        out_specs=[both] * len(kinds),
        out_shape=[jax.ShapeDtypeStruct(weights.shape, kind) for kind in kinds],
        scratch_shapes=[pltpu.VMEM((width, rows), bf16)],
        compiler_params=pltpu.CompilerParams(vmem_limit_bytes=56 << 20),
        cost_estimate=pl.CostEstimate(
            flops=6 * rows * width * units, bytes_accessed=28 * width * units, transcendentals=0
        ),
    )(error, weights, slope, hidden, inputs_t, *states)


def first_update(grad, moment, weights):
    moment = inner_beta * moment + grad
    return (moment, weights - learn_rate * moment)


def second_update(grad, moment, weights):
    moment_new = inner_beta * moment + grad
    return (moment_new, weights - learn_rate * moment_new, moment + (1.0 + inner_beta) * moment_new)


def third_update(grad, moment, known):
    return (inner_beta * moment + grad, known + grad)


def rounded(value):
    return lax.reduce_precision(value, 8, 7).astype(bf16)


def added(left, right):
    return rounded(left.astype(f32) + right.astype(f32))


def tied(early, late):
    return lax.optimization_barrier((early, late))[1]


def replica_sum(total):
    axis, cores = "replica", 2
    index = lax.axis_index(axis)
    core, chip = index % cores, index // cores
    length = lax.axis_size(axis) // cores
    half = length // 2
    mine = lax.dynamic_index_in_dim(total, core, 0, keepdims=False)
    other = lax.dynamic_index_in_dim(total, 1 - core, 0, keepdims=False)
    size = mine.shape[0] // chunks

    def moved(part, hops):
        return lax.ppermute(part, axis, [(cores * a + c, cores * b + c) for a, b in hops for c in range(cores)])

    stages = [("add", [(s, s + 1), (length - 1 - s, length - 2 - s)]) for s in range(half - 1)]
    if half:
        stages.append(("add", [(half - 1, half), (half, half - 1)]))
    stages += [("take", [(s + 1, s), (length - 2 - s, length - 1 - s)]) for s in reversed(range(half - 1))]

    blocks = []
    for c in range(chunks):
        part = slice(c * size, (c + 1) * size)
        blocks.append(added(mine[part], swapped(other[part], axis, 1)))
    ticks = []
    for tick in range(chunks + 2 * (len(stages) - 1)):
        work = [(tick - 2 * s, s) for s in range(len(stages)) if 0 <= tick - 2 * s < chunks]
        if tick >= 2:
            held = tied(ticks[tick - 2], [blocks[c] for c, _ in work])
            for (c, _), block in zip(work, held):
                blocks[c] = block
        arrivals = [moved(blocks[c], stages[s][1]) for c, s in work]
        ticks.append(arrivals)
        for (c, s), arrived in zip(work, arrivals):
            kind, hops = stages[s]
            if kind == "add":
                blocks[c] = added(blocks[c], arrived)
            else:
                landed = functools.reduce(jnp.logical_or, [chip == b for _, b in hops])
                blocks[c] = jnp.where(landed, arrived, blocks[c])
    sums = []
    for own in blocks:
        theirs = swapped(own, axis, 1)
        sums.append(jnp.stack([jnp.where(core == 0, own, theirs), jnp.where(core == 0, theirs, own)]))
    return jnp.concatenate(sums, axis=1)


def body(tokens, targets, row_ids, anchor, momentum, slow):
    row_count = tokens.shape[0]
    scale = 1.0 / row_count
    tensors = lax.axis_size("tensor")
    share_rows = row_count // tensors
    order = lax.axis_index("tensor") ^ jnp.arange(tensors)
    picks_all = row_ids[0].reshape(INNER, tensors, share_rows)[:, order].reshape(INNER, row_count)

    def error_of(partial, step):
        wanted = targets.at[picks_all[step, :share_rows]].get(mode="promise_in_bounds")
        share = partial[:share_rows].astype(f32)
        for m in range(1, tensors):
            share = share + swapped(partial[m * share_rows : (m + 1) * share_rows], "tensor", m).astype(f32)
        own = ((share - wanted.astype(f32)) * scale).astype(bf16)
        return jnp.concatenate([own] + [swapped(own, "tensor", m) for m in range(1, tensors)])

    inputs = [tokens.at[picks_all[step]].get(mode="promise_in_bounds") for step in range(INNER)]
    inputs_t = [block.T for block in inputs]

    hidden, slope, partial = forward(inputs[0], anchor)
    error = error_of(partial, 0)
    moment, weights = backward(
        error, anchor, slope, hidden, inputs_t[0], [momentum[0], anchor], first_update, [f32, bf16]
    )
    incoming = passed_along(weights, "replica", 1)
    hidden, slope, partial, weights = forward(inputs[1], weights, incoming)
    error = error_of(partial, 1)
    moment, weights, known = backward(
        error, weights, slope, hidden, inputs_t[1], [moment, weights], second_update, [f32, bf16, bf16]
    )
    incoming = passed_along(weights, "replica", 2)
    hidden, slope, partial, weights = forward(inputs[2], weights, incoming)
    error = error_of(partial, 2)
    moment, total = backward(
        error, weights, slope, hidden, inputs_t[2], [moment, known], third_update, [f32, bf16]
    )
    mean_total = replica_sum(total).astype(f32) / lax.axis_size("replica")
    slow_new = slow_beta * slow + mean_total
    anchor_new = anchor - learn_rate * slow_new
    return (anchor_new, slow_new, moment[None])


def solution(mesh):
    return jax.shard_map(
        body,
        mesh=mesh,
        in_specs=(
            P("replica", None),
            P("replica", None),
            P("replica", None, None),
            P(None, None, "tensor"),
            P("replica", None, None, "tensor"),
            P(None, None, "tensor"),
        ),
        out_specs=(
            P(None, None, "tensor"),
            P(None, None, "tensor"),
            P("replica", None, None, "tensor"),
        ),
        check_vma=False,
    )
```

```python
import functools

import jax
import jax.numpy as jnp
from jax import lax
from jax.experimental import pallas as pl
from jax.experimental.pallas import tpu as pltpu
from jax.sharding import PartitionSpec as P

INNER = 3


learn_rate = 0.02
inner_beta = 0.9
slow_beta = 0.5
chunks = 8
bf16, f32 = jnp.bfloat16, jnp.float32


def swapped(block, axis, mask):
    return lax.ppermute(block, axis, [(i, i ^ mask) for i in range(lax.axis_size(axis))])


def gelu_pair(pre):
    coeff = 0.7978845608028654
    square = pre * pre
    tanh_val = jnp.tanh(coeff * (pre + 0.044715 * square * pre))
    half = 0.5 * (1.0 + tanh_val)
    slope = half + 0.5 * pre * (1.0 - tanh_val * tanh_val) * coeff * (1.0 + 3.0 * 0.044715 * square)
    return (pre * half, slope)


def whole(shape):
    return pl.BlockSpec(shape, lambda j: (0,) * len(shape))


def forward_kernel(mix, taken, sums, emits, flag, inputs, *refs):
    sources, refs = refs[:taken], list(refs[taken:])
    hidden, slope = refs[:2]
    block = mix(flag[0], *[source[...].astype(f32) for source in sources]).astype(bf16)
    if emits:
        refs[2 + sums][...] = block
    j = pl.program_id(0)
    value, slope_val = gelu_pair(jnp.dot(inputs[...], block[0], preferred_element_type=f32))
    value = value.astype(bf16)
    hidden[...] = value
    slope[...] = slope_val.astype(bf16)
    if sums:
        partial, total = refs[2], refs[-1]
        out = lax.dot_general(value, block[1], (((1,), (1,)), ((), ())), preferred_element_type=f32)

        @pl.when(j == 0)
        def _():
            total[...] = out

        @pl.when(j > 0)
        def _():
            total[...] += out

        @pl.when(j == pl.num_programs(0) - 1)
        def _():
            partial[...] = total[...].astype(bf16)


def forward(flag, inputs, sources, mix, sums=True, emits=True):
    rows, width = inputs.shape
    units = sources[0].shape[2]
    block = min(units, 512)
    parts = 2 if sums or emits else 1
    weight_spec = pl.BlockSpec((parts, width, block), lambda j: (0, 0, j))
    unit_spec = pl.BlockSpec((rows, block), lambda j: (0, j))
    shapes = [((rows, units), unit_spec), ((rows, units), unit_spec)]
    shapes += [((rows, width), whole((rows, width)))] * sums + [(sources[0].shape, weight_spec)] * emits
    return pl.pallas_call(
        functools.partial(forward_kernel, mix, len(sources), sums, emits),
        grid=(units // block,),
        in_specs=[pl.BlockSpec(memory_space=pltpu.SMEM), whole((rows, width))] + [weight_spec] * len(sources),
        out_specs=[spec for _, spec in shapes],
        out_shape=[jax.ShapeDtypeStruct(shape, bf16) for shape, _ in shapes],
        scratch_shapes=[pltpu.VMEM((rows, width), f32)] * sums,
        compiler_params=pltpu.CompilerParams(vmem_limit_bytes=48 << 20),
        cost_estimate=pl.CostEstimate(
            flops=(2 + 2 * sums) * rows * width * units,
            bytes_accessed=16 * width * units,
            transcendentals=rows * units,
        ),
    )(flag, inputs, *sources)


def only(flag, weights):
    return weights


def pushed(flag, weights, first, second):
    return weights - 0.5 * learn_rate * (first + second)


def halved(flag, weights, sent, found):
    return 0.5 * (weights + jnp.where(flag == 0, sent, found))


def backward_kernel(update, taken, error, weights, slope, hidden, inputs_t, *refs):
    states, results, error_t = refs[:taken], refs[taken:-1], refs[-1]

    @pl.when(pl.program_id(0) == 0)
    def _():
        error_t[...] = error[...].T

    back = jnp.dot(error[...], weights[0].astype(bf16), preferred_element_type=f32) * slope[...].astype(f32)
    for k, (left, right) in enumerate(((inputs_t[...], back.astype(bf16)), (error_t[...], hidden[...]))):
        grad = jnp.dot(left, right, preferred_element_type=f32)
        values = update(grad, *[state[k].astype(f32) for state in states])
        for result, value in zip(results, values):
            result[k] = value.astype(result.dtype)


def backward(error, weights, slope, hidden, inputs_t, states, update, kinds):
    rows, width = error.shape
    units = weights.shape[2]
    block = min(units, 512)
    both = pl.BlockSpec((2, width, block), lambda j: (0, 0, j))
    out_only = pl.BlockSpec((1, width, block), lambda j: (1, 0, j))
    unit_spec = pl.BlockSpec((rows, block), lambda j: (0, j))
    return pl.pallas_call(
        functools.partial(backward_kernel, update, len(states)),
        grid=(units // block,),
        in_specs=[whole((rows, width)), out_only, unit_spec, unit_spec, whole((width, rows))] + [both] * len(states),
        out_specs=[both] * len(kinds),
        out_shape=[jax.ShapeDtypeStruct(weights.shape, kind) for kind in kinds],
        scratch_shapes=[pltpu.VMEM((width, rows), bf16)],
        compiler_params=pltpu.CompilerParams(vmem_limit_bytes=56 << 20),
        cost_estimate=pl.CostEstimate(
            flops=6 * rows * width * units, bytes_accessed=28 * width * units, transcendentals=0
        ),
    )(error, weights, slope, hidden, inputs_t, *states)


def first_update(grad, moment):
    moment = inner_beta * moment + grad
    return (moment, moment)


def first_beside(grad, moment, own_moment, weights):
    moment = inner_beta * moment + grad
    return (moment, weights - 0.5 * learn_rate * (own_moment + moment))


def second_update(grad, moment, weights):
    moment_new = inner_beta * moment + grad
    return (moment_new, weights - learn_rate * moment_new, moment + (1.0 + inner_beta) * moment_new)


def second_beside(grad, moment, weights):
    return (weights - learn_rate * (inner_beta * moment + grad),)


def third_update(grad, moment, known):
    return (inner_beta * moment + grad, known + grad)


def rounded(value):
    return lax.reduce_precision(value, 8, 7).astype(bf16)


def added(left, right):
    return rounded(left.astype(f32) + right.astype(f32))


def tied(early, late):
    return lax.optimization_barrier((early, late))[1]


def replica_sum(total):
    axis, cores = "replica", 2
    index = lax.axis_index(axis)
    core, chip = index % cores, index // cores
    length = lax.axis_size(axis) // cores
    half = length // 2
    mine = lax.dynamic_index_in_dim(total, core, 0, keepdims=False)
    other = lax.dynamic_index_in_dim(total, 1 - core, 0, keepdims=False)
    size = mine.shape[0] // chunks

    def moved(part, hops):
        return lax.ppermute(part, axis, [(cores * a + c, cores * b + c) for a, b in hops for c in range(cores)])

    stages = [("add", [(s, s + 1), (length - 1 - s, length - 2 - s)]) for s in range(half - 1)]
    if half:
        stages.append(("add", [(half - 1, half), (half, half - 1)]))
    stages += [("take", [(s + 1, s), (length - 2 - s, length - 1 - s)]) for s in reversed(range(half - 1))]

    blocks = []
    for c in range(chunks):
        part = slice(c * size, (c + 1) * size)
        blocks.append(added(mine[part], swapped(other[part], axis, 1)))
    ticks = []
    for tick in range(chunks + 2 * (len(stages) - 1)):
        work = [(tick - 2 * s, s) for s in range(len(stages)) if 0 <= tick - 2 * s < chunks]
        if tick >= 2:
            held = tied(ticks[tick - 2], [blocks[c] for c, _ in work])
            for (c, _), block in zip(work, held):
                blocks[c] = block
        arrivals = [moved(blocks[c], stages[s][1]) for c, s in work]
        ticks.append(arrivals)
        for (c, s), arrived in zip(work, arrivals):
            kind, hops = stages[s]
            if kind == "add":
                blocks[c] = added(blocks[c], arrived)
            else:
                landed = functools.reduce(jnp.logical_or, [chip == b for _, b in hops])
                blocks[c] = jnp.where(landed, arrived, blocks[c])
    sums = []
    for own in blocks:
        theirs = swapped(own, axis, 1)
        sums.append(jnp.stack([jnp.where(core == 0, own, theirs), jnp.where(core == 0, theirs, own)]))
    return jnp.concatenate(sums, axis=1)


def body(tokens, targets, row_ids, anchor, momentum, slow):
    row_count = tokens.shape[0]
    scale = 1.0 / row_count
    tensors = lax.axis_size("tensor")
    share_rows = row_count // tensors
    order = lax.axis_index("tensor") ^ jnp.arange(tensors)
    picks_all = row_ids[0].reshape(INNER, tensors, share_rows)[:, order].reshape(INNER, row_count)

    def error_of(partial, step):
        wanted = targets.at[picks_all[step, :share_rows]].get(mode="promise_in_bounds")
        share = partial[:share_rows].astype(f32)
        for m in range(1, tensors):
            share = share + swapped(partial[m * share_rows : (m + 1) * share_rows], "tensor", m).astype(f32)
        own = ((share - wanted.astype(f32)) * scale).astype(bf16)
        return jnp.concatenate([own] + [swapped(own, "tensor", m) for m in range(1, tensors)])

    replicas = lax.axis_size("replica")
    flag = (lax.axis_index("replica") % 2).astype(jnp.int32).reshape(1)

    def sent(block, distance, which=(0, 1)):
        route = [((i - distance) % replicas, i) for i in range(replicas) if i % 2 in which]
        return lax.ppermute(block, "replica", route)

    inputs = [tokens.at[picks_all[step]].get(mode="promise_in_bounds") for step in range(INNER)]
    inputs_t = [block.T for block in inputs]

    inputs_near = sent(inputs[0], 1)
    moment_near = sent(momentum[0].astype(bf16), 1)
    hidden, slope, partial = forward(flag, inputs[0], [anchor], only, emits=False)
    error = error_of(partial, 0)
    error_near = sent(error, 1)
    moment, moment_bf = backward(error, anchor, slope, hidden, inputs_t[0], [momentum[0]], first_update, [f32, bf16])
    moment_far = sent(moment_bf, 2, (0,))
    hidden, slope = forward(flag, inputs_near, [anchor], only, sums=False, emits=False)
    moment_near, weights = backward(
        error_near, anchor, slope, hidden, inputs_near.T, [moment_near, moment, anchor], first_beside, [bf16, bf16]
    )

    inputs_far = sent(tied(error_near, inputs[1]), 2, (1,))
    hidden, slope, partial = forward(flag, inputs[1], [weights], only, emits=False)
    error = error_of(partial, 1)
    error_far = sent(error, 2, (1,))
    moment, weights, known = backward(
        error, weights, slope, hidden, inputs_t[1], [moment, weights], second_update, [f32, bf16, bf16]
    )
    weights_sent = sent(weights, 2, (0,))
    moment_two = sent(moment_near, 1, (1,))
    moment_three = sent(moment_far, 1, (1,))
    inputs_far = tied(weights, inputs_far)
    hidden, slope, weights_far = forward(flag, inputs_far, [anchor, moment_two, moment_three], pushed, sums=False)
    (weights_found,) = backward(
        error_far, weights_far, slope, hidden, inputs_far.T, [moment_two, weights_far], second_beside, [bf16]
    )

    hidden, slope, partial, weights = forward(flag, inputs[2], [weights, weights_sent, weights_found], halved)
    error = error_of(partial, 2)
    moment, total = backward(
        error, weights, slope, hidden, inputs_t[2], [moment, known], third_update, [f32, bf16]
    )
    mean_total = replica_sum(total).astype(f32) / replicas
    slow_new = slow_beta * slow + mean_total
    anchor_new = anchor - learn_rate * slow_new
    return (anchor_new, slow_new, moment[None])


def solution(mesh):
    return jax.shard_map(
        body,
        mesh=mesh,
        in_specs=(
            P("replica", None),
            P("replica", None),
            P("replica", None, None),
            P(None, None, "tensor"),
            P("replica", None, None, "tensor"),
            P(None, None, "tensor"),
        ),
        out_specs=(
            P(None, None, "tensor"),
            P(None, None, "tensor"),
            P("replica", None, None, "tensor"),
        ),
        check_vma=False,
    )
```

```python
import functools

import jax
import jax.numpy as jnp
from jax import lax
from jax.experimental import pallas as pl
from jax.experimental.pallas import tpu as pltpu
from jax.sharding import PartitionSpec as P

INNER = 3


learn_rate = 0.02
inner_beta = 0.9
slow_beta = 0.5
chunks = 8
bf16, f32 = jnp.bfloat16, jnp.float32


def swapped(block, axis, mask):
    return lax.ppermute(block, axis, [(i, i ^ mask) for i in range(lax.axis_size(axis))])


def gelu_pair(pre):
    coeff = 0.7978845608028654
    square = pre * pre
    tanh_val = jnp.tanh(coeff * (pre + 0.044715 * square * pre))
    half = 0.5 * (1.0 + tanh_val)
    slope = half + 0.5 * pre * (1.0 - tanh_val * tanh_val) * coeff * (1.0 + 3.0 * 0.044715 * square)
    return (pre * half, slope)


def whole(shape):
    return pl.BlockSpec(shape, lambda j: (0,) * len(shape))


def forward_kernel(mix, taken, sums, emits, flag, inputs, *refs):
    sources, refs = refs[:taken], list(refs[taken:])
    hidden, slope = refs[:2]
    block = mix(flag[0], *[source[...].astype(f32) for source in sources]).astype(bf16)
    if emits:
        refs[2 + sums][...] = block
    j = pl.program_id(0)
    value, slope_val = gelu_pair(jnp.dot(inputs[...], block[0], preferred_element_type=f32))
    value = value.astype(bf16)
    hidden[...] = value
    slope[...] = slope_val.astype(bf16)
    if sums:
        partials, total = refs[2 : 2 + sums], refs[-1]
        out = lax.dot_general(value, block[1], (((1,), (1,)), ((), ())), preferred_element_type=f32)

        @pl.when(j == 0)
        def _():
            total[...] = out

        @pl.when(j > 0)
        def _():
            total[...] += out

        @pl.when(j == pl.num_programs(0) - 1)
        def _():
            size = partials[0].shape[0]
            for b, partial in enumerate(partials):
                partial[...] = total[b * size : (b + 1) * size].astype(bf16)


def forward(flag, inputs, sources, mix, sums, emits=True):
    rows, width = inputs.shape
    units = sources[0].shape[2]
    block = min(units, 512)
    parts = 2 if sums or emits else 1
    weight_spec = pl.BlockSpec((parts, width, block), lambda j: (0, 0, j))
    unit_spec = pl.BlockSpec((rows, block), lambda j: (0, j))
    shapes = [((rows, units), unit_spec), ((rows, units), unit_spec)]
    if sums:
        shapes += [((rows // sums, width), whole((rows // sums, width)))] * sums
    shapes += [(sources[0].shape, weight_spec)] * emits
    return pl.pallas_call(
        functools.partial(forward_kernel, mix, len(sources), sums, emits),
        grid=(units // block,),
        in_specs=[pl.BlockSpec(memory_space=pltpu.SMEM), whole((rows, width))] + [weight_spec] * len(sources),
        out_specs=[spec for _, spec in shapes],
        out_shape=[jax.ShapeDtypeStruct(shape, bf16) for shape, _ in shapes],
        scratch_shapes=[pltpu.VMEM((rows, width), f32)] * bool(sums),
        compiler_params=pltpu.CompilerParams(vmem_limit_bytes=48 << 20),
        cost_estimate=pl.CostEstimate(
            flops=(2 + 2 * bool(sums)) * rows * width * units,
            bytes_accessed=16 * width * units,
            transcendentals=rows * units,
        ),
    )(flag, inputs, *sources)


def only(flag, weights):
    return weights


def pushed(flag, weights, first, second):
    return weights - 0.5 * learn_rate * (first + second)


def halved(flag, weights, sent, found):
    return 0.5 * (weights + jnp.where(flag == 0, sent, found))


def backward_kernel(update, taken, pieces, weights, slope, hidden, inputs_t, *refs):
    states, refs = refs[:taken], refs[taken:]
    errors, results, error, error_t = refs[:pieces], refs[pieces:-2], refs[-2], refs[-1]

    @pl.when(pl.program_id(0) == 0)
    def _():
        size = errors[0].shape[0]
        for b, piece in enumerate(errors):
            error[b * size : (b + 1) * size] = piece[...]
        error_t[...] = error[...].T

    back = jnp.dot(error[...], weights[0].astype(bf16), preferred_element_type=f32) * slope[...].astype(f32)
    for k, (left, right) in enumerate(((inputs_t[...], back.astype(bf16)), (error_t[...], hidden[...]))):
        grad = jnp.dot(left, right, preferred_element_type=f32)
        values = update(grad, *[state[k].astype(f32) for state in states])
        for result, value in zip(results, values):
            result[k] = value.astype(result.dtype)


def backward(errors, weights, slope, hidden, inputs_t, states, update, kinds):
    width, rows = inputs_t.shape
    units = weights.shape[2]
    block = min(units, 512)
    both = pl.BlockSpec((2, width, block), lambda j: (0, 0, j))
    out_only = pl.BlockSpec((1, width, block), lambda j: (1, 0, j))
    unit_spec = pl.BlockSpec((rows, block), lambda j: (0, j))
    return pl.pallas_call(
        functools.partial(backward_kernel, update, len(states), len(errors)),
        grid=(units // block,),
        in_specs=[out_only, unit_spec, unit_spec, whole((width, rows))]
        + [both] * len(states)
        + [whole(piece.shape) for piece in errors],
        out_specs=[both] * len(kinds),
        out_shape=[jax.ShapeDtypeStruct(weights.shape, kind) for kind in kinds],
        scratch_shapes=[pltpu.VMEM((rows, width), bf16), pltpu.VMEM((width, rows), bf16)],
        compiler_params=pltpu.CompilerParams(vmem_limit_bytes=56 << 20),
        cost_estimate=pl.CostEstimate(
            flops=6 * rows * width * units, bytes_accessed=28 * width * units, transcendentals=0
        ),
    )(weights, slope, hidden, inputs_t, *states, *errors)


def first_update(grad, moment):
    moment = inner_beta * moment + grad
    return (moment, moment)


def first_beside(grad, moment, own_moment, weights):
    moment = inner_beta * moment + grad
    return (moment, weights - 0.5 * learn_rate * (own_moment + moment))


def second_update(grad, moment, weights):
    moment_new = inner_beta * moment + grad
    return (moment_new, weights - learn_rate * moment_new, moment + (1.0 + inner_beta) * moment_new)


def second_beside(grad, moment, weights):
    return (weights - learn_rate * (inner_beta * moment + grad),)


def third_update(grad, moment, known):
    return (inner_beta * moment + grad, known + grad)


def rounded(value):
    return lax.reduce_precision(value, 8, 7).astype(bf16)


def added(left, right):
    return rounded(left.astype(f32) + right.astype(f32))


def tied(early, late):
    return lax.optimization_barrier((early, late))[1]


def finish_kernel(replicas, flag, slow, anchor, own, theirs, *refs):
    anchor_new, slow_new = refs[-2:]
    for k in range(2):
        total = jnp.where(flag[0] == k, own[...].astype(f32), theirs[...].astype(f32))
        value = slow_beta * slow[k] + total / replicas
        slow_new[k] = value
        anchor_new[k] = anchor[k] - learn_rate * value


def finish(flag, replicas, slow, anchor, own, theirs, position, before):
    size, units = own.shape
    rows = pl.BlockSpec((2, size, units), lambda j: (0, position, 0))
    shape = jax.ShapeDtypeStruct(slow.shape, f32)
    return pl.pallas_call(
        functools.partial(finish_kernel, replicas),
        grid=(1,),
        in_specs=[pl.BlockSpec(memory_space=pltpu.SMEM), rows, rows, whole(own.shape), whole(own.shape)]
        + [pl.BlockSpec(memory_space=pl.ANY)] * len(before),
        out_specs=[rows, rows],
        out_shape=[shape, shape],
        input_output_aliases={5 + k: k for k in range(len(before))},
        compiler_params=pltpu.CompilerParams(vmem_limit_bytes=32 << 20),
        cost_estimate=pl.CostEstimate(flops=8 * size * units, bytes_accessed=36 * size * units, transcendentals=0),
    )(flag, slow, anchor, own, theirs, *before)


def slow_step(flag, total, slow, anchor):
    axis, cores = "replica", 2
    index = lax.axis_index(axis)
    replicas = lax.axis_size(axis)
    core, chip = index % cores, index // cores
    length = replicas // cores
    half = length // 2
    mine = lax.dynamic_index_in_dim(total, core, 0, keepdims=False)
    other = lax.dynamic_index_in_dim(total, 1 - core, 0, keepdims=False)
    size = mine.shape[0] // chunks

    def moved(part, hops):
        return lax.ppermute(part, axis, [(cores * a + c, cores * b + c) for a, b in hops for c in range(cores)])

    def at(*places):
        return functools.reduce(jnp.logical_or, [chip == place for place in places])

    blocks = []
    for c in range(chunks):
        part = slice(c * size, (c + 1) * size)
        blocks.append(added(mine[part], swapped(other[part], axis, 1)))
    lag = 2
    middle = lag * max(half - 1, 0)
    last = chunks - 1 + 2 * middle
    ticks, results = [], []
    for tick in range(last + 1):
        live = list(range(max(0, tick - 2 * middle), min(chunks, tick + 1)))
        if tick >= lag:
            for c, block in zip(live, tied(ticks[tick - lag], [blocks[c] for c in live])):
                blocks[c] = block
        arrivals, steps = [], []
        for s in range(half):
            inward = tick - lag * s
            outward = inward if s == half - 1 else tick - 2 * middle + lag * s
            inward = inward if 0 <= inward < chunks else None
            outward = outward if 0 <= outward < chunks else None
            if inward is None and outward is None:
                continue
            if s == half - 1:
                arrived = moved(blocks[inward], [(s, s + 1), (s + 1, s)])
            else:
                hops = []
                if inward is not None:
                    hops += [(s, s + 1), (length - 1 - s, length - 2 - s)]
                if outward is not None:
                    hops += [(s + 1, s), (length - 2 - s, length - 1 - s)]
                if inward is None or outward is None:
                    sent = blocks[outward if inward is None else inward]
                else:
                    sent = jnp.where(at(s, length - 1 - s), blocks[inward], blocks[outward])
                arrived = moved(sent, hops)
            arrivals.append(arrived)
            steps.append((s, inward, outward))
        ticks.append(arrivals)
        for (s, inward, outward), arrived in zip(steps, arrivals):
            if s == half - 1:
                blocks[inward] = jnp.where(at(s, s + 1), added(blocks[inward], arrived), blocks[inward])
                continue
            if inward is not None:
                blocks[inward] = jnp.where(at(s + 1, length - 2 - s), added(blocks[inward], arrived), blocks[inward])
            if outward is not None:
                blocks[outward] = jnp.where(at(s, length - 1 - s), arrived, blocks[outward])
        if tick >= 2 * middle:
            done = tick - 2 * middle
            theirs = swapped(blocks[done], axis, 1)
            results = finish(flag, replicas, slow, anchor, blocks[done], theirs, done, results)
    return results


def body(tokens, targets, row_ids, anchor, momentum, slow):
    row_count = tokens.shape[0]
    scale = 1.0 / row_count
    tensors = lax.axis_size("tensor")
    share_rows = row_count // tensors
    order = lax.axis_index("tensor") ^ jnp.arange(tensors)
    picks_all = row_ids[0].reshape(INNER, tensors, share_rows)[:, order].reshape(INNER, row_count)

    replicas = lax.axis_size("replica")
    flag = (lax.axis_index("replica") % 2).astype(jnp.int32).reshape(1)

    def errors_of(partials, step):
        wanted = targets.at[picks_all[step, :share_rows]].get(mode="promise_in_bounds")
        share = partials[0].astype(f32)
        for m in range(1, tensors):
            share = share + swapped(partials[m], "tensor", m).astype(f32)
        own = ((share - wanted.astype(f32)) * scale).astype(bf16)
        return [own] + [swapped(own, "tensor", m) for m in range(1, tensors)]

    def sent(block, distance, which=(0, 1)):
        route = [((i - distance) % replicas, i) for i in range(replicas) if i % 2 in which]
        return lax.ppermute(block, "replica", route)

    inputs = [tokens.at[picks_all[step]].get(mode="promise_in_bounds") for step in range(INNER)]
    inputs_t = [block.T for block in inputs]

    inputs_near = sent(inputs[0], 1)
    moment_near = sent(momentum[0].astype(bf16), 1)
    hidden, slope, *partials = forward(flag, inputs[0], [anchor], only, tensors, emits=False)
    partials = tied(inputs_near, partials)
    error = jnp.concatenate(errors_of(partials, 0))
    error_near = sent(error, 1)
    moment, moment_bf = backward([error], anchor, slope, hidden, inputs_t[0], [momentum[0]], first_update, [f32, bf16])
    moment_far = sent(tied(error_near, moment_bf), 2, (0,))
    hidden, slope = forward(flag, inputs_near, [anchor], only, 0, emits=False)
    moment_near, weights = backward(
        [error_near], anchor, slope, hidden, inputs_near.T, [moment_near, moment, anchor], first_beside, [bf16, bf16]
    )

    inputs_far = sent(tied(error_near, inputs[1]), 2, (1,))
    hidden, slope, *partials = forward(flag, inputs[1], [weights], only, tensors, emits=False)
    error = jnp.concatenate(errors_of(partials, 1))
    error = tied(inputs_far, error)
    error_far = sent(error, 2, (1,))
    moment, weights, known = backward(
        [error], weights, slope, hidden, inputs_t[1], [moment, weights], second_update, [f32, bf16, bf16]
    )
    weights_sent = sent(tied(error_far, weights), 2, (0,))
    moment_two = sent(moment_near, 1, (1,))
    moment_three = sent(moment_far, 1, (1,))
    inputs_far = tied(weights, inputs_far)
    hidden, slope, weights_far = forward(flag, inputs_far, [anchor, moment_two, moment_three], pushed, 0)
    (weights_found,) = backward(
        [error_far], weights_far, slope, hidden, inputs_far.T, [moment_two, weights_far], second_beside, [bf16]
    )

    hidden, slope, *rest = forward(flag, inputs[2], [weights, weights_sent, weights_found], halved, tensors)
    errors = errors_of(rest[:tensors], 2)
    moment, total = backward(
        errors, rest[tensors], slope, hidden, inputs_t[2], [moment, known], third_update, [f32, bf16]
    )
    anchor_new, slow_new = slow_step(flag, total, slow, anchor)
    return (anchor_new, slow_new, moment[None])


def solution(mesh):
    return jax.shard_map(
        body,
        mesh=mesh,
        in_specs=(
            P("replica", None),
            P("replica", None),
            P("replica", None, None),
            P(None, None, "tensor"),
            P("replica", None, None, "tensor"),
            P(None, None, "tensor"),
        ),
        out_specs=(
            P(None, None, "tensor"),
            P(None, None, "tensor"),
            P("replica", None, None, "tensor"),
        ),
        check_vma=False,
    )
```

```python
import functools

import jax
import jax.numpy as jnp
from jax import lax
from jax.experimental import pallas as pl
from jax.experimental.pallas import tpu as pltpu
from jax.sharding import PartitionSpec as P

INNER = 3


learn_rate = 0.02
inner_beta = 0.9
slow_beta = 0.5
chunks = 8
bf16, f32 = jnp.bfloat16, jnp.float32


def swapped(block, axis, mask):
    return lax.ppermute(block, axis, [(i, i ^ mask) for i in range(lax.axis_size(axis))])


def gelu_pair(pre):
    coeff = 0.7978845608028654
    square = pre * pre
    tanh_val = jnp.tanh(coeff * (pre + 0.044715 * square * pre))
    half = 0.5 * (1.0 + tanh_val)
    slope = half + 0.5 * pre * (1.0 - tanh_val * tanh_val) * coeff * (1.0 + 3.0 * 0.044715 * square)
    return (pre * half, slope)


def whole(shape):
    return pl.BlockSpec(shape, lambda j: (0,) * len(shape))


def forward_kernel(mix, taken, sums, emits, flag, inputs, *refs):
    sources, refs = refs[:taken], list(refs[taken:])
    hidden, slope = refs[:2]
    block = mix(flag[0], *[source[...].astype(f32) for source in sources]).astype(bf16)
    if emits:
        refs[2 + sums][...] = block
    j = pl.program_id(0)
    value, slope_val = gelu_pair(jnp.dot(inputs[...], block[0], preferred_element_type=f32))
    value = value.astype(bf16)
    hidden[...] = value
    slope[...] = slope_val.astype(bf16)
    if sums:
        partials, total = refs[2 : 2 + sums], refs[-1]
        out = lax.dot_general(value, block[1], (((1,), (1,)), ((), ())), preferred_element_type=f32)

        @pl.when(j == 0)
        def _():
            total[...] = out

        @pl.when(j > 0)
        def _():
            total[...] += out

        @pl.when(j == pl.num_programs(0) - 1)
        def _():
            size = partials[0].shape[0]
            for b, partial in enumerate(partials):
                partial[...] = total[b * size : (b + 1) * size].astype(bf16)


def forward(flag, inputs, sources, mix, sums, emits=True):
    rows, width = inputs.shape
    units = sources[0].shape[2]
    block = min(units, 512)
    parts = 2 if sums or emits else 1
    weight_spec = pl.BlockSpec((parts, width, block), lambda j: (0, 0, j))
    unit_spec = pl.BlockSpec((rows, block), lambda j: (0, j))
    shapes = [((rows, units), unit_spec), ((rows, units), unit_spec)]
    if sums:
        shapes += [((rows // sums, width), whole((rows // sums, width)))] * sums
    shapes += [(sources[0].shape, weight_spec)] * emits
    return pl.pallas_call(
        functools.partial(forward_kernel, mix, len(sources), sums, emits),
        grid=(units // block,),
        in_specs=[pl.BlockSpec(memory_space=pltpu.SMEM), whole((rows, width))] + [weight_spec] * len(sources),
        out_specs=[spec for _, spec in shapes],
        out_shape=[jax.ShapeDtypeStruct(shape, bf16) for shape, _ in shapes],
        scratch_shapes=[pltpu.VMEM((rows, width), f32)] * bool(sums),
        compiler_params=pltpu.CompilerParams(vmem_limit_bytes=48 << 20),
        cost_estimate=pl.CostEstimate(
            flops=(2 + 2 * bool(sums)) * rows * width * units,
            bytes_accessed=16 * width * units,
            transcendentals=rows * units,
        ),
    )(flag, inputs, *sources)


def only(flag, weights):
    return weights


def pushed(flag, weights, first, second):
    return weights - 0.5 * learn_rate * (first + second)


def halved(flag, weights, sent, found):
    return 0.5 * (weights + jnp.where(flag == 0, sent, found))


def backward_kernel(update, taken, pieces, weights, slope, hidden, inputs_t, *refs):
    states, refs = [], list(refs)
    for split in taken:
        states.append(tuple(refs[:2]) if split else refs[0])
        del refs[: 1 + split]
    errors, results, error, error_t = refs[:pieces], refs[pieces:-2], refs[-2], refs[-1]

    @pl.when(pl.program_id(0) == 0)
    def _():
        size = errors[0].shape[0]
        for b, piece in enumerate(errors):
            error[b * size : (b + 1) * size] = piece[...]
        error_t[...] = error[...].T

    back = jnp.dot(error[...], weights[0].astype(bf16), preferred_element_type=f32) * slope[...].astype(f32)
    for k, (left, right) in enumerate(((inputs_t[...], back.astype(bf16)), (error_t[...], hidden[...]))):
        grad = jnp.dot(left, right, preferred_element_type=f32)
        values = update(grad, *[(state[k] if type(state) is tuple else state.at[k])[...].astype(f32) for state in states])
        for result, value in zip(results, values):
            result[k] = value.astype(result.dtype)


def backward(errors, weights, slope, hidden, inputs_t, states, update, kinds):
    width, rows = inputs_t.shape
    units = weights.shape[2]
    block = min(units, 512)
    both = pl.BlockSpec((2, width, block), lambda j: (0, 0, j))
    half = pl.BlockSpec((width, block), lambda j: (0, j))
    out_only = pl.BlockSpec((1, width, block), lambda j: (1, 0, j))
    split = [type(state) is tuple for state in states]
    flat = [part for state in states for part in (state if type(state) is tuple else (state,))]
    unit_spec = pl.BlockSpec((rows, block), lambda j: (0, j))
    return pl.pallas_call(
        functools.partial(backward_kernel, update, split, len(errors)),
        grid=(units // block,),
        in_specs=[out_only, unit_spec, unit_spec, whole((width, rows))]
        + [half if part.ndim == 2 else both for part in flat]
        + [whole(piece.shape) for piece in errors],
        out_specs=[both] * len(kinds),
        out_shape=[jax.ShapeDtypeStruct(weights.shape, kind) for kind in kinds],
        scratch_shapes=[pltpu.VMEM((rows, width), bf16), pltpu.VMEM((width, rows), bf16)],
        compiler_params=pltpu.CompilerParams(vmem_limit_bytes=56 << 20),
        cost_estimate=pl.CostEstimate(
            flops=6 * rows * width * units, bytes_accessed=28 * width * units, transcendentals=0
        ),
    )(weights, slope, hidden, inputs_t, *flat, *errors)


def first_update(grad, moment):
    moment = inner_beta * moment + grad
    return (moment, moment)


def first_beside(grad, moment, own_moment, weights):
    moment = inner_beta * moment + grad
    return (moment, weights - 0.5 * learn_rate * (own_moment + moment))


def second_update(grad, moment, weights):
    moment_new = inner_beta * moment + grad
    return (moment_new, weights - learn_rate * moment_new, moment + (1.0 + inner_beta) * moment_new)


def second_beside(grad, moment, weights):
    return (weights - learn_rate * (inner_beta * moment + grad),)


def third_update(grad, moment, known):
    return (inner_beta * moment + grad, known + grad)


def rounded(value):
    return lax.reduce_precision(value, 8, 7).astype(bf16)


def added(left, right):
    return rounded(left.astype(f32) + right.astype(f32))


def tied(early, late):
    return lax.optimization_barrier((early, late))[1]


def finish_kernel(replicas, flag, slow, anchor, own, theirs, *refs):
    anchor_new, slow_new, token = refs[-3:]
    for k in range(2):
        total = jnp.where(flag[0] == k, own[...].astype(f32), theirs[...].astype(f32))
        value = slow_beta * slow[k] + total / replicas
        slow_new[k] = value
        anchor_new[k] = anchor[k] - learn_rate * value
    token[...] = jnp.zeros_like(token)


def finish(flag, replicas, slow, anchor, own, theirs, position, before):
    size, units = own.shape
    rows = pl.BlockSpec((2, size, units), lambda j: (0, position, 0))
    shape = jax.ShapeDtypeStruct(slow.shape, f32)
    return pl.pallas_call(
        functools.partial(finish_kernel, replicas),
        grid=(1,),
        in_specs=[pl.BlockSpec(memory_space=pltpu.SMEM), rows, rows, whole(own.shape), whole(own.shape)]
        + [pl.BlockSpec(memory_space=pl.ANY)] * len(before),
        out_specs=[rows, rows, whole((8, 128))],
        out_shape=[shape, shape, jax.ShapeDtypeStruct((8, 128), bf16)],
        input_output_aliases={5 + k: k for k in range(len(before))},
        compiler_params=pltpu.CompilerParams(vmem_limit_bytes=32 << 20),
        cost_estimate=pl.CostEstimate(flops=8 * size * units, bytes_accessed=36 * size * units, transcendentals=0),
    )(flag, slow, anchor, own, theirs, *before)


def slow_step(flag, total, slow, anchor):
    axis, cores = "replica", 2
    index = lax.axis_index(axis)
    replicas = lax.axis_size(axis)
    core, chip = index % cores, index // cores
    length = replicas // cores
    half = length // 2
    mine = lax.dynamic_index_in_dim(total, core, 0, keepdims=False)
    other = lax.dynamic_index_in_dim(total, 1 - core, 0, keepdims=False)
    rows = mine.shape[0]
    size = rows // chunks

    def moved(part, hops):
        return lax.ppermute(part, axis, [(cores * a + c, cores * b + c) for a, b in hops for c in range(cores)])

    def at(places):
        return functools.reduce(jnp.logical_or, [chip == place for place in places])

    stages = [(True, [(s, s + 1), (length - 1 - s, length - 2 - s)]) for s in range(half - 1)]
    if half:
        stages.append((True, [(half - 1, half), (half, half - 1)]))
    stages += [(False, [(s + 1, s), (length - 2 - s, length - 1 - s)]) for s in reversed(range(half - 1))]

    pair_rows = rows // 2
    pairs = [swapped(other[p * pair_rows : (p + 1) * pair_rows], axis, 1) for p in range(2)]
    blocks = []
    for c in range(chunks):
        p, start = divmod(c * size, pair_rows)
        blocks.append(added(mine[c * size : (c + 1) * size], pairs[p][start : start + size]))
    arrived = {}
    tokens, results = {}, []
    for tick in range(chunks + 2 * len(stages) + 1):
        for s in range(len(stages) + 1):
            c = tick - 2 * s
            if not 0 <= c < chunks:
                continue
            if s:
                adds, hops = stages[s - 1]
                fresh = added(blocks[c], arrived[s - 1, c]) if adds else arrived[s - 1, c]
                blocks[c] = jnp.where(at([b for _, b in hops]), fresh, blocks[c])
            if s < len(stages):
                block = blocks[c]
                if s:
                    if (s + 1, c - 4) in arrived:
                        block = tied(arrived[s + 1, c - 4], block)
                    if s == len(stages) - 1 and (c - 4) // 2 in tokens:
                        block = tied(tokens[(c - 4) // 2], block)
                arrived[s, c] = moved(block, stages[s][1])
            elif c % 2:
                own = jnp.concatenate(blocks[c - 1 : c + 1])
                *results, tokens[c // 2] = finish(
                    flag, replicas, slow, anchor, own, swapped(own, axis, 1), c // 2, results
                )
    return results


def body(tokens, targets, row_ids, anchor, momentum, slow):
    row_count = tokens.shape[0]
    scale = 1.0 / row_count
    tensors = lax.axis_size("tensor")
    share_rows = row_count // tensors
    order = lax.axis_index("tensor") ^ jnp.arange(tensors)
    picks_all = row_ids[0].reshape(INNER, tensors, share_rows)[:, order].reshape(INNER, row_count)

    replicas = lax.axis_size("replica")
    flag = (lax.axis_index("replica") % 2).astype(jnp.int32).reshape(1)

    def gathered(own):
        return [own] + [swapped(own, "tensor", m) for m in range(1, tensors)]

    def error_share(partials, step):
        wanted = targets.at[picks_all[step, :share_rows]].get(mode="promise_in_bounds")
        share = partials[0].astype(f32)
        for m in range(1, tensors):
            share = share + swapped(partials[m], "tensor", m).astype(f32)
        return ((share - wanted.astype(f32)) * scale).astype(bf16)

    def sent(block, distance, which=(0, 1)):
        route = [((i - distance) % replicas, i) for i in range(replicas) if i % 2 in which]
        return lax.ppermute(block, "replica", route)

    def picked(step, count):
        return tokens.at[picks_all[step, :count]].get(mode="promise_in_bounds")

    near_share = sent(picked(0, share_rows), 1)
    far_share = sent(picked(1, share_rows), 2, (1,))
    moment_near_in = sent(tied(near_share, momentum[0, 0]).astype(bf16), 1)
    inputs_near = jnp.concatenate(gathered(near_share))

    inputs = picked(0, row_count)
    hidden, slope, *partials = forward(flag, inputs, [anchor], only, tensors, emits=False)
    own_error = error_share(tied(inputs_near, partials), 0)
    error_near = sent(own_error, 1)
    moment_near_out = sent(tied(own_error, momentum[0, 1]).astype(bf16), 1)
    hidden_near, slope_near = forward(flag, inputs_near, [anchor], only, 0, emits=False)
    errors = tied(hidden_near, gathered(own_error))
    moment, moment_bf = backward(errors, anchor, slope, hidden, inputs.T, [momentum[0]], first_update, [f32, bf16])
    errors_near = gathered(error_near)
    moment_far = sent(moment_bf, 2, (0,))
    moment_near, weights = backward(
        errors_near,
        anchor,
        slope_near,
        hidden_near,
        inputs_near.T,
        [(moment_near_in, moment_near_out), moment, anchor],
        first_beside,
        [bf16, bf16],
    )

    inputs_far = jnp.concatenate(gathered(tied(errors_near, far_share)))
    inputs = picked(1, row_count)
    hidden, slope, *partials = forward(flag, inputs, [weights], only, tensors, emits=False)
    own_error = error_share(tied(inputs_far, partials), 1)
    error_far = sent(own_error, 2, (1,))
    moment, weights, known = backward(
        gathered(own_error), weights, slope, hidden, inputs.T, [moment, weights], second_update, [f32, bf16, bf16]
    )
    weights_sent = sent(weights, 2, (0,))
    moment_two, moment_three, error_far = tied(weights, (moment_near, moment_far, error_far))
    moment_two = sent(moment_two, 1, (1,))
    moment_three = sent(moment_three, 1, (1,))
    hidden, slope, weights_far = forward(flag, inputs_far, [anchor, moment_two, moment_three], pushed, 0)
    (weights_found,) = backward(
        gathered(error_far), weights_far, slope, hidden, inputs_far.T, [moment_two, weights_far], second_beside, [bf16]
    )

    inputs = picked(2, row_count)
    hidden, slope, *rest = forward(flag, inputs, [weights, weights_sent, weights_found], halved, tensors)
    errors = gathered(error_share(rest[:tensors], 2))
    moment, total = backward(
        errors, rest[tensors], slope, hidden, inputs.T, [moment, known], third_update, [f32, bf16]
    )
    anchor_new, slow_new = slow_step(flag, total, slow, anchor)
    return (anchor_new, slow_new, moment[None])


def solution(mesh):
    return jax.shard_map(
        body,
        mesh=mesh,
        in_specs=(
            P("replica", None),
            P("replica", None),
            P("replica", None, None),
            P(None, None, "tensor"),
            P("replica", None, None, "tensor"),
            P(None, None, "tensor"),
        ),
        out_specs=(
            P(None, None, "tensor"),
            P(None, None, "tensor"),
            P("replica", None, None, "tensor"),
        ),
        check_vma=False,
    )
```

```python
import functools

import jax
import jax.numpy as jnp
from jax import lax
from jax.experimental import pallas as pl
from jax.experimental.pallas import tpu as pltpu
from jax.sharding import PartitionSpec as P

INNER = 3


learn_rate = 0.02
inner_beta = 0.9
slow_beta = 0.5
chunks = 8
bf16, f32 = jnp.bfloat16, jnp.float32


def swapped(block, axis, mask):
    return lax.ppermute(block, axis, [(i, i ^ mask) for i in range(lax.axis_size(axis))])


def gelu_pair(pre):
    coeff = 0.7978845608028654
    square = pre * pre
    tanh_val = jnp.tanh(coeff * (pre + 0.044715 * square * pre))
    half = 0.5 * (1.0 + tanh_val)
    slope = half + 0.5 * pre * (1.0 - tanh_val * tanh_val) * coeff * (1.0 + 3.0 * 0.044715 * square)
    return (pre * half, slope)


def whole(shape):
    return pl.BlockSpec(shape, lambda j: (0,) * len(shape))


def loaded(state, k):
    if type(state) is not tuple:
        return state[k].astype(f32)
    each = len(state) // 2
    return jnp.concatenate([piece[...].astype(f32) for piece in state[k * each : (k + 1) * each]], axis=0)


def regrouped(refs, counts):
    refs, states = list(refs), []
    for count in counts:
        states.append(tuple(refs[:count]) if count > 1 else refs[0])
        del refs[:count]
    return states, refs


def flattened(states):
    flat = [state if type(state) is tuple else (state,) for state in states]
    return [len(state) for state in flat], [part for state in flat for part in state]


def block_of(part, block, parts=2):
    if part.ndim == 2:
        return pl.BlockSpec((part.shape[0], block), lambda j: (0, j))
    return pl.BlockSpec((parts, part.shape[1], block), lambda j: (0, 0, j))


def forward_kernel(mix, taken, sums, emits, flag, inputs, *refs):
    sources, refs = regrouped(refs, taken)
    hidden, slope = refs[:2]
    block = [mix(flag[0], *[loaded(source, k) for source in sources]).astype(bf16) for k in range(2 if sums or emits else 1)]
    if emits:
        for k in range(2):
            refs[2 + sums][k] = block[k]
    j = pl.program_id(0)
    value, slope_val = gelu_pair(jnp.dot(inputs[...], block[0], preferred_element_type=f32))
    value = value.astype(bf16)
    hidden[...] = value
    slope[...] = slope_val.astype(bf16)
    if sums:
        partials, total = refs[2 : 2 + sums], refs[-1]
        out = lax.dot_general(value, block[1], (((1,), (1,)), ((), ())), preferred_element_type=f32)

        @pl.when(j == 0)
        def _():
            total[...] = out

        @pl.when(j > 0)
        def _():
            total[...] += out

        @pl.when(j == pl.num_programs(0) - 1)
        def _():
            size = partials[0].shape[0]
            for b, partial in enumerate(partials):
                partial[...] = total[b * size : (b + 1) * size].astype(bf16)


def forward(flag, inputs, sources, mix, sums, emits=True):
    rows, width = inputs.shape
    units = sources[0].shape[2]
    block = min(units, 512)
    parts = 2 if sums or emits else 1
    counts, flat = flattened(sources)
    unit_spec = pl.BlockSpec((rows, block), lambda j: (0, j))
    shapes = [((rows, units), unit_spec), ((rows, units), unit_spec)]
    if sums:
        shapes += [((rows // sums, width), whole((rows // sums, width)))] * sums
    shapes += [(sources[0].shape, block_of(sources[0], block))] * emits
    return pl.pallas_call(
        functools.partial(forward_kernel, mix, counts, sums, emits),
        grid=(units // block,),
        in_specs=[pl.BlockSpec(memory_space=pltpu.SMEM), whole((rows, width))]
        + [block_of(part, block, parts) for part in flat],
        out_specs=[spec for _, spec in shapes],
        out_shape=[jax.ShapeDtypeStruct(shape, bf16) for shape, _ in shapes],
        scratch_shapes=[pltpu.VMEM((rows, width), f32)] * bool(sums),
        compiler_params=pltpu.CompilerParams(vmem_limit_bytes=48 << 20),
        cost_estimate=pl.CostEstimate(
            flops=(2 + 2 * bool(sums)) * rows * width * units,
            bytes_accessed=16 * width * units,
            transcendentals=rows * units,
        ),
    )(flag, inputs, *flat)


def only(flag, weights):
    return weights


def pushed(flag, weights, first, second):
    return weights - 0.5 * learn_rate * (first + second)


def halved(flag, found, weights, sent):
    return 0.5 * (weights + jnp.where(flag == 0, sent, found))


def backward_kernel(update, taken, pieces, given, weights, slope, hidden, inputs_t, *refs):
    states, refs = regrouped(refs, taken)
    errors, refs, error, error_t = refs[:pieces], refs[pieces:-2], refs[-2], refs[-1]
    results, _ = regrouped(refs, given)

    @pl.when(pl.program_id(0) == 0)
    def _():
        size = errors[0].shape[0]
        for b, piece in enumerate(errors):
            error[b * size : (b + 1) * size] = piece[...]
        error_t[...] = error[...].T

    back = jnp.dot(error[...], weights[0].astype(bf16), preferred_element_type=f32) * slope[...].astype(f32)
    for k, (left, right) in enumerate(((inputs_t[...], back.astype(bf16)), (error_t[...], hidden[...]))):
        grad = jnp.dot(left, right, preferred_element_type=f32)
        values = update(grad, *[loaded(state, k) for state in states])
        for result, value in zip(results, values):
            if type(result) is not tuple:
                result[k] = value.astype(result.dtype)
                continue
            each = len(result) // 2
            for i, piece in enumerate(result[k * each : (k + 1) * each]):
                size = piece.shape[0]
                piece[...] = value[i * size : (i + 1) * size].astype(piece.dtype)


def backward(errors, weights, slope, hidden, inputs_t, states, update, kinds):
    width, rows = inputs_t.shape
    units = weights.shape[2]
    block = min(units, 512)
    counts, flat = flattened(states)
    kinds = [kind if type(kind) is tuple else (kind, 1) for kind in kinds]
    shapes = []
    for kind, count in kinds:
        shape = weights.shape if count == 1 else (2 * width // count, units)
        shapes += [jax.ShapeDtypeStruct(shape, kind)] * count
    results = pl.pallas_call(
        functools.partial(backward_kernel, update, counts, len(errors), [count for _, count in kinds]),
        grid=(units // block,),
        in_specs=[
            pl.BlockSpec((1, width, block), lambda j: (1, 0, j)),
            pl.BlockSpec((rows, block), lambda j: (0, j)),
            pl.BlockSpec((rows, block), lambda j: (0, j)),
            whole((width, rows)),
        ]
        + [block_of(part, block) for part in flat]
        + [whole(piece.shape) for piece in errors],
        out_specs=[block_of(shape, block) for shape in shapes],
        out_shape=shapes,
        scratch_shapes=[pltpu.VMEM((rows, width), bf16), pltpu.VMEM((width, rows), bf16)],
        compiler_params=pltpu.CompilerParams(vmem_limit_bytes=56 << 20),
        cost_estimate=pl.CostEstimate(
            flops=6 * rows * width * units, bytes_accessed=28 * width * units, transcendentals=0
        ),
    )(weights, slope, hidden, inputs_t, *flat, *errors)
    return regrouped(results, [count for _, count in kinds])[0]


def first_update(grad, moment):
    moment = inner_beta * moment + grad
    return (moment, moment)


def first_beside(grad, moment, own_moment, weights):
    moment = inner_beta * moment + grad
    return (moment, weights - 0.5 * learn_rate * (own_moment + moment))


def second_update(grad, moment, weights):
    moment_new = inner_beta * moment + grad
    return (moment_new, weights - learn_rate * moment_new, moment + (1.0 + inner_beta) * moment_new)


def second_beside(grad, moment, weights):
    return (weights - learn_rate * (inner_beta * moment + grad),)


def third_update(grad, moment, known):
    return (inner_beta * moment + grad, known + grad)


def rounded(value):
    return lax.reduce_precision(value, 8, 7).astype(bf16)


def added(left, right):
    return rounded(left.astype(f32) + right.astype(f32))


def tied(early, late):
    return lax.optimization_barrier((early, late))[1]


def finish_kernel(replicas, flag, slow, anchor, own, theirs, *refs):
    anchor_new, slow_new, token = refs[-3:]
    for k in range(2):
        total = jnp.where(flag[0] == k, own[...].astype(f32), theirs[...].astype(f32))
        value = slow_beta * slow[k] + total / replicas
        slow_new[k] = value
        anchor_new[k] = anchor[k] - learn_rate * value
    token[...] = jnp.zeros_like(token)


def finish(flag, replicas, slow, anchor, own, theirs, position, before):
    size, units = own.shape
    rows = pl.BlockSpec((2, size, units), lambda j: (0, position, 0))
    shape = jax.ShapeDtypeStruct(slow.shape, f32)
    return pl.pallas_call(
        functools.partial(finish_kernel, replicas),
        grid=(1,),
        in_specs=[pl.BlockSpec(memory_space=pltpu.SMEM), rows, rows, whole(own.shape), whole(own.shape)]
        + [pl.BlockSpec(memory_space=pl.ANY)] * len(before),
        out_specs=[rows, rows, whole((8, 128))],
        out_shape=[shape, shape, jax.ShapeDtypeStruct((8, 128), bf16)],
        input_output_aliases={5 + k: k for k in range(len(before))},
        compiler_params=pltpu.CompilerParams(vmem_limit_bytes=32 << 20),
        cost_estimate=pl.CostEstimate(flops=8 * size * units, bytes_accessed=36 * size * units, transcendentals=0),
    )(flag, slow, anchor, own, theirs, *before)


def slow_step(flag, total, slow, anchor):
    axis, cores = "replica", 2
    index = lax.axis_index(axis)
    replicas = lax.axis_size(axis)
    core, chip = index % cores, index // cores
    length = replicas // cores
    half = length // 2
    mine = lax.dynamic_index_in_dim(total, core, 0, keepdims=False)
    other = lax.dynamic_index_in_dim(total, 1 - core, 0, keepdims=False)
    rows = mine.shape[0]
    size = rows // chunks

    def moved(part, hops):
        return lax.ppermute(part, axis, [(cores * a + c, cores * b + c) for a, b in hops for c in range(cores)])

    def at(places):
        return functools.reduce(jnp.logical_or, [chip == place for place in places])

    stages = [(True, [(s, s + 1), (length - 1 - s, length - 2 - s)]) for s in range(half - 1)]
    if half:
        stages.append((True, [(half - 1, half), (half, half - 1)]))
    stages += [(False, [(s + 1, s), (length - 2 - s, length - 1 - s)]) for s in reversed(range(half - 1))]

    pair_rows = rows // 2
    pairs = [swapped(other[p * pair_rows : (p + 1) * pair_rows], axis, 1) for p in range(2)]
    blocks = []
    for c in range(chunks):
        p, start = divmod(c * size, pair_rows)
        blocks.append(added(mine[c * size : (c + 1) * size], pairs[p][start : start + size]))
    arrived = {}
    tokens, results = {}, []
    final = len(stages) - 1

    def after(block, *waits):
        waits = [arrived.get(wait, tokens.get(wait)) for wait in waits]
        waits = [wait for wait in waits if wait is not None]
        return tied(waits, block) if waits else block

    for tick in range(chunks + 2 * len(stages) + 1):
        for s in reversed(range(len(stages) + 1)):
            c = tick - 2 * s
            if not 0 <= c < chunks:
                continue
            if s:
                adds, hops = stages[s - 1]
                fresh = added(blocks[c], arrived[s - 1, c]) if adds else arrived[s - 1, c]
                blocks[c] = jnp.where(at([b for _, b in hops]), fresh, blocks[c])
            if s < len(stages):
                block = blocks[c]
                if s == 0:
                    block = after(block, (0, c - 2), *((t, c - 1 - 2 * t) for t in range(1, len(stages))))
                elif s < final:
                    block = after(block, (s + 1, c - 3))
                else:
                    block = after(block, (c - 4) // 2)
                arrived[s, c] = moved(block, stages[s][1])
            elif c % 2:
                own = jnp.concatenate(blocks[c - 1 : c + 1])
                *results, tokens[c // 2] = finish(
                    flag, replicas, slow, anchor, own, swapped(own, axis, 1), c // 2, results
                )
    return results


def body(tokens, targets, row_ids, anchor, momentum, slow):
    row_count = tokens.shape[0]
    scale = 1.0 / row_count
    tensors = lax.axis_size("tensor")
    share_rows = row_count // tensors
    order = lax.axis_index("tensor") ^ jnp.arange(tensors)
    picks_all = row_ids[0].reshape(INNER, tensors, share_rows)[:, order].reshape(INNER, row_count)

    replicas = lax.axis_size("replica")
    flag = (lax.axis_index("replica") % 2).astype(jnp.int32).reshape(1)

    def gathered(own):
        return [own] + [swapped(own, "tensor", m) for m in range(1, tensors)]

    def error_share(partials, step):
        wanted = targets.at[picks_all[step, :share_rows]].get(mode="promise_in_bounds")
        share = partials[0].astype(f32)
        for m in range(1, tensors):
            share = share + swapped(partials[m], "tensor", m).astype(f32)
        return ((share - wanted.astype(f32)) * scale).astype(bf16)

    def sent(block, distance, which=(0, 1)):
        route = [((i - distance) % replicas, i) for i in range(replicas) if i % 2 in which]
        return lax.ppermute(block, "replica", route)

    def picked(step, count):
        return tokens.at[picks_all[step, :count]].get(mode="promise_in_bounds")

    near_rows = picked(0, share_rows)
    near_share = sent(near_rows, 1)
    far_share = sent(picked(1, share_rows), 2, (1,))
    quarter = anchor.shape[1] // 2
    moment_pieces = [momentum[0, k, i * quarter : (i + 1) * quarter] for k in range(2) for i in range(2)]
    moment_near = [sent(tied(near_rows, moment_pieces[0]).astype(bf16), 1)]
    inputs_near = jnp.concatenate(gathered(near_share))

    inputs = picked(0, row_count)
    hidden, slope, *partials = forward(flag, inputs, [anchor], only, tensors, emits=False)
    moment_near.append(sent(tied(near_share, moment_pieces[1]).astype(bf16), 1))
    own_error = error_share(tied((inputs_near, moment_near[0]), partials), 0)
    error_near = sent(own_error, 1)
    moment_near.append(sent(tied(moment_near[0], moment_pieces[2]).astype(bf16), 1))
    hidden_near, slope_near = forward(flag, inputs_near, [anchor], only, 0, emits=False)
    errors = tied((hidden_near, moment_near[1]), gathered(tied(moment_near[0], own_error)))
    moment_near.append(sent(tied(moment_near[1], moment_pieces[3]).astype(bf16), 1))
    errors = tied(moment_near[2], errors)
    moment, moment_bf = backward(errors, anchor, slope, hidden, inputs.T, [momentum[0]], first_update, [f32, (bf16, 4)])
    errors_near = gathered(error_near)
    moment_far = [sent(tied(moment_near[3], piece), 2, (0,)) for piece in moment_bf]
    moment_near, weights = backward(
        errors_near,
        anchor,
        slope_near,
        hidden_near,
        inputs_near.T,
        [tuple(moment_near), moment, anchor],
        first_beside,
        [bf16, bf16],
    )

    weights = tied(moment_far[0], weights)
    inputs = picked(1, row_count)
    hidden, slope, *partials = forward(flag, inputs, [weights], only, tensors, emits=False)
    inputs_far = jnp.concatenate(gathered(tied(errors_near, far_share)))
    own_error = error_share(tied(inputs_far, partials), 1)
    moment_two = sent(tied(weights, moment_near), 1, (1,))
    own_error = tied((moment_far[1], moment_two), own_error)
    error_far = sent(own_error, 2, (1,))
    errors = tied(moment_far[2], gathered(own_error))
    moment, weights, known = backward(
        errors, weights, slope, hidden, inputs.T, [moment, weights], second_update, [f32, (bf16, 2), bf16]
    )
    weights_sent = tuple(sent(part, 2, (0,)) for part in weights)
    errors_far = gathered(tied(weights, error_far))
    moment_three = tuple(sent(tied(weights, piece), 1, (1,)) for piece in moment_far)
    hidden, slope, weights_far = forward(flag, inputs_far, [anchor, moment_two, moment_three], pushed, 0)
    (weights_found,) = backward(
        errors_far, weights_far, slope, hidden, inputs_far.T, [moment_two, weights_far], second_beside, [bf16]
    )

    inputs = picked(2, row_count)
    hidden, slope, *rest = forward(flag, inputs, [weights_found, weights, weights_sent], halved, tensors)
    errors = gathered(error_share(rest[:tensors], 2))
    moment, total = backward(
        errors, rest[tensors], slope, hidden, inputs.T, [moment, known], third_update, [f32, bf16]
    )
    anchor_new, slow_new = slow_step(flag, total, slow, anchor)
    return (anchor_new, slow_new, moment[None])


def solution(mesh):
    return jax.shard_map(
        body,
        mesh=mesh,
        in_specs=(
            P("replica", None),
            P("replica", None),
            P("replica", None, None),
            P(None, None, "tensor"),
            P("replica", None, None, "tensor"),
            P(None, None, "tensor"),
        ),
        out_specs=(
            P(None, None, "tensor"),
            P(None, None, "tensor"),
            P("replica", None, None, "tensor"),
        ),
        check_vma=False,
    )
```

```python
import functools

import jax
import jax.numpy as jnp
from jax import lax
from jax.experimental import pallas as pl
from jax.experimental.pallas import tpu as pltpu
from jax.sharding import PartitionSpec as P

INNER = 3


learn_rate = 0.02
inner_beta = 0.9
slow_beta = 0.5
chunks = 4
bf16, f32 = jnp.bfloat16, jnp.float32


def swapped(block, axis, mask):
    return lax.ppermute(block, axis, [(i, i ^ mask) for i in range(lax.axis_size(axis))])


def gelu_pair(pre):
    coeff = 0.7978845608028654
    square = pre * pre
    tanh_val = jnp.tanh(coeff * (pre + 0.044715 * square * pre))
    half = 0.5 * (1.0 + tanh_val)
    slope = half + 0.5 * pre * (1.0 - tanh_val * tanh_val) * coeff * (1.0 + 3.0 * 0.044715 * square)
    return (pre * half, slope)


def whole(shape):
    return pl.BlockSpec(shape, lambda j: (0,) * len(shape))


def loaded(state, k):
    if type(state) is not tuple:
        return state[k].astype(f32)
    each = len(state) // 2
    return jnp.concatenate([piece[...].astype(f32) for piece in state[k * each : (k + 1) * each]], axis=0)


def regrouped(refs, counts):
    refs, states = list(refs), []
    for count in counts:
        states.append(tuple(refs[:count]) if count > 1 else refs[0])
        del refs[:count]
    return states, refs


def flattened(states):
    flat = [state if type(state) is tuple else (state,) for state in states]
    return [len(state) for state in flat], [part for state in flat for part in state]


def block_of(part, block, parts=2):
    if part.ndim == 2:
        return pl.BlockSpec((part.shape[0], block), lambda j: (0, j))
    return pl.BlockSpec((parts, part.shape[1], block), lambda j: (0, 0, j))


def forward_kernel(mix, taken, sums, emits, flag, inputs, *refs):
    sources, refs = regrouped(refs, taken)
    hidden, slope = refs[:2]
    block = [mix(flag[0], *[loaded(source, k) for source in sources]).astype(bf16) for k in range(2 if sums or emits else 1)]
    if emits:
        for k in range(2):
            refs[2 + sums][k] = block[k]
    j = pl.program_id(0)
    value, slope_val = gelu_pair(jnp.dot(inputs[...], block[0], preferred_element_type=f32))
    value = value.astype(bf16)
    hidden[...] = value
    slope[...] = slope_val.astype(bf16)
    if sums:
        partials, total = refs[2 : 2 + sums], refs[-1]
        out = lax.dot_general(value, block[1], (((1,), (1,)), ((), ())), preferred_element_type=f32)

        @pl.when(j == 0)
        def _():
            total[...] = out

        @pl.when(j > 0)
        def _():
            total[...] += out

        @pl.when(j == pl.num_programs(0) - 1)
        def _():
            size = partials[0].shape[0]
            for b, partial in enumerate(partials):
                partial[...] = total[b * size : (b + 1) * size].astype(bf16)


def forward(flag, inputs, sources, mix, sums, emits=True):
    rows, width = inputs.shape
    units = sources[0].shape[2]
    block = min(units, 512)
    parts = 2 if sums or emits else 1
    counts, flat = flattened(sources)
    unit_spec = pl.BlockSpec((rows, block), lambda j: (0, j))
    shapes = [((rows, units), unit_spec), ((rows, units), unit_spec)]
    if sums:
        shapes += [((rows // sums, width), whole((rows // sums, width)))] * sums
    shapes += [(sources[0].shape, block_of(sources[0], block))] * emits
    return pl.pallas_call(
        functools.partial(forward_kernel, mix, counts, sums, emits),
        grid=(units // block,),
        in_specs=[pl.BlockSpec(memory_space=pltpu.SMEM), whole((rows, width))]
        + [block_of(part, block, parts) for part in flat],
        out_specs=[spec for _, spec in shapes],
        out_shape=[jax.ShapeDtypeStruct(shape, bf16) for shape, _ in shapes],
        scratch_shapes=[pltpu.VMEM((rows, width), f32)] * bool(sums),
        compiler_params=pltpu.CompilerParams(vmem_limit_bytes=48 << 20),
        cost_estimate=pl.CostEstimate(
            flops=(2 + 2 * bool(sums)) * rows * width * units,
            bytes_accessed=16 * width * units,
            transcendentals=rows * units,
        ),
    )(flag, inputs, *flat)


def only(flag, weights):
    return weights


def pushed(flag, weights, first, second):
    return weights - 0.5 * learn_rate * (first + second)


def halved(flag, found, weights, sent):
    return 0.5 * (weights + jnp.where(flag == 0, sent, found))


def backward_kernel(update, taken, pieces, given, by_core, flag, weights, slope, hidden, inputs_t, *refs):
    states, refs = regrouped(refs, taken)
    errors, refs, error, error_t = refs[:pieces], refs[pieces:-2], refs[-2], refs[-1]
    results, _ = regrouped(refs, given)

    @pl.when(pl.program_id(0) == 0)
    def _():
        size = errors[0].shape[0]
        for b, piece in enumerate(errors):
            error[b * size : (b + 1) * size] = piece[...]
        error_t[...] = error[...].T

    back = jnp.dot(error[...], weights[0].astype(bf16), preferred_element_type=f32) * slope[...].astype(f32)
    for k, (left, right) in enumerate(((inputs_t[...], back.astype(bf16)), (error_t[...], hidden[...]))):
        grad = jnp.dot(left, right, preferred_element_type=f32)
        values = update(grad, *[loaded(state, k) for state in states])
        for result, apart, value in zip(results, by_core, values):
            if type(result) is not tuple:
                result[k] = value.astype(result.dtype)
                continue
            if apart:
                for place, piece in enumerate(result):

                    @pl.when((flag[0] == k) == (place == 0))
                    def _():
                        piece[...] = value.astype(piece.dtype)

                continue
            each = len(result) // 2
            for i, piece in enumerate(result[k * each : (k + 1) * each]):
                size = piece.shape[0]
                piece[...] = value[i * size : (i + 1) * size].astype(piece.dtype)


def backward(flag, errors, weights, slope, hidden, inputs_t, states, update, kinds):
    width, rows = inputs_t.shape
    units = weights.shape[2]
    block = min(units, 512)
    counts, flat = flattened(states)
    kinds = [kind if type(kind) is tuple else (kind, 1) for kind in kinds]
    by_core = [count == "core" for _, count in kinds]
    kinds = [(kind, 2 if apart else count) for (kind, count), apart in zip(kinds, by_core)]
    shapes = []
    for kind, count in kinds:
        shape = weights.shape if count == 1 else (2 * width // count, units)
        shapes += [jax.ShapeDtypeStruct(shape, kind)] * count
    results = pl.pallas_call(
        functools.partial(backward_kernel, update, counts, len(errors), [count for _, count in kinds], by_core),
        grid=(units // block,),
        in_specs=[
            pl.BlockSpec(memory_space=pltpu.SMEM),
            pl.BlockSpec((1, width, block), lambda j: (1, 0, j)),
            pl.BlockSpec((rows, block), lambda j: (0, j)),
            pl.BlockSpec((rows, block), lambda j: (0, j)),
            whole((width, rows)),
        ]
        + [block_of(part, block) for part in flat]
        + [whole(piece.shape) for piece in errors],
        out_specs=[block_of(shape, block) for shape in shapes],
        out_shape=shapes,
        scratch_shapes=[pltpu.VMEM((rows, width), bf16), pltpu.VMEM((width, rows), bf16)],
        compiler_params=pltpu.CompilerParams(vmem_limit_bytes=56 << 20),
        cost_estimate=pl.CostEstimate(
            flops=6 * rows * width * units, bytes_accessed=28 * width * units, transcendentals=0
        ),
    )(flag, weights, slope, hidden, inputs_t, *flat, *errors)
    return regrouped(results, [count for _, count in kinds])[0]


def first_update(grad, moment):
    moment = inner_beta * moment + grad
    return (moment, moment)


def first_beside(grad, moment, own_moment, weights):
    moment = inner_beta * moment + grad
    return (moment, weights - 0.5 * learn_rate * (own_moment + moment))


def second_update(grad, moment, weights):
    moment_new = inner_beta * moment + grad
    return (moment_new, weights - learn_rate * moment_new, moment + (1.0 + inner_beta) * moment_new)


def second_beside(grad, moment, weights):
    return (weights - learn_rate * (inner_beta * moment + grad),)


def third_update(grad, moment, known):
    return (inner_beta * moment + grad, known + grad)


def rounded(value):
    return lax.reduce_precision(value, 8, 7).astype(bf16)


def added(left, right):
    return rounded(left.astype(f32) + right.astype(f32))


def tied(early, late):
    return lax.optimization_barrier((early, late))[1]


def finish_kernel(replicas, flag, slow, anchor, own, theirs, *refs):
    anchor_new, slow_new, token = refs[-3:]
    for k in range(2):
        total = jnp.where(flag[0] == k, own[...].astype(f32), theirs[...].astype(f32))
        value = slow_beta * slow[k] + total / replicas
        slow_new[k] = value
        anchor_new[k] = anchor[k] - learn_rate * value
    token[...] = jnp.zeros_like(token)


def finish(flag, replicas, slow, anchor, own, theirs, position, before):
    size, units = own.shape
    rows = pl.BlockSpec((2, size, units), lambda j: (0, position, 0))
    shape = jax.ShapeDtypeStruct(slow.shape, f32)
    return pl.pallas_call(
        functools.partial(finish_kernel, replicas),
        grid=(1,),
        in_specs=[pl.BlockSpec(memory_space=pltpu.SMEM), rows, rows, whole(own.shape), whole(own.shape)]
        + [pl.BlockSpec(memory_space=pl.ANY)] * len(before),
        out_specs=[rows, rows, whole((8, 128))],
        out_shape=[shape, shape, jax.ShapeDtypeStruct((8, 128), bf16)],
        input_output_aliases={5 + k: k for k in range(len(before))},
        compiler_params=pltpu.CompilerParams(vmem_limit_bytes=60 << 20),
        cost_estimate=pl.CostEstimate(flops=8 * size * units, bytes_accessed=36 * size * units, transcendentals=0),
    )(flag, slow, anchor, own, theirs, *before)


def slow_step(flag, mine, other, slow, anchor):
    axis, cores = "replica", 2
    index = lax.axis_index(axis)
    replicas = lax.axis_size(axis)
    chip = index // cores
    length = replicas // cores
    half = length // 2
    rows = mine.shape[0]
    size = rows // chunks

    def moved(part, hops):
        return lax.ppermute(part, axis, [(cores * a + c, cores * b + c) for a, b in hops for c in range(cores)])

    def at(places):
        return functools.reduce(jnp.logical_or, [chip == place for place in places])

    stages = [(True, [(s, s + 1), (length - 1 - s, length - 2 - s)]) for s in range(half - 1)]
    if half:
        stages.append((True, [(half - 1, half), (half, half - 1)]))
    stages += [(False, [(s + 1, s), (length - 2 - s, length - 1 - s)]) for s in reversed(range(half - 1))]

    pair_rows = rows // 2
    pairs = [swapped(other[p * pair_rows : (p + 1) * pair_rows], axis, 1) for p in range(2)]
    blocks = []
    for c in range(chunks):
        p, start = divmod(c * size, pair_rows)
        blocks.append(added(mine[c * size : (c + 1) * size], pairs[p][start : start + size]))
    arrived = {}
    tokens, results = {}, []
    final = len(stages) - 1

    def after(block, *waits):
        waits = [arrived.get(wait, tokens.get(wait)) for wait in waits]
        waits = [wait for wait in waits if wait is not None]
        return tied(waits, block) if waits else block

    for tick in range(chunks + 2 * len(stages) + 1):
        for s in reversed(range(len(stages) + 1)):
            c = tick - 2 * s
            if not 0 <= c < chunks:
                continue
            if s:
                adds, hops = stages[s - 1]
                fresh = added(blocks[c], arrived[s - 1, c]) if adds else arrived[s - 1, c]
                blocks[c] = jnp.where(at([b for _, b in hops]), fresh, blocks[c])
            if s < len(stages):
                block = blocks[c]
                if 0 < s < final:
                    block = after(block, (s + 1, c - 3))
                elif s:
                    block = after(block, c - 3)
                arrived[s, c] = moved(block, stages[s][1])
            else:
                own = blocks[c]
                *results, tokens[c] = finish(flag, replicas, slow, anchor, own, swapped(own, axis, 1), c, results)
    return results


def body(tokens, targets, row_ids, anchor, momentum, slow):
    row_count = tokens.shape[0]
    scale = 1.0 / row_count
    tensors = lax.axis_size("tensor")
    share_rows = row_count // tensors
    order = lax.axis_index("tensor") ^ jnp.arange(tensors)
    picks_all = row_ids[0].reshape(INNER, tensors, share_rows)[:, order].reshape(INNER, row_count)

    replicas = lax.axis_size("replica")
    flag = (lax.axis_index("replica") % 2).astype(jnp.int32).reshape(1)

    def gathered(own):
        return [own] + [swapped(own, "tensor", m) for m in range(1, tensors)]

    def error_share(partials, step):
        wanted = targets.at[picks_all[step, :share_rows]].get(mode="promise_in_bounds")
        share = partials[0].astype(f32)
        for m in range(1, tensors):
            share = share + swapped(partials[m], "tensor", m).astype(f32)
        return ((share - wanted.astype(f32)) * scale).astype(bf16)

    def sent(block, distance, which=(0, 1)):
        route = [((i - distance) % replicas, i) for i in range(replicas) if i % 2 in which]
        return lax.ppermute(block, "replica", route)

    def picked(step, count):
        return tokens.at[picks_all[step, :count]].get(mode="promise_in_bounds")

    near_rows = picked(0, share_rows)
    near_share = sent(near_rows, 1)
    moment_near = sent(tied(near_rows, momentum[0]).astype(bf16), 1)
    inputs_near = jnp.concatenate(gathered(near_share))

    inputs = picked(0, row_count)
    hidden, slope, *partials = forward(flag, inputs, [anchor], only, tensors, emits=False)
    own_error = error_share(partials, 0)
    hidden_near, slope_near = forward(flag, inputs_near, [anchor], only, 0, emits=False)
    error = tied((hidden_near, inputs_near.T), jnp.concatenate(gathered(own_error)))
    error_near = sent(error, 1)
    moment, moment_bf = backward(
        flag, [error], anchor, slope, hidden, inputs.T, [momentum[0]], first_update, [f32, bf16]
    )
    moment_far = sent(tied(error_near, moment_bf), 2, (0,))
    moment_near, weights = backward(
        flag,
        [error_near],
        anchor,
        slope_near,
        hidden_near,
        inputs_near.T,
        [moment_near, moment, anchor],
        first_beside,
        [bf16, bf16],
    )

    inputs = picked(1, row_count)
    inputs_far = sent(tied(error_near, inputs), 2, (1,))
    hidden, slope, *partials = forward(flag, inputs, [weights], only, tensors, emits=False)
    moment_two = sent(moment_near, 1, (1,))
    own_error = error_share(partials, 1)
    own_error = tied(moment_two, own_error)
    error = tied((inputs_far, inputs.T), jnp.concatenate(gathered(own_error)))
    error_far = sent(error, 2, (1,))
    moment, weights, known = backward(
        flag, [error], weights, slope, hidden, inputs.T, [moment, weights], second_update, [f32, bf16, bf16]
    )
    weights_sent = sent(weights, 2, (0,))
    moment_three = sent(moment_far, 1, (1,))
    inputs_far = tied(weights, inputs_far)
    hidden, slope, weights_far = forward(flag, inputs_far, [anchor, moment_two, moment_three], pushed, 0)
    (weights_found,) = backward(
        flag, [error_far], weights_far, slope, hidden, inputs_far.T, [moment_two, weights_far], second_beside, [bf16]
    )

    inputs = picked(2, row_count)
    hidden, slope, *rest = forward(flag, inputs, [weights_found, weights, weights_sent], halved, tensors)
    errors = tied(inputs.T, gathered(error_share(rest[:tensors], 2)))
    moment, total = backward(
        flag, errors, rest[tensors], slope, hidden, inputs.T, [moment, known], third_update, [f32, (bf16, "core")]
    )
    anchor_new, slow_new = slow_step(flag, *total, slow, anchor)
    return (anchor_new, slow_new, moment[None])


def solution(mesh):
    return jax.shard_map(
        body,
        mesh=mesh,
        in_specs=(
            P("replica", None),
            P("replica", None),
            P("replica", None, None),
            P(None, None, "tensor"),
            P("replica", None, None, "tensor"),
            P(None, None, "tensor"),
        ),
        out_specs=(
            P(None, None, "tensor"),
            P(None, None, "tensor"),
            P("replica", None, None, "tensor"),
        ),
        check_vma=False,
    )
```

```python
import functools

import jax
import jax.numpy as jnp
from jax import lax
from jax.experimental import pallas as pl
from jax.experimental.pallas import tpu as pltpu
from jax.sharding import PartitionSpec as P

INNER = 3


learn_rate = 0.02
inner_beta = 0.9
slow_beta = 0.5
chunks = 4
bf16, f32 = jnp.bfloat16, jnp.float32


def swapped(block, axis, mask):
    return lax.ppermute(block, axis, [(i, i ^ mask) for i in range(lax.axis_size(axis))])


def gelu_pair(pre):
    coeff = 0.7978845608028654
    square = pre * pre
    tanh_val = jnp.tanh(coeff * (pre + 0.044715 * square * pre))
    half = 0.5 * (1.0 + tanh_val)
    slope = half + 0.5 * pre * (1.0 - tanh_val * tanh_val) * coeff * (1.0 + 3.0 * 0.044715 * square)
    return (pre * half, slope)


def whole(shape):
    return pl.BlockSpec(shape, lambda j: (0,) * len(shape))


def loaded(state, k):
    if type(state) is not tuple:
        return state[k].astype(f32)
    each = len(state) // 2
    return jnp.concatenate([piece[...].astype(f32) for piece in state[k * each : (k + 1) * each]], axis=0)


def regrouped(refs, counts):
    refs, states = list(refs), []
    for count in counts:
        states.append(tuple(refs[:count]) if count > 1 else refs[0])
        del refs[:count]
    return states, refs


def flattened(states):
    flat = [state if type(state) is tuple else (state,) for state in states]
    return [len(state) for state in flat], [part for state in flat for part in state]


def block_of(part, block, parts=2):
    if part.ndim == 2:
        return pl.BlockSpec((part.shape[0], block), lambda j: (0, j))
    return pl.BlockSpec((parts, part.shape[1], block), lambda j: (0, 0, j))


def forward_kernel(mix, taken, sums, emits, flag, inputs, *refs):
    sources, refs = regrouped(refs, taken)
    hidden, slope = refs[:2]
    block = [mix(flag[0], *[loaded(source, k) for source in sources]).astype(bf16) for k in range(2 if sums or emits else 1)]
    if emits:
        for k in range(2):
            refs[2 + sums][k] = block[k]
    j = pl.program_id(0)
    value, slope_val = gelu_pair(jnp.dot(inputs[...], block[0], preferred_element_type=f32))
    value = value.astype(bf16)
    hidden[...] = value
    slope[...] = slope_val.astype(bf16)
    if sums:
        partials, total = refs[2 : 2 + sums], refs[-1]
        out = lax.dot_general(value, block[1], (((1,), (1,)), ((), ())), preferred_element_type=f32)

        @pl.when(j == 0)
        def _():
            total[...] = out

        @pl.when(j > 0)
        def _():
            total[...] += out

        @pl.when(j == pl.num_programs(0) - 1)
        def _():
            size = partials[0].shape[0]
            for b, partial in enumerate(partials):
                partial[...] = total[b * size : (b + 1) * size].astype(bf16)


def forward(flag, inputs, sources, mix, sums, emits=True):
    rows, width = inputs.shape
    units = sources[0].shape[2]
    block = min(units, 512)
    parts = 2 if sums or emits else 1
    counts, flat = flattened(sources)
    unit_spec = pl.BlockSpec((rows, block), lambda j: (0, j))
    shapes = [((rows, units), unit_spec), ((rows, units), unit_spec)]
    if sums:
        shapes += [((rows // sums, width), whole((rows // sums, width)))] * sums
    shapes += [(sources[0].shape, block_of(sources[0], block))] * emits
    return pl.pallas_call(
        functools.partial(forward_kernel, mix, counts, sums, emits),
        grid=(units // block,),
        in_specs=[pl.BlockSpec(memory_space=pltpu.SMEM), whole((rows, width))]
        + [block_of(part, block, parts) for part in flat],
        out_specs=[spec for _, spec in shapes],
        out_shape=[jax.ShapeDtypeStruct(shape, bf16) for shape, _ in shapes],
        scratch_shapes=[pltpu.VMEM((rows, width), f32)] * bool(sums),
        compiler_params=pltpu.CompilerParams(vmem_limit_bytes=48 << 20),
        cost_estimate=pl.CostEstimate(
            flops=(2 + 2 * bool(sums)) * rows * width * units,
            bytes_accessed=16 * width * units,
            transcendentals=rows * units,
        ),
    )(flag, inputs, *flat)


def only(flag, weights):
    return weights


def pushed(flag, weights, first, second):
    return weights - 0.5 * learn_rate * (first + second)


def halved(flag, found, weights, sent):
    return 0.5 * (weights + jnp.where(flag == 0, sent, found))


def backward_kernel(update, taken, pieces, given, by_core, flag, weights, slope, hidden, inputs_t, *refs):
    states, refs = regrouped(refs, taken)
    errors, refs, error, error_t = refs[:pieces], refs[pieces:-2], refs[-2], refs[-1]
    results, _ = regrouped(refs[len(refs) - sum(given) :], given)

    @pl.when(pl.program_id(0) == 0)
    def _():
        size = errors[0].shape[0]
        for b, piece in enumerate(errors):
            error[b * size : (b + 1) * size] = piece[...]
        error_t[...] = error[...].T

    back = jnp.dot(error[...], weights[0].astype(bf16), preferred_element_type=f32) * slope[...].astype(f32)
    for k, (left, right) in enumerate(((inputs_t[...], back.astype(bf16)), (error_t[...], hidden[...]))):
        grad = jnp.dot(left, right, preferred_element_type=f32)
        values = update(grad, *[loaded(state, k) for state in states])
        for result, apart, value in zip(results, by_core, values):
            if type(result) is not tuple:
                result[k] = value.astype(result.dtype)
                continue
            if apart:
                for place, piece in enumerate(result):

                    @pl.when((flag[0] == k) == (place == 0))
                    def _():
                        piece[...] = value.astype(piece.dtype)

                continue
            each = len(result) // 2
            for i, piece in enumerate(result[k * each : (k + 1) * each]):
                size = piece.shape[0]
                piece[...] = value[i * size : (i + 1) * size].astype(piece.dtype)


def backward(flag, errors, weights, slope, hidden, inputs_t, states, update, kinds, waits=()):
    width, rows = inputs_t.shape
    units = weights.shape[2]
    block = min(units, 512)
    counts, flat = flattened(states)
    kinds = [kind if type(kind) is tuple else (kind, 1) for kind in kinds]
    by_core = [count == "core" for _, count in kinds]
    kinds = [(kind, 2 if apart else count) for (kind, count), apart in zip(kinds, by_core)]
    shapes = []
    for kind, count in kinds:
        shape = weights.shape if count == 1 else (2 * width // count, units)
        shapes += [jax.ShapeDtypeStruct(shape, kind)] * count
    results = pl.pallas_call(
        functools.partial(backward_kernel, update, counts, len(errors), [count for _, count in kinds], by_core),
        grid=(units // block,),
        in_specs=[
            pl.BlockSpec(memory_space=pltpu.SMEM),
            pl.BlockSpec((1, width, block), lambda j: (1, 0, j)),
            pl.BlockSpec((rows, block), lambda j: (0, j)),
            pl.BlockSpec((rows, block), lambda j: (0, j)),
            whole((width, rows)),
        ]
        + [block_of(part, block) for part in flat]
        + [whole(piece.shape) for piece in errors]
        + [ANY] * len(waits),
        out_specs=[block_of(shape, block) for shape in shapes],
        out_shape=shapes,
        scratch_shapes=[pltpu.VMEM((rows, width), bf16), pltpu.VMEM((width, rows), bf16)],
        compiler_params=pltpu.CompilerParams(vmem_limit_bytes=56 << 20),
        cost_estimate=pl.CostEstimate(
            flops=6 * rows * width * units, bytes_accessed=28 * width * units, transcendentals=0
        ),
    )(flag, weights, slope, hidden, inputs_t, *flat, *errors, *waits)
    return regrouped(results, [count for _, count in kinds])[0]


def first_update(grad, moment):
    moment = inner_beta * moment + grad
    return (moment, moment)


def first_beside(grad, moment, own_moment, weights):
    moment = inner_beta * moment + grad
    return (moment, weights - 0.5 * learn_rate * (own_moment + moment))


def second_update(grad, moment, weights):
    moment_new = inner_beta * moment + grad
    return (moment_new, weights - learn_rate * moment_new, moment + (1.0 + inner_beta) * moment_new)


def second_beside(grad, moment, weights):
    return (weights - learn_rate * (inner_beta * moment + grad),)


def third_update(grad, moment, known):
    return (inner_beta * moment + grad, known + grad)


def rounded(value):
    return lax.reduce_precision(value, 8, 7).astype(bf16)


def added(left, right):
    return rounded(left.astype(f32) + right.astype(f32))


ANY = pl.BlockSpec(memory_space=pl.ANY)


def nothing(*refs):
    pass


def tied(waits, block):
    return pl.pallas_call(
        nothing,
        in_specs=[ANY] * (1 + len(waits)),
        out_specs=ANY,
        out_shape=jax.ShapeDtypeStruct(block.shape, block.dtype),
        input_output_aliases={0: 0},
    )(block, *waits)


def cast_kernel(block, *refs):
    refs[-1][...] = block[...].astype(bf16)


def narrowed(block, waits):
    _, rows, units = block.shape
    spec = pl.BlockSpec((1, rows // 4, units), lambda k, j: (k, j, 0))
    return pl.pallas_call(
        cast_kernel,
        grid=(2, 4),
        in_specs=[spec] + [ANY] * len(waits),
        out_specs=spec,
        out_shape=jax.ShapeDtypeStruct(block.shape, bf16),
        cost_estimate=pl.CostEstimate(flops=2 * rows * units, bytes_accessed=12 * rows * units, transcendentals=0),
    )(block, *waits)


def finish_kernel(replicas, flag, slow, anchor, own, theirs, *refs):
    anchor_new, slow_new, token = refs[-3:]
    for k in range(2):
        total = jnp.where(flag[0] == k, own[...].astype(f32), theirs[...].astype(f32))
        value = slow_beta * slow[k] + total / replicas
        slow_new[k] = value
        anchor_new[k] = anchor[k] - learn_rate * value
    token[...] = jnp.zeros_like(token)


def finish(flag, replicas, slow, anchor, own, theirs, position, before, waits):
    size, units = own.shape
    steps = 4
    rows = pl.BlockSpec((2, size // steps, units), lambda j: (0, position * steps + j, 0))
    part = pl.BlockSpec((size // steps, units), lambda j: (j, 0))
    shape = jax.ShapeDtypeStruct(slow.shape, f32)
    return pl.pallas_call(
        functools.partial(finish_kernel, replicas),
        grid=(steps,),
        in_specs=[pl.BlockSpec(memory_space=pltpu.SMEM), rows, rows, part, part] + [ANY] * (len(before) + len(waits)),
        out_specs=[rows, rows, whole((8, 128))],
        out_shape=[shape, shape, jax.ShapeDtypeStruct((8, 128), bf16)],
        input_output_aliases={5 + k: k for k in range(len(before))},
        compiler_params=pltpu.CompilerParams(vmem_limit_bytes=60 << 20),
        cost_estimate=pl.CostEstimate(flops=8 * size * units, bytes_accessed=36 * size * units, transcendentals=0),
    )(flag, slow, anchor, own, theirs, *before, *waits)


def slow_step(flag, mine, other, slow, anchor):
    axis, cores = "replica", 2
    index = lax.axis_index(axis)
    replicas = lax.axis_size(axis)
    chip = index // cores
    length = replicas // cores
    half = length // 2
    rows = mine.shape[0]
    size = rows // chunks

    def moved(part, hops):
        return lax.ppermute(part, axis, [(cores * a + c, cores * b + c) for a, b in hops for c in range(cores)])

    def at(places):
        return functools.reduce(jnp.logical_or, [chip == place for place in places])

    stages = [(True, [(s, s + 1), (length - 1 - s, length - 2 - s)]) for s in range(half - 1)]
    if half:
        stages.append((True, [(half - 1, half), (half, half - 1)]))
    stages += [(False, [(s + 1, s), (length - 2 - s, length - 1 - s)]) for s in reversed(range(half - 1))]

    pair_rows = rows // 2
    pairs = [swapped(other[p * pair_rows : (p + 1) * pair_rows], axis, 1) for p in range(2)]
    blocks = []
    for c in range(chunks):
        p, start = divmod(c * size, pair_rows)
        blocks.append(added(mine[c * size : (c + 1) * size], pairs[p][start : start + size]))
    order = []
    for tick in range(chunks + 2 * len(stages) + 1):
        for s in range(len(stages) + 1):
            c = tick - 2 * s
            if 0 <= c < chunks:
                order.append((s, c))
    arrived = {}
    results, last = [], None

    def chained(block):
        return block if last is None else jnp.where(chip < length, block, last)

    for s, c in order:
        if s:
            adds, hops = stages[s - 1]
            fresh = added(blocks[c], arrived[s - 1, c]) if adds else arrived[s - 1, c]
            last = blocks[c] = chained(jnp.where(at([b for _, b in hops]), fresh, blocks[c]))
        if s < len(stages):
            arrived[s, c] = moved(blocks[c], stages[s][1])
        else:
            own = blocks[c]
            *results, token = finish(
                flag, replicas, slow, anchor, own, swapped(own, axis, 1), c, results, [] if c == 0 else [last]
            )
            last = jnp.broadcast_to(token[:1, :1], own.shape)
    return results


def body(tokens, targets, row_ids, anchor, momentum, slow):
    row_count = tokens.shape[0]
    scale = 1.0 / row_count
    tensors = lax.axis_size("tensor")
    share_rows = row_count // tensors
    order = lax.axis_index("tensor") ^ jnp.arange(tensors)
    picks_all = row_ids[0].reshape(INNER, tensors, share_rows)[:, order].reshape(INNER, row_count)

    replicas = lax.axis_size("replica")
    flag = (lax.axis_index("replica") % 2).astype(jnp.int32).reshape(1)

    def gathered(own):
        return [own] + [swapped(own, "tensor", m) for m in range(1, tensors)]

    def error_share(partials, step):
        wanted = targets.at[picks_all[step, :share_rows]].get(mode="promise_in_bounds")
        share = partials[0].astype(f32)
        for m in range(1, tensors):
            share = share + swapped(partials[m], "tensor", m).astype(f32)
        return ((share - wanted.astype(f32)) * scale).astype(bf16)

    def sent(block, distance, which=(0, 1)):
        route = [((i - distance) % replicas, i) for i in range(replicas) if i % 2 in which]
        return lax.ppermute(block, "replica", route)

    def picked(step, count):
        return tokens.at[picks_all[step, :count]].get(mode="promise_in_bounds")

    inputs = picked(0, row_count)
    inputs_near = sent(inputs, 1)
    moment_near = sent(narrowed(momentum[0], [inputs]), 1)

    hidden, slope, *partials = forward(flag, inputs, [anchor], only, tensors, emits=False)
    error = jnp.concatenate(gathered(error_share(partials, 0)))
    error_near = sent(error, 1)
    hidden_near, slope_near = forward(flag, inputs_near, [anchor], only, 0, emits=False)
    inputs_near_t = inputs_near.T
    moment, moment_bf = backward(
        flag,
        [error],
        anchor,
        slope,
        hidden,
        inputs.T,
        [momentum[0]],
        first_update,
        [f32, bf16],
        waits=[hidden_near, inputs_near_t],
    )
    moment_far = sent(moment_bf, 2, (0,))
    inputs = tied([moment], picked(1, row_count))
    inputs_far = sent(inputs, 2, (1,))
    moment_near, weights = backward(
        flag,
        [error_near],
        anchor,
        slope_near,
        hidden_near,
        inputs_near_t,
        [moment_near, moment, anchor],
        first_beside,
        [bf16, bf16],
    )

    moment_two = sent(moment_near, 1, (1,))
    hidden, slope, *partials = forward(flag, inputs, [weights], only, tensors, emits=False)
    error = jnp.concatenate(gathered(error_share(partials, 1)))
    error_far = sent(error, 2, (1,))
    inputs_far_t = inputs_far.T
    moment, weights, known = backward(
        flag,
        [error],
        weights,
        slope,
        hidden,
        inputs.T,
        [moment, weights],
        second_update,
        [f32, bf16, bf16],
        waits=[inputs_far_t, moment_two],
    )
    weights = tied([error_far], weights)
    weights_sent = sent(weights, 2, (0,))
    moment_three = sent(tied([weights], moment_far), 1, (1,))
    hidden, slope, weights_far = forward(flag, inputs_far, [anchor, moment_two, moment_three], pushed, 0)
    (weights_found,) = backward(
        flag, [error_far], weights_far, slope, hidden, inputs_far_t, [moment_two, weights_far], second_beside, [bf16]
    )

    inputs = picked(2, row_count)
    hidden, slope, *rest = forward(flag, inputs, [weights_found, weights, weights_sent], halved, tensors)
    errors = gathered(error_share(rest[:tensors], 2))
    moment, total = backward(
        flag, errors, rest[tensors], slope, hidden, inputs.T, [moment, known], third_update, [f32, (bf16, "core")]
    )
    anchor_new, slow_new = slow_step(flag, *total, slow, anchor)
    return (anchor_new, slow_new, moment[None])


def solution(mesh):
    return jax.shard_map(
        body,
        mesh=mesh,
        in_specs=(
            P("replica", None),
            P("replica", None),
            P("replica", None, None),
            P(None, None, "tensor"),
            P("replica", None, None, "tensor"),
            P(None, None, "tensor"),
        ),
        out_specs=(
            P(None, None, "tensor"),
            P(None, None, "tensor"),
            P("replica", None, None, "tensor"),
        ),
        check_vma=False,
    )
```

```python
import functools

import jax
import jax.numpy as jnp
from jax import lax
from jax.experimental import pallas as pl
from jax.experimental.pallas import tpu as pltpu
from jax.sharding import PartitionSpec as P

INNER = 3


learn_rate = 0.02
inner_beta = 0.9
slow_beta = 0.5
chunks = 4
bf16, f32 = jnp.bfloat16, jnp.float32


def swapped(block, axis, mask):
    return lax.ppermute(block, axis, [(i, i ^ mask) for i in range(lax.axis_size(axis))])


def gelu_pair(pre):
    coeff = 0.7978845608028654
    square = pre * pre
    tanh_val = jnp.tanh(coeff * (pre + 0.044715 * square * pre))
    half = 0.5 * (1.0 + tanh_val)
    slope = half + 0.5 * pre * (1.0 - tanh_val * tanh_val) * coeff * (1.0 + 3.0 * 0.044715 * square)
    return (pre * half, slope)


def whole(shape):
    return pl.BlockSpec(shape, lambda j: (0,) * len(shape))


def loaded(state, k):
    if type(state) is not tuple:
        return state[k].astype(f32)
    each = len(state) // 2
    return jnp.concatenate([piece[...].astype(f32) for piece in state[k * each : (k + 1) * each]], axis=0)


def regrouped(refs, counts):
    refs, states = list(refs), []
    for count in counts:
        states.append(tuple(refs[:count]) if count > 1 else refs[0])
        del refs[:count]
    return states, refs


def flattened(states):
    flat = [state if type(state) is tuple else (state,) for state in states]
    return [len(state) for state in flat], [part for state in flat for part in state]


def block_of(part, block, parts=2):
    if part.ndim == 2:
        return pl.BlockSpec((part.shape[0], block), lambda j: (0, j))
    return pl.BlockSpec((parts, part.shape[1], block), lambda j: (0, 0, j))


def joined(pieces, place):
    if len(pieces) == 1:
        return pieces[0]

    @pl.when(pl.program_id(0) == 0)
    def _():
        size = pieces[0].shape[0]
        for b, piece in enumerate(pieces):
            place[b * size : (b + 1) * size] = piece[...]

    return place


def forward_kernel(mix, taken, pieces, sums, emits, flag, *refs):
    rows, refs = refs[:pieces], refs[pieces:]
    sources, refs = regrouped(refs, taken)
    hidden, slope = refs[:2]
    inputs = joined(rows, refs[-1])
    block = [mix(flag[0], *[loaded(source, k) for source in sources]).astype(bf16) for k in range(2 if sums or emits else 1)]
    if emits:
        for k in range(2):
            refs[2 + sums][k] = block[k]
    j = pl.program_id(0)
    value, slope_val = gelu_pair(jnp.dot(inputs[...], block[0], preferred_element_type=f32))
    value = value.astype(bf16)
    hidden[...] = value
    slope[...] = slope_val.astype(bf16)
    if sums:
        partials, total = refs[2 : 2 + sums], refs[-2]
        out = lax.dot_general(value, block[1], (((1,), (1,)), ((), ())), preferred_element_type=f32)

        @pl.when(j == 0)
        def _():
            total[...] = out

        @pl.when(j > 0)
        def _():
            total[...] += out

        @pl.when(j == pl.num_programs(0) - 1)
        def _():
            size = partials[0].shape[0]
            for b, partial in enumerate(partials):
                partial[...] = total[b * size : (b + 1) * size].astype(bf16)


def forward(flag, inputs, sources, mix, sums, emits=True):
    count, width = inputs[0].shape
    rows = count * len(inputs)
    units = sources[0].shape[2]
    block = min(units, 512)
    parts = 2 if sums or emits else 1
    counts, flat = flattened(sources)
    unit_spec = pl.BlockSpec((rows, block), lambda j: (0, j))
    shapes = [((rows, units), unit_spec), ((rows, units), unit_spec)]
    if sums:
        shapes += [((rows // sums, width), whole((rows // sums, width)))] * sums
    shapes += [(sources[0].shape, block_of(sources[0], block))] * emits
    return pl.pallas_call(
        functools.partial(forward_kernel, mix, counts, len(inputs), sums, emits),
        grid=(units // block,),
        in_specs=[pl.BlockSpec(memory_space=pltpu.SMEM)]
        + [whole(piece.shape) for piece in inputs]
        + [block_of(part, block, parts) for part in flat],
        out_specs=[spec for _, spec in shapes],
        out_shape=[jax.ShapeDtypeStruct(shape, bf16) for shape, _ in shapes],
        scratch_shapes=[pltpu.VMEM((rows, width), f32)] * bool(sums) + [pltpu.VMEM((rows, width), bf16)],
        compiler_params=pltpu.CompilerParams(vmem_limit_bytes=48 << 20),
        cost_estimate=pl.CostEstimate(
            flops=(2 + 2 * bool(sums)) * rows * width * units,
            bytes_accessed=16 * width * units,
            transcendentals=rows * units,
        ),
    )(flag, *inputs, *flat)


def only(flag, weights):
    return weights


def pushed(flag, weights, first, second):
    return weights - 0.5 * learn_rate * (first + second)


def halved(flag, found, weights, sent):
    return 0.5 * (weights + jnp.where(flag == 0, sent, found))


def backward_kernel(update, taken, pieces, given, by_core, flag, weights, slope, hidden, *refs):
    states, refs = regrouped(refs, taken)
    error_count, input_count = pieces
    errors, inputs = refs[:error_count], refs[error_count : error_count + input_count]
    error, error_t, rows, inputs_t = refs[-4:]
    refs = refs[error_count + input_count : -4]
    results, _ = regrouped(refs[len(refs) - sum(given) :], given)
    error, rows = joined(errors, error), joined(inputs, rows)

    @pl.when(pl.program_id(0) == 0)
    def _():
        error_t[...] = error[...].T
        inputs_t[...] = rows[...].T

    back = jnp.dot(error[...], weights[0].astype(bf16), preferred_element_type=f32) * slope[...].astype(f32)
    for k, (left, right) in enumerate(((inputs_t[...], back.astype(bf16)), (error_t[...], hidden[...]))):
        grad = jnp.dot(left, right, preferred_element_type=f32)
        values = update(grad, *[loaded(state, k) for state in states])
        for result, apart, value in zip(results, by_core, values):
            if type(result) is not tuple:
                result[k] = value.astype(result.dtype)
                continue
            if apart:
                for place, piece in enumerate(result):

                    @pl.when((flag[0] == k) == (place == 0))
                    def _():
                        piece[...] = value.astype(piece.dtype)

                continue
            each = len(result) // 2
            for i, piece in enumerate(result[k * each : (k + 1) * each]):
                size = piece.shape[0]
                piece[...] = value[i * size : (i + 1) * size].astype(piece.dtype)


def backward(flag, errors, weights, slope, hidden, inputs, states, update, kinds, waits=()):
    rows, width = hidden.shape[0], weights.shape[1]
    units = weights.shape[2]
    block = min(units, 512)
    counts, flat = flattened(states)
    kinds = [kind if type(kind) is tuple else (kind, 1) for kind in kinds]
    by_core = [count == "core" for _, count in kinds]
    kinds = [(kind, 2 if apart else count) for (kind, count), apart in zip(kinds, by_core)]
    shapes = []
    for kind, count in kinds:
        shape = weights.shape if count == 1 else (2 * width // count, units)
        shapes += [jax.ShapeDtypeStruct(shape, kind)] * count
    results = pl.pallas_call(
        functools.partial(
            backward_kernel, update, counts, (len(errors), len(inputs)), [count for _, count in kinds], by_core
        ),
        grid=(units // block,),
        in_specs=[
            pl.BlockSpec(memory_space=pltpu.SMEM),
            pl.BlockSpec((1, width, block), lambda j: (1, 0, j)),
            pl.BlockSpec((rows, block), lambda j: (0, j)),
            pl.BlockSpec((rows, block), lambda j: (0, j)),
        ]
        + [block_of(part, block) for part in flat]
        + [whole(piece.shape) for piece in (*errors, *inputs)]
        + [ANY] * len(waits),
        out_specs=[block_of(shape, block) for shape in shapes],
        out_shape=shapes,
        scratch_shapes=[pltpu.VMEM((rows, width), bf16), pltpu.VMEM((width, rows), bf16)] * 2,
        compiler_params=pltpu.CompilerParams(vmem_limit_bytes=56 << 20),
        cost_estimate=pl.CostEstimate(
            flops=6 * rows * width * units, bytes_accessed=28 * width * units, transcendentals=0
        ),
    )(flag, weights, slope, hidden, *flat, *errors, *inputs, *waits)
    return regrouped(results, [count for _, count in kinds])[0]


def first_update(grad, moment):
    moment = inner_beta * moment + grad
    return (moment, moment)


def first_beside(grad, moment, own_moment, weights):
    moment = inner_beta * moment + grad
    return (moment, weights - 0.5 * learn_rate * (own_moment + moment))


def second_update(grad, moment, weights):
    moment_new = inner_beta * moment + grad
    return (moment_new, weights - learn_rate * moment_new, moment + (1.0 + inner_beta) * moment_new)


def second_beside(grad, moment, weights):
    return (weights - learn_rate * (inner_beta * moment + grad),)


def third_update(grad, moment, known):
    return (inner_beta * moment + grad, known + grad)


def rounded(value):
    return lax.reduce_precision(value, 8, 7).astype(bf16)


def added(left, right):
    return rounded(left.astype(f32) + right.astype(f32))


ANY = pl.BlockSpec(memory_space=pl.ANY)


def nothing(*refs):
    pass


def tied(waits, block):
    return pl.pallas_call(
        nothing,
        in_specs=[ANY] * (1 + len(waits)),
        out_specs=ANY,
        out_shape=jax.ShapeDtypeStruct(block.shape, block.dtype),
        input_output_aliases={0: 0},
    )(block, *waits)


def combine_kernel(adds, places, chip, block, arrived, *refs):
    inside = functools.reduce(jnp.logical_or, [chip[0] == place for place in places])
    fresh = arrived[...]
    if adds:
        fresh = (block[...].astype(f32) + fresh.astype(f32)).astype(bf16)
    refs[-1][...] = jnp.where(inside, fresh, block[...])


def combined(adds, places, chip, block, arrived, waits):
    return pl.pallas_call(
        functools.partial(combine_kernel, adds, places),
        grid=(1,),
        in_specs=[pl.BlockSpec(memory_space=pltpu.SMEM), whole(block.shape), whole(block.shape)] + [ANY] * len(waits),
        out_specs=whole(block.shape),
        out_shape=jax.ShapeDtypeStruct(block.shape, bf16),
    )(chip, block, arrived, *waits)


def finish_kernel(replicas, flag, slow, anchor, own, theirs, *refs):
    anchor_new, slow_new, token = refs[-3:]
    for k in range(2):
        total = jnp.where(flag[0] == k, own[...].astype(f32), theirs[...].astype(f32))
        value = slow_beta * slow[k] + total / replicas
        slow_new[k] = value
        anchor_new[k] = anchor[k] - learn_rate * value
    token[...] = jnp.zeros_like(token)


def finish(flag, replicas, slow, anchor, own, theirs, position, before, waits):
    size, units = own.shape
    steps = 4
    rows = pl.BlockSpec((2, size // steps, units), lambda j: (0, position * steps + j, 0))
    part = pl.BlockSpec((size // steps, units), lambda j: (j, 0))
    shape = jax.ShapeDtypeStruct(slow.shape, f32)
    return pl.pallas_call(
        functools.partial(finish_kernel, replicas),
        grid=(steps,),
        in_specs=[pl.BlockSpec(memory_space=pltpu.SMEM), rows, rows, part, part] + [ANY] * (len(before) + len(waits)),
        out_specs=[rows, rows, whole((8, 128))],
        out_shape=[shape, shape, jax.ShapeDtypeStruct((8, 128), bf16)],
        input_output_aliases={5 + k: k for k in range(len(before))},
        compiler_params=pltpu.CompilerParams(vmem_limit_bytes=60 << 20),
        cost_estimate=pl.CostEstimate(flops=8 * size * units, bytes_accessed=36 * size * units, transcendentals=0),
    )(flag, slow, anchor, own, theirs, *before, *waits)


def slow_step(flag, mine, other, slow, anchor):
    axis, cores = "replica", 2
    index = lax.axis_index(axis)
    replicas = lax.axis_size(axis)
    chip = (index // cores).astype(jnp.int32).reshape(1)
    length = replicas // cores
    half = length // 2
    rows = mine.shape[0]
    size = rows // chunks

    def moved(part, hops):
        return lax.ppermute(part, axis, [(cores * a + c, cores * b + c) for a, b in hops for c in range(cores)])

    stages = [(True, [(s, s + 1), (length - 1 - s, length - 2 - s)]) for s in range(half - 1)]
    if half:
        stages.append((True, [(half - 1, half), (half, half - 1)]))
    stages += [(False, [(s + 1, s), (length - 2 - s, length - 1 - s)]) for s in reversed(range(half - 1))]

    pair_rows = rows // 2
    pairs = [swapped(other[p * pair_rows : (p + 1) * pair_rows], axis, 1) for p in range(2)]
    blocks = []
    for c in range(chunks):
        p, start = divmod(c * size, pair_rows)
        blocks.append(added(mine[c * size : (c + 1) * size], pairs[p][start : start + size]))
    arrived = {}
    results, waits = [], []
    for tick in range(chunks + 2 * len(stages) + 1):
        for s in range(len(stages) + 1):
            c = tick - 2 * s
            if not 0 <= c < chunks:
                continue
            if s:
                adds, hops = stages[s - 1]
                blocks[c] = combined(adds, [b for _, b in hops], chip, blocks[c], arrived[s - 1, c], waits)
                waits = [blocks[c]]
            if s < len(stages):
                arrived[s, c] = moved(blocks[c], stages[s][1])
            else:
                theirs = swapped(blocks[c], axis, 1)
                *results, token = finish(flag, replicas, slow, anchor, blocks[c], theirs, c, results, waits)
                waits = [token]
    return results


def body(tokens, targets, row_ids, anchor, momentum, slow):
    row_count = tokens.shape[0]
    scale = 1.0 / row_count
    tensors = lax.axis_size("tensor")
    share_rows = row_count // tensors
    order = lax.axis_index("tensor") ^ jnp.arange(tensors)
    picks_all = row_ids[0].reshape(INNER, tensors, share_rows)[:, order].reshape(INNER, row_count)

    replicas = lax.axis_size("replica")
    flag = (lax.axis_index("replica") % 2).astype(jnp.int32).reshape(1)

    def gathered(own):
        return [own] + [swapped(own, "tensor", m) for m in range(1, tensors)]

    def error_share(partials, step):
        wanted = targets.at[picks_all[step, :share_rows]].get(mode="promise_in_bounds")
        share = partials[0].astype(f32)
        for m in range(1, tensors):
            share = share + swapped(partials[m], "tensor", m).astype(f32)
        return ((share - wanted.astype(f32)) * scale).astype(bf16)

    def sent(block, distance, which=(0, 1)):
        route = [((i - distance) % replicas, i) for i in range(replicas) if i % 2 in which]
        return lax.ppermute(block, "replica", route)

    def picked(step, count):
        return tokens.at[picks_all[step, :count]].get(mode="promise_in_bounds")

    near_share = sent(picked(0, share_rows), 1)
    moment_near = sent(tied([near_share], momentum[0].astype(bf16)), 1)

    inputs = [picked(0, row_count)]
    hidden, slope, *partials = forward(flag, inputs, [anchor], only, tensors, emits=False)
    error = jnp.concatenate(gathered(error_share(partials, 0)))
    error_near = sent(error, 1)
    inputs_near = gathered(near_share)
    hidden_near, slope_near = forward(flag, inputs_near, [anchor], only, 0, emits=False)
    moment, moment_bf = backward(
        flag,
        [error],
        anchor,
        slope,
        hidden,
        inputs,
        [momentum[0]],
        first_update,
        [f32, bf16],
        waits=[hidden_near],
    )
    moment_far = sent(moment_bf, 2, (0,))
    moment_near, weights = backward(
        flag,
        [error_near],
        anchor,
        slope_near,
        hidden_near,
        inputs_near,
        [moment_near, moment, anchor],
        first_beside,
        [bf16, bf16],
    )

    inputs = [tied([moment], picked(1, row_count))]
    inputs_far = sent(inputs[0], 2, (1,))
    moment_two = sent(moment_near, 1, (1,))
    moment_three = sent(moment_far, 1, (1,))
    hidden, slope, *partials = forward(flag, inputs, [weights], only, tensors, emits=False)
    error = jnp.concatenate(gathered(error_share(partials, 1)))
    error_far = sent(error, 2, (1,))
    moment, weights, known = backward(
        flag,
        [error],
        weights,
        slope,
        hidden,
        inputs,
        [moment, weights],
        second_update,
        [f32, bf16, bf16],
        waits=[inputs_far, moment_two, moment_three],
    )
    weights = tied([error_far], weights)
    weights_sent = sent(weights, 2, (0,))
    hidden, slope, weights_far = forward(flag, [inputs_far], [anchor, moment_two, moment_three], pushed, 0)
    (weights_found,) = backward(
        flag, [error_far], weights_far, slope, hidden, [inputs_far], [moment_two, weights_far], second_beside, [bf16]
    )

    inputs = [picked(2, row_count)]
    hidden, slope, *rest = forward(flag, inputs, [weights_found, weights, weights_sent], halved, tensors)
    errors = gathered(error_share(rest[:tensors], 2))
    moment, total = backward(
        flag, errors, rest[tensors], slope, hidden, inputs, [moment, known], third_update, [f32, (bf16, "core")]
    )
    anchor_new, slow_new = slow_step(flag, *total, slow, anchor)
    return (anchor_new, slow_new, moment[None])


def solution(mesh):
    return jax.shard_map(
        body,
        mesh=mesh,
        in_specs=(
            P("replica", None),
            P("replica", None),
            P("replica", None, None),
            P(None, None, "tensor"),
            P("replica", None, None, "tensor"),
            P(None, None, "tensor"),
        ),
        out_specs=(
            P(None, None, "tensor"),
            P(None, None, "tensor"),
            P("replica", None, None, "tensor"),
        ),
        check_vma=False,
    )
```

```python
import functools

import jax
import jax.numpy as jnp
from jax import lax
from jax.experimental import pallas as pl
from jax.experimental.pallas import tpu as pltpu
from jax.sharding import PartitionSpec as P

INNER = 3


learn_rate = 0.02
inner_beta = 0.9
slow_beta = 0.5
chunks = 4
bf16, f32 = jnp.bfloat16, jnp.float32
ANY = pl.BlockSpec(memory_space=pl.ANY)
LIGHT = pl.CostEstimate(flops=1, bytes_accessed=1, transcendentals=0)


def swapped(block, axis, mask):
    return lax.ppermute(block, axis, [(i, i ^ mask) for i in range(lax.axis_size(axis))])


def gelu_pair(pre):
    coeff = 0.7978845608028654
    square = pre * pre
    tanh_val = jnp.tanh(coeff * (pre + 0.044715 * square * pre))
    half = 0.5 * (1.0 + tanh_val)
    slope = half + 0.5 * pre * (1.0 - tanh_val * tanh_val) * coeff * (1.0 + 3.0 * 0.044715 * square)
    return (pre * half, slope)


def whole(shape):
    return pl.BlockSpec(shape, lambda j: (0,) * len(shape))


def loaded(state, k):
    if type(state) is not tuple:
        return state[k].astype(f32)
    each = len(state) // 2
    return jnp.concatenate([piece[...].astype(f32) for piece in state[k * each : (k + 1) * each]], axis=0)


def regrouped(refs, counts):
    refs, states = list(refs), []
    for count in counts:
        states.append(tuple(refs[:count]) if count > 1 else refs[0])
        del refs[:count]
    return states, refs


def flattened(states):
    flat = [state if type(state) is tuple else (state,) for state in states]
    return [len(state) for state in flat], [part for state in flat for part in state]


def block_of(part, block, parts=2):
    if part.ndim == 2:
        return pl.BlockSpec((part.shape[0], block), lambda j: (0, j))
    return pl.BlockSpec((parts, part.shape[1], block), lambda j: (0, 0, j))


def joined(pieces, place):
    if len(pieces) == 1:
        return pieces[0]

    @pl.when(pl.program_id(0) == 0)
    def _():
        size = pieces[0].shape[0]
        for b, piece in enumerate(pieces):
            place[b * size : (b + 1) * size] = piece[...]

    return place


def forward_kernel(mix, taken, pieces, sums, emits, flag, *refs):
    rows, refs = refs[:pieces], refs[pieces:]
    sources, refs = regrouped(refs, taken)
    hidden, slope = refs[:2]
    inputs = joined(rows, refs[-1])
    block = [mix(flag[0], *[loaded(source, k) for source in sources]).astype(bf16) for k in range(2 if sums or emits else 1)]
    if emits:
        for k in range(2):
            refs[2 + sums][k] = block[k]
    j = pl.program_id(0)
    value, slope_val = gelu_pair(jnp.dot(inputs[...], block[0], preferred_element_type=f32))
    value = value.astype(bf16)
    hidden[...] = value
    slope[...] = slope_val.astype(bf16)
    if sums:
        partials, total = refs[2 : 2 + sums], refs[-2]
        out = lax.dot_general(value, block[1], (((1,), (1,)), ((), ())), preferred_element_type=f32)

        @pl.when(j == 0)
        def _():
            total[...] = out

        @pl.when(j > 0)
        def _():
            total[...] += out

        @pl.when(j == pl.num_programs(0) - 1)
        def _():
            size = partials[0].shape[0]
            for b, partial in enumerate(partials):
                partial[...] = total[b * size : (b + 1) * size].astype(bf16)


def forward(flag, inputs, sources, mix, sums, emits=True):
    count, width = inputs[0].shape
    rows = count * len(inputs)
    units = sources[0].shape[2]
    block = min(units, 512)
    parts = 2 if sums or emits else 1
    counts, flat = flattened(sources)
    unit_spec = pl.BlockSpec((rows, block), lambda j: (0, j))
    shapes = [((rows, units), unit_spec), ((rows, units), unit_spec)]
    if sums:
        shapes += [((rows // sums, width), whole((rows // sums, width)))] * sums
    shapes += [(sources[0].shape, block_of(sources[0], block))] * emits
    return pl.pallas_call(
        functools.partial(forward_kernel, mix, counts, len(inputs), sums, emits),
        grid=(units // block,),
        in_specs=[pl.BlockSpec(memory_space=pltpu.SMEM)]
        + [whole(piece.shape) for piece in inputs]
        + [block_of(part, block, parts) for part in flat],
        out_specs=[spec for _, spec in shapes],
        out_shape=[jax.ShapeDtypeStruct(shape, bf16) for shape, _ in shapes],
        scratch_shapes=[pltpu.VMEM((rows, width), f32)] * bool(sums) + [pltpu.VMEM((rows, width), bf16)],
        compiler_params=pltpu.CompilerParams(vmem_limit_bytes=48 << 20),
        cost_estimate=LIGHT,
    )(flag, *inputs, *flat)


def only(flag, weights):
    return weights


def pushed(flag, weights, first, second):
    return weights - 0.5 * learn_rate * (first + second)


def halved(flag, found, weights, sent):
    return 0.5 * (weights + jnp.where(flag == 0, sent, found))


def backward_kernel(update, taken, pieces, given, by_core, flag, weights, slope, hidden, *refs):
    states, refs = regrouped(refs, taken)
    error_count, input_count = pieces
    errors, inputs = refs[:error_count], refs[error_count : error_count + input_count]
    error, error_t, rows, inputs_t = refs[-4:]
    refs = refs[error_count + input_count : -4]
    results, _ = regrouped(refs[len(refs) - sum(given) :], given)
    error, rows = joined(errors, error), joined(inputs, rows)

    @pl.when(pl.program_id(0) == 0)
    def _():
        error_t[...] = error[...].T
        inputs_t[...] = rows[...].T

    back = jnp.dot(error[...], weights[0].astype(bf16), preferred_element_type=f32) * slope[...].astype(f32)
    for k, (left, right) in enumerate(((inputs_t[...], back.astype(bf16)), (error_t[...], hidden[...]))):
        grad = jnp.dot(left, right, preferred_element_type=f32)
        values = update(grad, *[loaded(state, k) for state in states])
        for result, apart, value in zip(results, by_core, values):
            if type(result) is not tuple:
                result[k] = value.astype(result.dtype)
                continue
            if apart:
                for place, piece in enumerate(result):

                    @pl.when((flag[0] == k) == (place == 0))
                    def _():
                        piece[...] = value.astype(piece.dtype)

                continue
            each = len(result) // 2
            for i, piece in enumerate(result[k * each : (k + 1) * each]):
                size = piece.shape[0]
                piece[...] = value[i * size : (i + 1) * size].astype(piece.dtype)


def backward(flag, errors, weights, slope, hidden, inputs, states, update, kinds, waits=()):
    rows, width = hidden.shape[0], weights.shape[1]
    units = weights.shape[2]
    block = min(units, 512)
    counts, flat = flattened(states)
    kinds = [kind if type(kind) is tuple else (kind, 1) for kind in kinds]
    by_core = [count == "core" for _, count in kinds]
    kinds = [(kind, 2 if apart else count) for (kind, count), apart in zip(kinds, by_core)]
    shapes = []
    for kind, count in kinds:
        shape = weights.shape if count == 1 else (2 * width // count, units)
        shapes += [jax.ShapeDtypeStruct(shape, kind)] * count
    results = pl.pallas_call(
        functools.partial(
            backward_kernel, update, counts, (len(errors), len(inputs)), [count for _, count in kinds], by_core
        ),
        grid=(units // block,),
        in_specs=[
            pl.BlockSpec(memory_space=pltpu.SMEM),
            pl.BlockSpec((1, width, block), lambda j: (1, 0, j)),
            pl.BlockSpec((rows, block), lambda j: (0, j)),
            pl.BlockSpec((rows, block), lambda j: (0, j)),
        ]
        + [block_of(part, block) for part in flat]
        + [whole(piece.shape) for piece in (*errors, *inputs)]
        + [ANY] * len(waits),
        out_specs=[block_of(shape, block) for shape in shapes],
        out_shape=shapes,
        scratch_shapes=[pltpu.VMEM((rows, width), bf16), pltpu.VMEM((width, rows), bf16)] * 2,
        compiler_params=pltpu.CompilerParams(vmem_limit_bytes=56 << 20),
        cost_estimate=LIGHT,
    )(flag, weights, slope, hidden, *flat, *errors, *inputs, *waits)
    return regrouped(results, [count for _, count in kinds])[0]


def first_update(grad, moment):
    moment = inner_beta * moment + grad
    return (moment, moment)


def first_beside(grad, moment, own_moment, weights):
    moment = inner_beta * moment + grad
    return (moment, weights - 0.5 * learn_rate * (own_moment + moment))


def second_update(grad, moment, weights):
    moment_new = inner_beta * moment + grad
    return (moment_new, weights - learn_rate * moment_new, moment + (1.0 + inner_beta) * moment_new)


def second_beside(grad, moment, weights):
    return (weights - learn_rate * (inner_beta * moment + grad),)


def third_update(grad, moment, known):
    return (inner_beta * moment + grad, known + grad)


def rounded(value):
    return lax.reduce_precision(value, 8, 7).astype(bf16)


def added(left, right):
    return rounded(left.astype(f32) + right.astype(f32))


def nothing(*refs):
    pass


def tied(waits, block):
    return pl.pallas_call(
        nothing,
        in_specs=[ANY] * (1 + len(waits)),
        out_specs=ANY,
        out_shape=jax.ShapeDtypeStruct(block.shape, block.dtype),
        input_output_aliases={0: 0},
        cost_estimate=LIGHT,
    )(block, *waits)


def finish_kernel(replicas, flag, slow, anchor, own, theirs, *refs):
    anchor_new, slow_new, token = refs[-3:]
    for k in range(2):
        total = jnp.where(flag[0] == k, own[...].astype(f32), theirs[...].astype(f32))
        value = slow_beta * slow[k] + total / replicas
        slow_new[k] = value
        anchor_new[k] = anchor[k] - learn_rate * value
    token[...] = jnp.zeros_like(token)


def finish(flag, replicas, slow, anchor, own, theirs, position, before):
    size, units = own.shape
    steps = 4
    rows = pl.BlockSpec((2, size // steps, units), lambda j: (0, position * steps + j, 0))
    part = pl.BlockSpec((size // steps, units), lambda j: (j, 0))
    shape = jax.ShapeDtypeStruct(slow.shape, f32)
    return pl.pallas_call(
        functools.partial(finish_kernel, replicas),
        grid=(steps,),
        in_specs=[pl.BlockSpec(memory_space=pltpu.SMEM), rows, rows, part, part] + [ANY] * len(before),
        out_specs=[rows, rows, whole((8, 128))],
        out_shape=[shape, shape, jax.ShapeDtypeStruct((8, 128), bf16)],
        input_output_aliases={5 + k: k for k in range(len(before))},
        compiler_params=pltpu.CompilerParams(vmem_limit_bytes=60 << 20),
        cost_estimate=LIGHT,
    )(flag, slow, anchor, own, theirs, *before)


def slow_step(flag, mine, other, slow, anchor):
    axis, cores = "replica", 2
    index = lax.axis_index(axis)
    replicas = lax.axis_size(axis)
    chip = index // cores
    length = replicas // cores
    half = length // 2
    rows = mine.shape[0]
    size = rows // chunks

    def moved(part, hops):
        return lax.ppermute(part, axis, [(cores * a + c, cores * b + c) for a, b in hops for c in range(cores)])

    def at(places):
        return functools.reduce(jnp.logical_or, [chip == place for place in places])

    stages = [(True, [(s, s + 1), (length - 1 - s, length - 2 - s)]) for s in range(half - 1)]
    if half:
        stages.append((True, [(half - 1, half), (half, half - 1)]))
    stages += [(False, [(s + 1, s), (length - 2 - s, length - 1 - s)]) for s in reversed(range(half - 1))]

    pair_rows = rows // 2
    pairs = [swapped(other[p * pair_rows : (p + 1) * pair_rows], axis, 1) for p in range(2)]
    blocks = []
    for c in range(chunks):
        p, start = divmod(c * size, pair_rows)
        blocks.append(added(mine[c * size : (c + 1) * size], pairs[p][start : start + size]))
    arrived, made, results, tokens = {}, {}, [], []
    final = len(stages) - 1
    for tick in range(chunks + len(stages)):
        for s in reversed(range(len(stages) + 1)):
            c = tick - s
            if not 0 <= c < chunks:
                continue
            block = blocks[c]
            if s:
                adds, hops = stages[s - 1]
                fresh = added(block, arrived[s - 1, c]) if adds else arrived[s - 1, c]
                block = jnp.where(at([b for _, b in hops]), fresh, block)
                if s == final and c >= 3:
                    block = tied([tokens[c - 3]], block)
                elif s > final and c >= 3:
                    block = tied([tokens[c - 1]], block)
            if s == 0 and c >= 3 and (2, c - 3) in made:
                block = tied([made[2, c - 3]], block)
            blocks[c] = made[s, c] = block
            if s < len(stages):
                arrived[s, c] = moved(block, stages[s][1])
            else:
                theirs = swapped(block, axis, 1)
                *results, token = finish(flag, replicas, slow, anchor, block, theirs, c, results)
                tokens.append(token)
    return results


def body(tokens, targets, row_ids, anchor, momentum, slow):
    row_count = tokens.shape[0]
    scale = 1.0 / row_count
    tensors = lax.axis_size("tensor")
    share_rows = row_count // tensors
    order = lax.axis_index("tensor") ^ jnp.arange(tensors)
    picks_all = row_ids[0].reshape(INNER, tensors, share_rows)[:, order].reshape(INNER, row_count)

    replicas = lax.axis_size("replica")
    flag = (lax.axis_index("replica") % 2).astype(jnp.int32).reshape(1)

    def gathered(own):
        return [own] + [swapped(own, "tensor", m) for m in range(1, tensors)]

    def error_share(partials, step):
        wanted = targets.at[picks_all[step, :share_rows]].get(mode="promise_in_bounds")
        share = partials[0].astype(f32)
        for m in range(1, tensors):
            share = share + swapped(partials[m], "tensor", m).astype(f32)
        return ((share - wanted.astype(f32)) * scale).astype(bf16)

    def sent(block, distance, which=(0, 1)):
        route = [((i - distance) % replicas, i) for i in range(replicas) if i % 2 in which]
        return lax.ppermute(block, "replica", route)

    def picked(step, count):
        return tokens.at[picks_all[step, :count]].get(mode="promise_in_bounds")

    near_share = sent(picked(0, share_rows), 1)
    moment_near = sent(tied([near_share], momentum[0].astype(bf16)), 1)

    inputs = [picked(0, row_count)]
    hidden, slope, *partials = forward(flag, inputs, [anchor], only, tensors, emits=False)
    error = jnp.concatenate(gathered(error_share(partials, 0)))
    error_near = sent(error, 1)
    inputs_near = gathered(near_share)
    hidden_near, slope_near = forward(flag, inputs_near, [anchor], only, 0, emits=False)
    moment, moment_bf = backward(
        flag,
        [error],
        anchor,
        slope,
        hidden,
        inputs,
        [momentum[0]],
        first_update,
        [f32, bf16],
        waits=[hidden_near],
    )
    moment_far = sent(tied([error_near], moment_bf), 2, (0,))
    moment_near, weights = backward(
        flag,
        [error_near],
        anchor,
        slope_near,
        hidden_near,
        inputs_near,
        [moment_near, moment, anchor],
        first_beside,
        [bf16, bf16],
    )

    inputs = [tied([moment_near], picked(1, row_count))]
    inputs_far = sent(inputs[0], 2, (1,))
    moment_two = sent(moment_near, 1, (1,))
    moment_three = sent(moment_far, 1, (1,))
    hidden, slope, *partials = forward(flag, inputs, [weights], only, tensors, emits=False)
    error = jnp.concatenate(gathered(error_share(partials, 1)))
    error_far = sent(error, 2, (1,))
    moment, weights, known = backward(
        flag,
        [error],
        weights,
        slope,
        hidden,
        inputs,
        [moment, weights],
        second_update,
        [f32, bf16, bf16],
        waits=[inputs_far],
    )
    weights = tied([error_far], weights)
    weights_sent = sent(weights, 2, (0,))
    hidden, slope, weights_far = forward(flag, [inputs_far], [anchor, moment_two, moment_three], pushed, 0)
    (weights_found,) = backward(
        flag, [error_far], weights_far, slope, hidden, [inputs_far], [moment_two, weights_far], second_beside, [bf16]
    )

    inputs = [picked(2, row_count)]
    hidden, slope, *rest = forward(flag, inputs, [weights_found, weights, weights_sent], halved, tensors)
    errors = gathered(error_share(rest[:tensors], 2))
    moment, total = backward(
        flag, errors, rest[tensors], slope, hidden, inputs, [moment, known], third_update, [f32, (bf16, "core")]
    )
    anchor_new, slow_new = slow_step(flag, *total, slow, anchor)
    return (anchor_new, slow_new, moment[None])


def solution(mesh):
    return jax.shard_map(
        body,
        mesh=mesh,
        in_specs=(
            P("replica", None),
            P("replica", None),
            P("replica", None, None),
            P(None, None, "tensor"),
            P("replica", None, None, "tensor"),
            P(None, None, "tensor"),
        ),
        out_specs=(
            P(None, None, "tensor"),
            P(None, None, "tensor"),
            P("replica", None, None, "tensor"),
        ),
        check_vma=False,
    )
```

```python
import functools

import jax
import jax.numpy as jnp
from jax import lax
from jax.experimental import pallas as pl
from jax.experimental.pallas import tpu as pltpu
from jax.sharding import PartitionSpec as P

INNER = 3


learn_rate = 0.02
inner_beta = 0.9
slow_beta = 0.5
chunks = 4
bf16, f32 = jnp.bfloat16, jnp.float32
ANY = pl.BlockSpec(memory_space=pl.ANY)
LIGHT = pl.CostEstimate(flops=1, bytes_accessed=1, transcendentals=0)


def swapped(block, axis, mask):
    return lax.ppermute(block, axis, [(i, i ^ mask) for i in range(lax.axis_size(axis))])


def gelu_pair(pre):
    coeff = 0.7978845608028654
    square = pre * pre
    tanh_val = jnp.tanh(coeff * (pre + 0.044715 * square * pre))
    half = 0.5 * (1.0 + tanh_val)
    slope = half + 0.5 * pre * (1.0 - tanh_val * tanh_val) * coeff * (1.0 + 3.0 * 0.044715 * square)
    return (pre * half, slope)


def whole(shape):
    return pl.BlockSpec(shape, lambda j: (0,) * len(shape))


def loaded(state, k):
    if type(state) is not tuple:
        return state[k].astype(f32)
    each = len(state) // 2
    return jnp.concatenate([piece[...].astype(f32) for piece in state[k * each : (k + 1) * each]], axis=0)


def regrouped(refs, counts):
    refs, states = list(refs), []
    for count in counts:
        states.append(tuple(refs[:count]) if count > 1 else refs[0])
        del refs[:count]
    return states, refs


def flattened(states):
    flat = [state if type(state) is tuple else (state,) for state in states]
    return [len(state) for state in flat], [part for state in flat for part in state]


def block_of(part, block, parts=2):
    if part.ndim == 2:
        return pl.BlockSpec((part.shape[0], block), lambda j: (0, j))
    return pl.BlockSpec((parts, part.shape[1], block), lambda j: (0, 0, j))


def joined(pieces, place):
    if len(pieces) == 1:
        return pieces[0]

    @pl.when(pl.program_id(0) == 0)
    def _():
        size = pieces[0].shape[0]
        for b, piece in enumerate(pieces):
            place[b * size : (b + 1) * size] = piece[...]

    return place


def forward_kernel(mix, taken, pieces, waits, sums, emits, flag, *refs):
    rows, refs = refs[:pieces], refs[pieces:]
    sources, refs = regrouped(refs, taken)
    refs = refs[waits:]
    hidden, slope = refs[:2]
    inputs = joined(rows, refs[-1])
    block = [mix(flag[0], *[loaded(source, k) for source in sources]).astype(bf16) for k in range(2 if sums or emits else 1)]
    if emits:
        for k in range(2):
            refs[2 + sums][k] = block[k]
    j = pl.program_id(0)
    value, slope_val = gelu_pair(jnp.dot(inputs[...], block[0], preferred_element_type=f32))
    value = value.astype(bf16)
    hidden[...] = value
    slope[...] = slope_val.astype(bf16)
    if sums:
        partials, total = refs[2 : 2 + sums], refs[-2]
        out = lax.dot_general(value, block[1], (((1,), (1,)), ((), ())), preferred_element_type=f32)

        @pl.when(j == 0)
        def _():
            total[...] = out

        @pl.when(j > 0)
        def _():
            total[...] += out

        @pl.when(j == pl.num_programs(0) - 1)
        def _():
            size = partials[0].shape[0]
            for b, partial in enumerate(partials):
                partial[...] = total[b * size : (b + 1) * size].astype(bf16)


def forward(flag, inputs, sources, mix, sums, emits=True, waits=()):
    count, width = inputs[0].shape
    rows = count * len(inputs)
    units = sources[0].shape[2]
    block = min(units, 512)
    parts = 2 if sums or emits else 1
    counts, flat = flattened(sources)
    unit_spec = pl.BlockSpec((rows, block), lambda j: (0, j))
    shapes = [((rows, units), unit_spec), ((rows, units), unit_spec)]
    if sums:
        shapes += [((rows // sums, width), whole((rows // sums, width)))] * sums
    shapes += [(sources[0].shape, block_of(sources[0], block))] * emits
    return pl.pallas_call(
        functools.partial(forward_kernel, mix, counts, len(inputs), len(waits), sums, emits),
        grid=(units // block,),
        in_specs=[pl.BlockSpec(memory_space=pltpu.SMEM)]
        + [whole(piece.shape) for piece in inputs]
        + [block_of(part, block, parts) for part in flat]
        + [ANY] * len(waits),
        out_specs=[spec for _, spec in shapes],
        out_shape=[jax.ShapeDtypeStruct(shape, bf16) for shape, _ in shapes],
        scratch_shapes=[pltpu.VMEM((rows, width), f32)] * bool(sums) + [pltpu.VMEM((rows, width), bf16)],
        compiler_params=pltpu.CompilerParams(vmem_limit_bytes=36 << 20),
        cost_estimate=LIGHT,
    )(flag, *inputs, *flat, *waits)


def only(flag, weights):
    return weights


def pushed(flag, weights, first, second):
    return weights - 0.5 * learn_rate * (first + second)


def halved(flag, found, weights, sent):
    return 0.5 * (weights + jnp.where(flag == 0, sent, found))


def backward_kernel(update, taken, pieces, given, by_core, flag, weights, slope, hidden, *refs):
    states, refs = regrouped(refs, taken)
    error_count, input_count = pieces
    errors, inputs = refs[:error_count], refs[error_count : error_count + input_count]
    error, error_t, rows, inputs_t = refs[-4:]
    refs = refs[error_count + input_count : -4]
    results, _ = regrouped(refs[len(refs) - sum(given) :], given)
    error, rows = joined(errors, error), joined(inputs, rows)

    @pl.when(pl.program_id(0) == 0)
    def _():
        error_t[...] = error[...].T
        inputs_t[...] = rows[...].T

    back = jnp.dot(error[...], weights[0].astype(bf16), preferred_element_type=f32) * slope[...].astype(f32)
    for k, (left, right) in enumerate(((inputs_t[...], back.astype(bf16)), (error_t[...], hidden[...]))):
        grad = jnp.dot(left, right, preferred_element_type=f32)
        values = update(grad, *[loaded(state, k) for state in states])
        for result, apart, value in zip(results, by_core, values):
            if type(result) is not tuple:
                result[k] = value.astype(result.dtype)
                continue
            if apart:
                for place, piece in enumerate(result):

                    @pl.when((flag[0] == k) == (place == 0))
                    def _():
                        piece[...] = value.astype(piece.dtype)

                continue
            each = len(result) // 2
            for i, piece in enumerate(result[k * each : (k + 1) * each]):
                size = piece.shape[0]
                piece[...] = value[i * size : (i + 1) * size].astype(piece.dtype)


def backward(flag, errors, weights, slope, hidden, inputs, states, update, kinds, waits=()):
    rows, width = hidden.shape[0], weights.shape[1]
    units = weights.shape[2]
    block = min(units, 512)
    counts, flat = flattened(states)
    kinds = [kind if type(kind) is tuple else (kind, 1) for kind in kinds]
    by_core = [count == "core" for _, count in kinds]
    kinds = [(kind, 2 if apart else count) for (kind, count), apart in zip(kinds, by_core)]
    shapes = []
    for kind, count in kinds:
        shape = weights.shape if count == 1 else (2 * width // count, units)
        shapes += [jax.ShapeDtypeStruct(shape, kind)] * count
    results = pl.pallas_call(
        functools.partial(
            backward_kernel, update, counts, (len(errors), len(inputs)), [count for _, count in kinds], by_core
        ),
        grid=(units // block,),
        in_specs=[
            pl.BlockSpec(memory_space=pltpu.SMEM),
            pl.BlockSpec((1, width, block), lambda j: (1, 0, j)),
            pl.BlockSpec((rows, block), lambda j: (0, j)),
            pl.BlockSpec((rows, block), lambda j: (0, j)),
        ]
        + [block_of(part, block) for part in flat]
        + [whole(piece.shape) for piece in (*errors, *inputs)]
        + [ANY] * len(waits),
        out_specs=[block_of(shape, block) for shape in shapes],
        out_shape=shapes,
        scratch_shapes=[pltpu.VMEM((rows, width), bf16), pltpu.VMEM((width, rows), bf16)] * 2,
        compiler_params=pltpu.CompilerParams(vmem_limit_bytes=46 << 20),
        cost_estimate=LIGHT,
    )(flag, weights, slope, hidden, *flat, *errors, *inputs, *waits)
    return regrouped(results, [count for _, count in kinds])[0]


def first_update(grad, moment):
    moment = inner_beta * moment + grad
    return (moment, moment)


def first_beside(grad, moment, own_moment, weights):
    moment = inner_beta * moment + grad
    return (moment, weights - 0.5 * learn_rate * (own_moment + moment))


def second_update(grad, moment, weights):
    moment_new = inner_beta * moment + grad
    return (moment_new, weights - learn_rate * moment_new, moment + (1.0 + inner_beta) * moment_new)


def second_beside(grad, moment, weights):
    return (weights - learn_rate * (inner_beta * moment + grad),)


def third_update(grad, moment, known):
    return (inner_beta * moment + grad, known + grad)


def rounded(value):
    return lax.reduce_precision(value, 8, 7).astype(bf16)


def added(left, right):
    return rounded(left.astype(f32) + right.astype(f32))


def nothing(*refs):
    pass


def tied(waits, block):
    return pl.pallas_call(
        nothing,
        in_specs=[ANY] * (1 + len(waits)),
        out_specs=ANY,
        out_shape=jax.ShapeDtypeStruct(block.shape, block.dtype),
        input_output_aliases={0: 0},
        cost_estimate=LIGHT,
    )(block, *waits)


def finish_kernel(replicas, flag, slow, anchor, own, theirs, *refs):
    anchor_new, slow_new, token = refs[-3:]
    for k in range(2):
        total = jnp.where(flag[0] == k, own[...].astype(f32), theirs[...].astype(f32))
        value = slow_beta * slow[k] + total / replicas
        slow_new[k] = value
        anchor_new[k] = anchor[k] - learn_rate * value
    token[...] = jnp.zeros_like(token)


def finish(flag, replicas, slow, anchor, own, theirs, position, before):
    size, units = own.shape
    steps = 4
    rows = pl.BlockSpec((2, size // steps, units), lambda j: (0, position * steps + j, 0))
    part = pl.BlockSpec((size // steps, units), lambda j: (j, 0))
    shape = jax.ShapeDtypeStruct(slow.shape, f32)
    return pl.pallas_call(
        functools.partial(finish_kernel, replicas),
        grid=(steps,),
        in_specs=[pl.BlockSpec(memory_space=pltpu.SMEM), rows, rows, part, part] + [ANY] * len(before),
        out_specs=[rows, rows, whole((8, 128))],
        out_shape=[shape, shape, jax.ShapeDtypeStruct((8, 128), bf16)],
        input_output_aliases={5 + k: k for k in range(len(before))},
        compiler_params=pltpu.CompilerParams(vmem_limit_bytes=60 << 20),
        cost_estimate=LIGHT,
    )(flag, slow, anchor, own, theirs, *before)


def slow_step(flag, mine, other, slow, anchor):
    axis, cores = "replica", 2
    index = lax.axis_index(axis)
    replicas = lax.axis_size(axis)
    chip = index // cores
    length = replicas // cores
    half = length // 2
    rows = mine.shape[0]
    size = rows // chunks

    def moved(part, hops):
        return lax.ppermute(part, axis, [(cores * a + c, cores * b + c) for a, b in hops for c in range(cores)])

    def at(places):
        return functools.reduce(jnp.logical_or, [chip == place for place in places])

    stages = [(True, [(s, s + 1), (length - 1 - s, length - 2 - s)]) for s in range(half - 1)]
    if half:
        stages.append((True, [(half - 1, half), (half, half - 1)]))
    stages += [(False, [(s + 1, s), (length - 2 - s, length - 1 - s)]) for s in reversed(range(half - 1))]

    pair_rows = rows // 2
    pairs = [swapped(other[p * pair_rows : (p + 1) * pair_rows], axis, 1) for p in range(2)]
    blocks = []
    for c in range(chunks):
        p, start = divmod(c * size, pair_rows)
        blocks.append(added(mine[c * size : (c + 1) * size], pairs[p][start : start + size]))
    arrived, made, results, tokens = {}, {}, [], []
    final = len(stages) - 1
    for tick in range(chunks + len(stages)):
        for s in reversed(range(len(stages) + 1)):
            c = tick - s
            if not 0 <= c < chunks:
                continue
            block = blocks[c]
            if s:
                adds, hops = stages[s - 1]
                fresh = added(block, arrived[s - 1, c]) if adds else arrived[s - 1, c]
                block = jnp.where(at([b for _, b in hops]), fresh, block)
                if s > final and c >= 3:
                    block = tied([tokens[c - 1]], block)
            if s == 0 and c >= 3 and (2, c - 3) in made:
                block = tied([made[2, c - 3]], block)
            blocks[c] = made[s, c] = block
            if s < len(stages):
                arrived[s, c] = moved(block, stages[s][1])
            else:
                theirs = swapped(block, axis, 1)
                *results, token = finish(flag, replicas, slow, anchor, block, theirs, c, results)
                tokens.append(token)
    return results


def body(tokens, targets, row_ids, anchor, momentum, slow):
    row_count = tokens.shape[0]
    scale = 1.0 / row_count
    tensors = lax.axis_size("tensor")
    share_rows = row_count // tensors
    order = lax.axis_index("tensor") ^ jnp.arange(tensors)
    picks_all = row_ids[0].reshape(INNER, tensors, share_rows)[:, order].reshape(INNER, row_count)

    replicas = lax.axis_size("replica")
    flag = (lax.axis_index("replica") % 2).astype(jnp.int32).reshape(1)

    def gathered(own):
        return [own] + [swapped(own, "tensor", m) for m in range(1, tensors)]

    def error_share(partials, step):
        wanted = targets.at[picks_all[step, :share_rows]].get(mode="promise_in_bounds")
        share = partials[0].astype(f32)
        for m in range(1, tensors):
            share = share + swapped(partials[m], "tensor", m).astype(f32)
        return ((share - wanted.astype(f32)) * scale).astype(bf16)

    def sent(block, distance, which=(0, 1)):
        route = [((i - distance) % replicas, i) for i in range(replicas) if i % 2 in which]
        return lax.ppermute(block, "replica", route)

    def picked(step, count):
        return tokens.at[picks_all[step, :count]].get(mode="promise_in_bounds")

    near_share = sent(picked(0, share_rows), 1)
    narrow = tied([near_share], momentum[0].astype(bf16))
    moment_near = sent(narrow, 1)

    inputs = [picked(0, row_count)]
    hidden, slope, *partials = forward(flag, inputs, [anchor], only, tensors, emits=False, waits=[narrow])
    error = jnp.concatenate(gathered(error_share(partials, 0)))
    error_near = sent(error, 1)
    inputs_near = gathered(near_share)
    hidden_near, slope_near = forward(flag, inputs_near, [anchor], only, 0, emits=False)
    moment, moment_bf = backward(
        flag,
        [error],
        anchor,
        slope,
        hidden,
        inputs,
        [momentum[0]],
        first_update,
        [f32, (bf16, 2)],
    )
    moment_far = [sent(tied([error_near, hidden_near], part), 2, (0,)) for part in moment_bf]
    moment_near, weights = backward(
        flag,
        [error_near],
        anchor,
        slope_near,
        hidden_near,
        inputs_near,
        [moment_near, moment, anchor],
        first_beside,
        [(bf16, 2), bf16],
    )

    inputs = [tied([moment_near[0]], picked(1, row_count))]
    inputs_far = sent(inputs[0], 2, (1,))
    hidden, slope, *partials = forward(flag, inputs, [weights], only, tensors, emits=False)
    error = jnp.concatenate(gathered(error_share(partials, 1)))
    error_far = sent(error, 2, (1,))
    moment, weights, known = backward(
        flag,
        [error],
        weights,
        slope,
        hidden,
        inputs,
        [moment, weights],
        second_update,
        [f32, bf16, bf16],
        waits=[inputs_far, *moment_far],
    )
    weights = tied([error_far], weights)
    weights_sent = sent(weights, 2, (0,))
    moment_two = tuple(sent(tied([weights], part), 1, (1,)) for part in moment_near)
    moment_three = tuple(sent(tied([weights], part), 1, (1,)) for part in moment_far)
    hidden, slope, weights_far = forward(flag, [inputs_far], [anchor, moment_two, moment_three], pushed, 0)
    (weights_found,) = backward(
        flag, [error_far], weights_far, slope, hidden, [inputs_far], [moment_two, weights_far], second_beside, [bf16]
    )

    inputs = [picked(2, row_count)]
    hidden, slope, *rest = forward(flag, inputs, [weights_found, weights, weights_sent], halved, tensors)
    errors = gathered(error_share(rest[:tensors], 2))
    moment, total = backward(
        flag, errors, rest[tensors], slope, hidden, inputs, [moment, known], third_update, [f32, (bf16, "core")]
    )
    anchor_new, slow_new = slow_step(flag, *total, slow, anchor)
    return (anchor_new, slow_new, moment[None])


def solution(mesh):
    return jax.shard_map(
        body,
        mesh=mesh,
        in_specs=(
            P("replica", None),
            P("replica", None),
            P("replica", None, None),
            P(None, None, "tensor"),
            P("replica", None, None, "tensor"),
            P(None, None, "tensor"),
        ),
        out_specs=(
            P(None, None, "tensor"),
            P(None, None, "tensor"),
            P("replica", None, None, "tensor"),
        ),
        check_vma=False,
    )
```

```python
import functools

import jax
import jax.numpy as jnp
from jax import lax
from jax.experimental import pallas as pl
from jax.experimental.pallas import tpu as pltpu
from jax.sharding import PartitionSpec as P

INNER = 3


learn_rate = 0.02
inner_beta = 0.9
slow_beta = 0.5
chunks = 4
bf16, f32 = jnp.bfloat16, jnp.float32
ANY = pl.BlockSpec(memory_space=pl.ANY)
LIGHT = pl.CostEstimate(flops=1, bytes_accessed=1, transcendentals=0)


def swapped(block, axis, mask):
    return lax.ppermute(block, axis, [(i, i ^ mask) for i in range(lax.axis_size(axis))])


def gelu_pair(pre):
    coeff = 0.7978845608028654
    square = pre * pre
    tanh_val = jnp.tanh(coeff * (pre + 0.044715 * square * pre))
    half = 0.5 * (1.0 + tanh_val)
    slope = half + 0.5 * pre * (1.0 - tanh_val * tanh_val) * coeff * (1.0 + 3.0 * 0.044715 * square)
    return (pre * half, slope)


def whole(shape):
    return pl.BlockSpec(shape, lambda j: (0,) * len(shape))


def loaded(state, k):
    if type(state) is not tuple:
        return state[k].astype(f32)
    each = len(state) // 2
    return jnp.concatenate([piece[...].astype(f32) for piece in state[k * each : (k + 1) * each]], axis=0)


def regrouped(refs, counts):
    refs, states = list(refs), []
    for count in counts:
        states.append(tuple(refs[:count]) if count > 1 else refs[0])
        del refs[:count]
    return states, refs


def flattened(states):
    flat = [state if type(state) is tuple else (state,) for state in states]
    return [len(state) for state in flat], [part for state in flat for part in state]


def block_of(part, block, parts=2):
    if part.ndim == 2:
        return pl.BlockSpec((part.shape[0], block), lambda j: (0, j))
    return pl.BlockSpec((parts, part.shape[1], block), lambda j: (0, 0, j))


def joined(pieces, place):
    if len(pieces) == 1:
        return pieces[0]

    @pl.when(pl.program_id(0) == 0)
    def _():
        size = pieces[0].shape[0]
        for b, piece in enumerate(pieces):
            place[b * size : (b + 1) * size] = piece[...]

    return place


def forward_kernel(mix, taken, pieces, waits, sums, emits, flag, *refs):
    rows, refs = refs[:pieces], refs[pieces:]
    sources, refs = regrouped(refs, taken)
    refs = refs[waits:]
    hidden, slope = refs[:2]
    inputs = joined(rows, refs[-1])
    block = [mix(flag[0], *[loaded(source, k) for source in sources]).astype(bf16) for k in range(2 if sums or emits else 1)]
    if emits:
        for k in range(2):
            refs[2 + sums][k] = block[k]
    j = pl.program_id(0)
    value, slope_val = gelu_pair(jnp.dot(inputs[...], block[0], preferred_element_type=f32))
    value = value.astype(bf16)
    hidden[...] = value
    slope[...] = slope_val.astype(bf16)
    if sums:
        partials, total = refs[2 : 2 + sums], refs[-2]
        out = lax.dot_general(value, block[1], (((1,), (1,)), ((), ())), preferred_element_type=f32)

        @pl.when(j == 0)
        def _():
            total[...] = out

        @pl.when(j > 0)
        def _():
            total[...] += out

        @pl.when(j == pl.num_programs(0) - 1)
        def _():
            size = partials[0].shape[0]
            for b, partial in enumerate(partials):
                partial[...] = total[b * size : (b + 1) * size].astype(bf16)


def forward(flag, inputs, sources, mix, sums, emits=True, waits=()):
    count, width = inputs[0].shape
    rows = count * len(inputs)
    units = sources[0].shape[2]
    block = min(units, 512)
    parts = 2 if sums or emits else 1
    counts, flat = flattened(sources)
    unit_spec = pl.BlockSpec((rows, block), lambda j: (0, j))
    shapes = [((rows, units), unit_spec), ((rows, units), unit_spec)]
    if sums:
        shapes += [((rows // sums, width), whole((rows // sums, width)))] * sums
    shapes += [(sources[0].shape, block_of(sources[0], block))] * emits
    return pl.pallas_call(
        functools.partial(forward_kernel, mix, counts, len(inputs), len(waits), sums, emits),
        grid=(units // block,),
        in_specs=[pl.BlockSpec(memory_space=pltpu.SMEM)]
        + [whole(piece.shape) for piece in inputs]
        + [block_of(part, block, parts) for part in flat]
        + [ANY] * len(waits),
        out_specs=[spec for _, spec in shapes],
        out_shape=[jax.ShapeDtypeStruct(shape, bf16) for shape, _ in shapes],
        scratch_shapes=[pltpu.VMEM((rows, width), f32)] * bool(sums) + [pltpu.VMEM((rows, width), bf16)],
        compiler_params=pltpu.CompilerParams(vmem_limit_bytes=56 << 20),
        cost_estimate=LIGHT,
    )(flag, *inputs, *flat, *waits)


def only(flag, weights):
    return weights


def pushed(flag, weights, first, second):
    return weights - 0.5 * learn_rate * (first + second)


def halved(flag, found, weights, sent):
    return 0.5 * (weights + jnp.where(flag == 0, sent, found))


def backward_kernel(update, taken, pieces, given, by_core, flag, weights, slope, hidden, *refs):
    states, refs = regrouped(refs, taken)
    error_count, input_count = pieces
    errors, inputs = refs[:error_count], refs[error_count : error_count + input_count]
    error, error_t, rows, inputs_t = refs[-4:]
    refs = refs[error_count + input_count : -4]
    results, _ = regrouped(refs[len(refs) - sum(given) :], given)
    error, rows = joined(errors, error), joined(inputs, rows)

    @pl.when(pl.program_id(0) == 0)
    def _():
        error_t[...] = error[...].T
        inputs_t[...] = rows[...].T

    back = jnp.dot(error[...], weights[0].astype(bf16), preferred_element_type=f32) * slope[...].astype(f32)
    for k, (left, right) in enumerate(((inputs_t[...], back.astype(bf16)), (error_t[...], hidden[...]))):
        grad = jnp.dot(left, right, preferred_element_type=f32)
        values = update(grad, *[loaded(state, k) for state in states])
        for result, apart, value in zip(results, by_core, values):
            if type(result) is not tuple:
                result[k] = value.astype(result.dtype)
                continue
            if apart:
                for place, piece in enumerate(result):

                    @pl.when((flag[0] == k) == (place == 0))
                    def _():
                        piece[...] = value.astype(piece.dtype)

                continue
            each = len(result) // 2
            for i, piece in enumerate(result[k * each : (k + 1) * each]):
                size = piece.shape[0]
                piece[...] = value[i * size : (i + 1) * size].astype(piece.dtype)


def backward(flag, errors, weights, slope, hidden, inputs, states, update, kinds, waits=()):
    rows, width = hidden.shape[0], weights.shape[1]
    units = weights.shape[2]
    block = min(units, 512)
    counts, flat = flattened(states)
    kinds = [kind if type(kind) is tuple else (kind, 1) for kind in kinds]
    by_core = [count == "core" for _, count in kinds]
    kinds = [(kind, 2 if apart else count) for (kind, count), apart in zip(kinds, by_core)]
    shapes = []
    for kind, count in kinds:
        shape = weights.shape if count == 1 else (2 * width // count, units)
        shapes += [jax.ShapeDtypeStruct(shape, kind)] * count
    results = pl.pallas_call(
        functools.partial(
            backward_kernel, update, counts, (len(errors), len(inputs)), [count for _, count in kinds], by_core
        ),
        grid=(units // block,),
        in_specs=[
            pl.BlockSpec(memory_space=pltpu.SMEM),
            pl.BlockSpec((1, width, block), lambda j: (1, 0, j)),
            pl.BlockSpec((rows, block), lambda j: (0, j)),
            pl.BlockSpec((rows, block), lambda j: (0, j)),
        ]
        + [block_of(part, block) for part in flat]
        + [whole(piece.shape) for piece in (*errors, *inputs)]
        + [ANY] * len(waits),
        out_specs=[block_of(shape, block) for shape in shapes],
        out_shape=shapes,
        scratch_shapes=[pltpu.VMEM((rows, width), bf16), pltpu.VMEM((width, rows), bf16)] * 2,
        compiler_params=pltpu.CompilerParams(vmem_limit_bytes=56 << 20),
        cost_estimate=LIGHT,
    )(flag, weights, slope, hidden, *flat, *errors, *inputs, *waits)
    return regrouped(results, [count for _, count in kinds])[0]


def first_update(grad, moment):
    moment = inner_beta * moment + grad
    return (moment, moment)


def first_beside(grad, moment, own_moment, weights):
    moment = inner_beta * moment + grad
    return (moment, weights - 0.5 * learn_rate * (own_moment + moment))


def second_update(grad, moment, weights):
    moment_new = inner_beta * moment + grad
    return (moment_new, weights - learn_rate * moment_new, moment + (1.0 + inner_beta) * moment_new)


def second_beside(grad, moment, weights):
    return (weights - learn_rate * (inner_beta * moment + grad),)


def third_update(grad, moment, known):
    return (inner_beta * moment + grad, known + grad)


def rounded(value):
    return lax.reduce_precision(value, 8, 7).astype(bf16)


def added(left, right):
    return rounded(left.astype(f32) + right.astype(f32))


def nothing(*refs):
    pass


def tied(waits, block):
    return pl.pallas_call(
        nothing,
        in_specs=[ANY] * (1 + len(waits)),
        out_specs=ANY,
        out_shape=jax.ShapeDtypeStruct(block.shape, block.dtype),
        input_output_aliases={0: 0},
        cost_estimate=LIGHT,
    )(block, *waits)


def finish_kernel(replicas, flag, slow, anchor, own, theirs, *refs):
    anchor_new, slow_new, token = refs[-3:]
    for k in range(2):
        total = jnp.where(flag[0] == k, own[...].astype(f32), theirs[...].astype(f32))
        value = slow_beta * slow[k] + total / replicas
        slow_new[k] = value
        anchor_new[k] = anchor[k] - learn_rate * value
    token[...] = jnp.zeros_like(token)


def finish(flag, replicas, slow, anchor, own, theirs, position, before):
    size, units = own.shape
    steps = 2
    rows = pl.BlockSpec((2, size // steps, units), lambda j: (0, position * steps + j, 0))
    part = pl.BlockSpec((size // steps, units), lambda j: (j, 0))
    shape = jax.ShapeDtypeStruct(slow.shape, f32)
    return pl.pallas_call(
        functools.partial(finish_kernel, replicas),
        grid=(steps,),
        in_specs=[pl.BlockSpec(memory_space=pltpu.SMEM), rows, rows, part, part] + [ANY] * len(before),
        out_specs=[rows, rows, whole((8, 128))],
        out_shape=[shape, shape, jax.ShapeDtypeStruct((8, 128), bf16)],
        input_output_aliases={5 + k: k for k in range(len(before))},
        compiler_params=pltpu.CompilerParams(vmem_limit_bytes=60 << 20),
        cost_estimate=LIGHT,
    )(flag, slow, anchor, own, theirs, *before)


def slow_step(flag, mine, other, slow, anchor):
    axis, cores = "replica", 2
    index = lax.axis_index(axis)
    replicas = lax.axis_size(axis)
    chip = index // cores
    length = replicas // cores
    half = length // 2
    rows = mine.shape[0]
    size = rows // chunks

    def moved(part, hops):
        return lax.ppermute(part, axis, [(cores * a + c, cores * b + c) for a, b in hops for c in range(cores)])

    def at(places):
        return functools.reduce(jnp.logical_or, [chip == place for place in places])

    stages = [(True, [(s, s + 1), (length - 1 - s, length - 2 - s)]) for s in range(half - 1)]
    if half:
        stages.append((True, [(half - 1, half), (half, half - 1)]))
    stages += [(False, [(s + 1, s), (length - 2 - s, length - 1 - s)]) for s in reversed(range(half - 1))]

    pair_rows = rows // 2
    pairs = [swapped(other[p * pair_rows : (p + 1) * pair_rows], axis, 1) for p in range(2)]
    blocks = []
    for c in range(chunks):
        p, start = divmod(c * size, pair_rows)
        blocks.append(added(mine[c * size : (c + 1) * size], pairs[p][start : start + size]))
    arrived, made, results, tokens = {}, {}, [], []
    final = len(stages) - 1
    for tick in range(chunks + len(stages)):
        for s in reversed(range(len(stages) + 1)):
            c = tick - s
            if not 0 <= c < chunks:
                continue
            block = blocks[c]
            if s:
                adds, hops = stages[s - 1]
                fresh = added(block, arrived[s - 1, c]) if adds else arrived[s - 1, c]
                block = jnp.where(at([b for _, b in hops]), fresh, block)
                if s > final and 0 < c < chunks - 1:
                    block = tied([tokens[c - 1]], block)
            if s == 0 and c >= 3 and (2, c - 3) in made:
                block = tied([made[2, c - 3]], block)
            blocks[c] = made[s, c] = block
            if s < len(stages):
                arrived[s, c] = moved(block, stages[s][1])
            else:
                theirs = swapped(block, axis, 1)
                *results, token = finish(flag, replicas, slow, anchor, block, theirs, c, results)
                tokens.append(token)
    return results


def body(tokens, targets, row_ids, anchor, momentum, slow):
    row_count = tokens.shape[0]
    scale = 1.0 / row_count
    tensors = lax.axis_size("tensor")
    share_rows = row_count // tensors
    order = lax.axis_index("tensor") ^ jnp.arange(tensors)
    picks_all = row_ids[0].reshape(INNER, tensors, share_rows)[:, order].reshape(INNER, row_count)

    replicas = lax.axis_size("replica")
    flag = (lax.axis_index("replica") % 2).astype(jnp.int32).reshape(1)

    def gathered(own):
        return [own] + [swapped(own, "tensor", m) for m in range(1, tensors)]

    def error_share(partials, step):
        wanted = targets.at[picks_all[step, :share_rows]].get(mode="promise_in_bounds")
        share = partials[0].astype(f32)
        for m in range(1, tensors):
            share = share + swapped(partials[m], "tensor", m).astype(f32)
        return ((share - wanted.astype(f32)) * scale).astype(bf16)

    def sent(block, distance, which=(0, 1)):
        route = [((i - distance) % replicas, i) for i in range(replicas) if i % 2 in which]
        return lax.ppermute(block, "replica", route)

    def picked(step, count):
        return tokens.at[picks_all[step, :count]].get(mode="promise_in_bounds")

    near_share = sent(picked(0, share_rows), 1)
    narrow = tied([near_share], momentum[0].astype(bf16))
    moment_near = sent(narrow, 1)

    inputs = [picked(0, row_count)]
    hidden, slope, *partials = forward(flag, inputs, [anchor], only, tensors, emits=False, waits=[narrow])
    error = jnp.concatenate(gathered(error_share(partials, 0)))
    error_near = sent(error, 1)
    moment, moment_bf = backward(
        flag,
        [error],
        anchor,
        slope,
        hidden,
        inputs,
        [momentum[0]],
        first_update,
        [f32, (bf16, 2)],
    )
    inputs_near = gathered(near_share)
    hidden_near, slope_near = forward(flag, inputs_near, [anchor], only, 0, emits=False, waits=[moment])
    moment_far = [sent(tied([error_near, hidden_near], part), 2, (0,)) for part in moment_bf]
    moment_near, weights = backward(
        flag,
        [error_near],
        anchor,
        slope_near,
        hidden_near,
        inputs_near,
        [moment_near, moment, anchor],
        first_beside,
        [(bf16, 2), bf16],
    )

    inputs = [tied([moment_near[0]], picked(1, row_count))]
    inputs_far = sent(inputs[0], 2, (1,))
    hidden, slope, *partials = forward(flag, inputs, [weights], only, tensors, emits=False)
    error = jnp.concatenate(gathered(error_share(partials, 1)))
    error_far = sent(error, 2, (1,))
    moment, weights, known = backward(
        flag,
        [error],
        weights,
        slope,
        hidden,
        inputs,
        [moment, weights],
        second_update,
        [f32, bf16, bf16],
        waits=moment_far,
    )
    weights = tied([error_far, inputs_far], weights)
    weights_sent = sent(weights, 2, (0,))
    moment_two = tuple(sent(tied([weights], part), 1, (1,)) for part in moment_near)
    moment_three = tuple(sent(tied([weights], part), 1, (1,)) for part in moment_far)
    hidden, slope, weights_far = forward(flag, [inputs_far], [anchor, moment_two, moment_three], pushed, 0)
    (weights_found,) = backward(
        flag, [error_far], weights_far, slope, hidden, [inputs_far], [moment_two, weights_far], second_beside, [bf16]
    )

    inputs = [picked(2, row_count)]
    hidden, slope, *rest = forward(flag, inputs, [weights_found, weights, weights_sent], halved, tensors)
    errors = gathered(error_share(rest[:tensors], 2))
    moment, total = backward(
        flag, errors, rest[tensors], slope, hidden, inputs, [moment, known], third_update, [f32, (bf16, "core")]
    )
    anchor_new, slow_new = slow_step(flag, *total, slow, anchor)
    return (anchor_new, slow_new, moment[None])


def solution(mesh):
    return jax.shard_map(
        body,
        mesh=mesh,
        in_specs=(
            P("replica", None),
            P("replica", None),
            P("replica", None, None),
            P(None, None, "tensor"),
            P("replica", None, None, "tensor"),
            P(None, None, "tensor"),
        ),
        out_specs=(
            P(None, None, "tensor"),
            P(None, None, "tensor"),
            P("replica", None, None, "tensor"),
        ),
        check_vma=False,
    )
```

```python
import functools

import jax
import jax.numpy as jnp
from jax import lax
from jax.experimental import pallas as pl
from jax.experimental.pallas import tpu as pltpu
from jax.sharding import PartitionSpec as P

INNER = 3


learn_rate = 0.02
inner_beta = 0.9
slow_beta = 0.5
chunks = 4
bf16, f32 = jnp.bfloat16, jnp.float32
ANY = pl.BlockSpec(memory_space=pl.ANY)
LIGHT = pl.CostEstimate(flops=1, bytes_accessed=1, transcendentals=0)


def swapped(block, axis, mask):
    return lax.ppermute(block, axis, [(i, i ^ mask) for i in range(lax.axis_size(axis))])


def gelu_pair(pre):
    coeff = 0.7978845608028654
    square = pre * pre
    tanh_val = jnp.tanh(coeff * (pre + 0.044715 * square * pre))
    half = 0.5 * (1.0 + tanh_val)
    slope = half + 0.5 * pre * (1.0 - tanh_val * tanh_val) * coeff * (1.0 + 3.0 * 0.044715 * square)
    return (pre * half, slope)


def whole(shape):
    return pl.BlockSpec(shape, lambda j: (0,) * len(shape))


def loaded(state, k):
    if type(state) is not tuple:
        return state[k].astype(f32)
    each = len(state) // 2
    return jnp.concatenate([piece[...].astype(f32) for piece in state[k * each : (k + 1) * each]], axis=0)


def regrouped(refs, counts):
    refs, states = list(refs), []
    for count in counts:
        states.append(tuple(refs[:count]) if count > 1 else refs[0])
        del refs[:count]
    return states, refs


def flattened(states):
    flat = [state if type(state) is tuple else (state,) for state in states]
    return [len(state) for state in flat], [part for state in flat for part in state]


def block_of(part, block, parts=2):
    if part.ndim == 2:
        return pl.BlockSpec((part.shape[0], block), lambda j: (0, j))
    return pl.BlockSpec((parts, part.shape[1], block), lambda j: (0, 0, j))


def joined(pieces, place):
    if len(pieces) == 1:
        return pieces[0]

    @pl.when(pl.program_id(0) == 0)
    def _():
        size = pieces[0].shape[0]
        for b, piece in enumerate(pieces):
            place[b * size : (b + 1) * size] = piece[...]

    return place


def forward_kernel(mix, taken, pieces, waits, sums, emits, flag, *refs):
    rows, refs = refs[:pieces], refs[pieces:]
    sources, refs = regrouped(refs, taken)
    refs = refs[waits:]
    hidden, slope = refs[:2]
    inputs = joined(rows, refs[-1])
    block = [mix(flag[0], *[loaded(source, k) for source in sources]).astype(bf16) for k in range(2 if sums or emits else 1)]
    if emits:
        for k in range(2):
            refs[2 + sums][k] = block[k]
    j = pl.program_id(0)
    value, slope_val = gelu_pair(jnp.dot(inputs[...], block[0], preferred_element_type=f32))
    value = value.astype(bf16)
    hidden[...] = value
    slope[...] = slope_val.astype(bf16)
    if sums:
        partials, total = refs[2 : 2 + sums], refs[-2]
        out = lax.dot_general(value, block[1], (((1,), (1,)), ((), ())), preferred_element_type=f32)

        @pl.when(j == 0)
        def _():
            total[...] = out

        @pl.when(j > 0)
        def _():
            total[...] += out

        @pl.when(j == pl.num_programs(0) - 1)
        def _():
            size = partials[0].shape[0]
            for b, partial in enumerate(partials):
                partial[...] = total[b * size : (b + 1) * size].astype(bf16)


def forward(flag, inputs, sources, mix, sums, emits=True, waits=()):
    count, width = inputs[0].shape
    rows = count * len(inputs)
    units = sources[0].shape[2]
    block = min(units, 512)
    parts = 2 if sums or emits else 1
    counts, flat = flattened(sources)
    unit_spec = pl.BlockSpec((rows, block), lambda j: (0, j))
    shapes = [((rows, units), unit_spec), ((rows, units), unit_spec)]
    if sums:
        shapes += [((rows // sums, width), whole((rows // sums, width)))] * sums
    shapes += [(sources[0].shape, block_of(sources[0], block))] * emits
    return pl.pallas_call(
        functools.partial(forward_kernel, mix, counts, len(inputs), len(waits), sums, emits),
        grid=(units // block,),
        in_specs=[pl.BlockSpec(memory_space=pltpu.SMEM)]
        + [whole(piece.shape) for piece in inputs]
        + [block_of(part, block, parts) for part in flat]
        + [ANY] * len(waits),
        out_specs=[spec for _, spec in shapes],
        out_shape=[jax.ShapeDtypeStruct(shape, bf16) for shape, _ in shapes],
        scratch_shapes=[pltpu.VMEM((rows, width), f32)] * bool(sums) + [pltpu.VMEM((rows, width), bf16)],
        compiler_params=pltpu.CompilerParams(vmem_limit_bytes=56 << 20),
        cost_estimate=LIGHT,
    )(flag, *inputs, *flat, *waits)


def only(flag, weights):
    return weights


def pushed(flag, weights, first, second):
    return weights - 0.5 * learn_rate * (first + second)


def halved(flag, found, weights, sent):
    return 0.5 * (weights + jnp.where(flag == 0, sent, found))


def backward_kernel(update, taken, pieces, given, by_core, flag, weights, slope, hidden, *refs):
    states, refs = regrouped(refs, taken)
    error_count, input_count = pieces
    errors, inputs = refs[:error_count], refs[error_count : error_count + input_count]
    error, error_t, rows, inputs_t = refs[-4:]
    refs = refs[error_count + input_count : -4]
    results, _ = regrouped(refs[len(refs) - sum(given) :], given)
    error, rows = joined(errors, error), joined(inputs, rows)

    @pl.when(pl.program_id(0) == 0)
    def _():
        error_t[...] = error[...].T
        inputs_t[...] = rows[...].T

    back = jnp.dot(error[...], weights[0].astype(bf16), preferred_element_type=f32) * slope[...].astype(f32)
    for k, (left, right) in enumerate(((inputs_t[...], back.astype(bf16)), (error_t[...], hidden[...]))):
        grad = jnp.dot(left, right, preferred_element_type=f32)
        values = update(grad, *[loaded(state, k) for state in states])
        for result, apart, value in zip(results, by_core, values):
            if type(result) is not tuple:
                result[k] = value.astype(result.dtype)
                continue
            if apart:
                mine, *others = result

                @pl.when(flag[0] == k)
                def _():
                    mine[...] = value.astype(mine.dtype)

                @pl.when(flag[0] != k)
                def _():
                    size = others[0].shape[0]
                    for i, piece in enumerate(others):
                        piece[...] = value[i * size : (i + 1) * size].astype(piece.dtype)

                continue
            each = len(result) // 2
            for i, piece in enumerate(result[k * each : (k + 1) * each]):
                size = piece.shape[0]
                piece[...] = value[i * size : (i + 1) * size].astype(piece.dtype)


def backward(flag, errors, weights, slope, hidden, inputs, states, update, kinds, waits=()):
    rows, width = hidden.shape[0], weights.shape[1]
    units = weights.shape[2]
    block = min(units, 512)
    counts, flat = flattened(states)
    kinds = [kind if type(kind) is tuple else (kind, 1) for kind in kinds]
    by_core = [count == "core" for _, count in kinds]
    kinds = [(kind, 3 if apart else count) for (kind, count), apart in zip(kinds, by_core)]
    shapes = []
    for (kind, count), apart in zip(kinds, by_core):
        if apart:
            parts = [(width, units), (width // 2, units), (width // 2, units)]
        else:
            parts = [weights.shape if count == 1 else (2 * width // count, units)] * count
        shapes += [jax.ShapeDtypeStruct(part, kind) for part in parts]
    results = pl.pallas_call(
        functools.partial(
            backward_kernel, update, counts, (len(errors), len(inputs)), [count for _, count in kinds], by_core
        ),
        grid=(units // block,),
        in_specs=[
            pl.BlockSpec(memory_space=pltpu.SMEM),
            pl.BlockSpec((1, width, block), lambda j: (1, 0, j)),
            pl.BlockSpec((rows, block), lambda j: (0, j)),
            pl.BlockSpec((rows, block), lambda j: (0, j)),
        ]
        + [block_of(part, block) for part in flat]
        + [whole(piece.shape) for piece in (*errors, *inputs)]
        + [ANY] * len(waits),
        out_specs=[block_of(shape, block) for shape in shapes],
        out_shape=shapes,
        scratch_shapes=[pltpu.VMEM((rows, width), bf16), pltpu.VMEM((width, rows), bf16)] * 2,
        compiler_params=pltpu.CompilerParams(vmem_limit_bytes=56 << 20),
        cost_estimate=LIGHT,
    )(flag, weights, slope, hidden, *flat, *errors, *inputs, *waits)
    return regrouped(results, [count for _, count in kinds])[0]


def first_update(grad, moment):
    moment = inner_beta * moment + grad
    return (moment, moment)


def first_beside(grad, moment, own_moment, weights):
    moment = inner_beta * moment + grad
    return (moment, weights - 0.5 * learn_rate * (own_moment + moment))


def second_update(grad, moment, weights):
    moment_new = inner_beta * moment + grad
    return (moment_new, weights - learn_rate * moment_new, moment + (1.0 + inner_beta) * moment_new)


def second_beside(grad, moment, weights):
    return (weights - learn_rate * (inner_beta * moment + grad),)


def third_update(grad, moment, known):
    return (inner_beta * moment + grad, known + grad)


def rounded(value):
    return lax.reduce_precision(value, 8, 7).astype(bf16)


def added(left, right):
    return rounded(left.astype(f32) + right.astype(f32))


def nothing(*refs):
    pass


def tied(waits, block):
    return pl.pallas_call(
        nothing,
        in_specs=[ANY] * (1 + len(waits)),
        out_specs=ANY,
        out_shape=jax.ShapeDtypeStruct(block.shape, block.dtype),
        input_output_aliases={0: 0},
        cost_estimate=LIGHT,
    )(block, *waits)


def finish_kernel(replicas, flag, slow, anchor, own, theirs, *refs):
    anchor_new, slow_new, token = refs[-3:]
    for k in range(2):
        total = jnp.where(flag[0] == k, own[...].astype(f32), theirs[...].astype(f32))
        value = slow_beta * slow[k] + total / replicas
        slow_new[k] = value
        anchor_new[k] = anchor[k] - learn_rate * value
    token[...] = jnp.zeros_like(token)


def finish(flag, replicas, slow, anchor, own, theirs, position, before):
    size, units = own.shape
    steps = 2
    rows = pl.BlockSpec((2, size // steps, units), lambda j: (0, position * steps + j, 0))
    part = pl.BlockSpec((size // steps, units), lambda j: (j, 0))
    shape = jax.ShapeDtypeStruct(slow.shape, f32)
    return pl.pallas_call(
        functools.partial(finish_kernel, replicas),
        grid=(steps,),
        in_specs=[pl.BlockSpec(memory_space=pltpu.SMEM), rows, rows, part, part] + [ANY] * len(before),
        out_specs=[rows, rows, whole((8, 128))],
        out_shape=[shape, shape, jax.ShapeDtypeStruct((8, 128), bf16)],
        input_output_aliases={5 + k: k for k in range(len(before))},
        compiler_params=pltpu.CompilerParams(vmem_limit_bytes=60 << 20),
        cost_estimate=LIGHT,
    )(flag, slow, anchor, own, theirs, *before)


def slow_step(flag, mine, others, slow, anchor):
    axis, cores = "replica", 2
    index = lax.axis_index(axis)
    replicas = lax.axis_size(axis)
    chip = index // cores
    length = replicas // cores
    half = length // 2
    rows = mine.shape[0]
    size = rows // chunks

    def moved(part, hops):
        return lax.ppermute(part, axis, [(cores * a + c, cores * b + c) for a, b in hops for c in range(cores)])

    def at(places):
        return functools.reduce(jnp.logical_or, [chip == place for place in places])

    stages = [(True, [(s, s + 1), (length - 1 - s, length - 2 - s)]) for s in range(half - 1)]
    if half:
        stages.append((True, [(half - 1, half), (half, half - 1)]))
    stages += [(False, [(s + 1, s), (length - 2 - s, length - 1 - s)]) for s in reversed(range(half - 1))]

    pair_rows = rows // 2
    pairs = [swapped(part, axis, 1) for part in others]
    blocks = []
    for c in range(chunks):
        p, start = divmod(c * size, pair_rows)
        blocks.append(added(mine[c * size : (c + 1) * size], pairs[p][start : start + size]))
    arrived, results, tokens = {}, [], []
    for tick in range(chunks + len(stages)):
        for s in reversed(range(len(stages) + 1)):
            c = tick - s
            if not 0 <= c < chunks:
                continue
            block = blocks[c]
            if s:
                adds, hops = stages[s - 1]
                fresh = added(block, arrived[s - 1, c]) if adds else arrived[s - 1, c]
                block = jnp.where(at([b for _, b in hops]), fresh, block)
                if s == len(stages) and c:
                    block = tied([tokens[c - 1]], block)
                if s == 1 and c:
                    block = tied([blocks[c - 1]], block)
            blocks[c] = block
            if s < len(stages):
                arrived[s, c] = moved(block, stages[s][1])
            else:
                theirs = swapped(block, axis, 1)
                *results, token = finish(flag, replicas, slow, anchor, block, theirs, c, results)
                tokens.append(token)
    return results


def body(tokens, targets, row_ids, anchor, momentum, slow):
    row_count = tokens.shape[0]
    scale = 1.0 / row_count
    tensors = lax.axis_size("tensor")
    share_rows = row_count // tensors
    order = lax.axis_index("tensor") ^ jnp.arange(tensors)
    picks_all = row_ids[0].reshape(INNER, tensors, share_rows)[:, order].reshape(INNER, row_count)

    replicas = lax.axis_size("replica")
    flag = (lax.axis_index("replica") % 2).astype(jnp.int32).reshape(1)

    def gathered(own):
        return [own] + [swapped(own, "tensor", m) for m in range(1, tensors)]

    def error_share(partials, step):
        wanted = targets.at[picks_all[step, :share_rows]].get(mode="promise_in_bounds")
        share = partials[0].astype(f32)
        for m in range(1, tensors):
            share = share + swapped(partials[m], "tensor", m).astype(f32)
        return ((share - wanted.astype(f32)) * scale).astype(bf16)

    def sent(block, distance, which=(0, 1)):
        route = [((i - distance) % replicas, i) for i in range(replicas) if i % 2 in which]
        return lax.ppermute(block, "replica", route)

    def picked(step, count):
        return tokens.at[picks_all[step, :count]].get(mode="promise_in_bounds")

    shares = jnp.concatenate([picks_all[step, :share_rows] for step in range(2)])
    shares = sent(tokens.at[shares].get(mode="promise_in_bounds"), 1)
    near_share, far_share = shares[:share_rows], shares[share_rows:]
    narrow = tied([shares], momentum[0].astype(bf16))
    moment_near = sent(narrow, 1)

    inputs = [picked(0, row_count)]
    hidden, slope, *partials = forward(flag, inputs, [anchor], only, tensors, emits=False, waits=[narrow])
    error = jnp.concatenate(gathered(error_share(partials, 0)))
    error_near = sent(error, 1)
    moment, moment_bf = backward(
        flag,
        [error],
        anchor,
        slope,
        hidden,
        inputs,
        [momentum[0]],
        first_update,
        [f32, bf16],
    )
    inputs_near = gathered(near_share)
    hidden_near, slope_near = forward(flag, inputs_near, [anchor], only, 0, emits=False, waits=[moment])
    moment_far = sent(tied([error_near, hidden_near], moment_bf), 2, (0,))
    moment_near, weights = backward(
        flag,
        [error_near],
        anchor,
        slope_near,
        hidden_near,
        inputs_near,
        [moment_near, moment, anchor],
        first_beside,
        [(bf16, 2), bf16],
    )

    inputs = [picked(1, row_count)]
    hidden, slope, *partials = forward(flag, inputs, [weights], only, tensors, emits=False)
    error = jnp.concatenate(gathered(error_share(partials, 1)))
    error_far = sent(error, 2, (1,))
    moment, weights, known = backward(
        flag,
        [error],
        weights,
        slope,
        hidden,
        inputs,
        [moment, weights],
        second_update,
        [f32, bf16, bf16],
        waits=[moment_far],
    )
    weights = tied([error_far], weights)
    weights_sent = sent(weights, 2, (0,))
    inputs_far = gathered(sent(tied([weights], far_share), 1, (1,)))
    moment_two = tuple(sent(tied([weights], part), 1, (1,)) for part in moment_near)
    moment_three = tuple(sent(tied([weights], moment_far[k]), 1, (1,)) for k in range(2))
    hidden, slope, weights_far = forward(flag, inputs_far, [anchor, moment_two, moment_three], pushed, 0)
    (weights_found,) = backward(
        flag, [error_far], weights_far, slope, hidden, inputs_far, [moment_two, weights_far], second_beside, [bf16]
    )

    inputs = [picked(2, row_count)]
    hidden, slope, *rest = forward(flag, inputs, [weights_found, weights, weights_sent], halved, tensors)
    errors = gathered(error_share(rest[:tensors], 2))
    moment, total = backward(
        flag, errors, rest[tensors], slope, hidden, inputs, [moment, known], third_update, [f32, (bf16, "core")]
    )
    anchor_new, slow_new = slow_step(flag, total[0], total[1:], slow, anchor)
    return (anchor_new, slow_new, moment[None])


def solution(mesh):
    return jax.shard_map(
        body,
        mesh=mesh,
        in_specs=(
            P("replica", None),
            P("replica", None),
            P("replica", None, None),
            P(None, None, "tensor"),
            P("replica", None, None, "tensor"),
            P(None, None, "tensor"),
        ),
        out_specs=(
            P(None, None, "tensor"),
            P(None, None, "tensor"),
            P("replica", None, None, "tensor"),
        ),
        check_vma=False,
    )
```

```python
import functools

import jax
import jax.numpy as jnp
from jax import lax
from jax.experimental import pallas as pl
from jax.experimental.pallas import tpu as pltpu
from jax.sharding import PartitionSpec as P

INNER = 3


learn_rate = 0.02
inner_beta = 0.9
slow_beta = 0.5
chunks = 4
bf16, f32 = jnp.bfloat16, jnp.float32
ANY = pl.BlockSpec(memory_space=pl.ANY)
LIGHT = pl.CostEstimate(flops=1, bytes_accessed=1, transcendentals=0)


def swapped(block, axis, mask):
    return lax.ppermute(block, axis, [(i, i ^ mask) for i in range(lax.axis_size(axis))])


def gelu_pair(pre):
    coeff = 0.7978845608028654
    square = pre * pre
    tanh_val = jnp.tanh(coeff * (pre + 0.044715 * square * pre))
    half = 0.5 * (1.0 + tanh_val)
    slope = half + 0.5 * pre * (1.0 - tanh_val * tanh_val) * coeff * (1.0 + 3.0 * 0.044715 * square)
    return (pre * half, slope)


def whole(shape):
    return pl.BlockSpec(shape, lambda j: (0,) * len(shape))


def loaded(state, k):
    if type(state) is not tuple:
        return state[k].astype(f32)
    each = len(state) // 2
    return jnp.concatenate([piece[...].astype(f32) for piece in state[k * each : (k + 1) * each]], axis=0)


def regrouped(refs, counts):
    refs, states = list(refs), []
    for count in counts:
        states.append(tuple(refs[:count]) if count > 1 else refs[0])
        del refs[:count]
    return states, refs


def flattened(states):
    flat = [state if type(state) is tuple else (state,) for state in states]
    return [len(state) for state in flat], [part for state in flat for part in state]


def block_of(part, block, parts=2):
    if part.ndim == 2:
        return pl.BlockSpec((part.shape[0], block), lambda j: (0, j))
    return pl.BlockSpec((parts, part.shape[1], block), lambda j: (0, 0, j))


def joined(pieces, place):
    if len(pieces) == 1:
        return pieces[0]

    @pl.when(pl.program_id(0) == 0)
    def _():
        size = pieces[0].shape[0]
        for b, piece in enumerate(pieces):
            place[b * size : (b + 1) * size] = piece[...]

    return place


def forward_kernel(mix, taken, pieces, waits, sums, emits, flag, *refs):
    rows, refs = refs[:pieces], refs[pieces:]
    sources, refs = regrouped(refs, taken)
    refs = refs[waits:]
    hidden, slope = refs[:2]
    inputs = joined(rows, refs[-1])
    block = [mix(flag[0], *[loaded(source, k) for source in sources]).astype(bf16) for k in range(2 if sums or emits else 1)]
    if emits:
        for k in range(2):
            refs[2 + sums][k] = block[k]
    j = pl.program_id(0)
    value, slope_val = gelu_pair(jnp.dot(inputs[...], block[0], preferred_element_type=f32))
    value = value.astype(bf16)
    hidden[...] = value
    slope[...] = slope_val.astype(bf16)
    if sums:
        partials, total = refs[2 : 2 + sums], refs[-2]
        out = lax.dot_general(value, block[1], (((1,), (1,)), ((), ())), preferred_element_type=f32)

        @pl.when(j == 0)
        def _():
            total[...] = out

        @pl.when(j > 0)
        def _():
            total[...] += out

        @pl.when(j == pl.num_programs(0) - 1)
        def _():
            size = partials[0].shape[0]
            for b, partial in enumerate(partials):
                partial[...] = total[b * size : (b + 1) * size].astype(bf16)


def forward(flag, inputs, sources, mix, sums, emits=True, waits=()):
    count, width = inputs[0].shape
    rows = count * len(inputs)
    units = sources[0].shape[2]
    block = min(units, 512)
    parts = 2 if sums or emits else 1
    counts, flat = flattened(sources)
    unit_spec = pl.BlockSpec((rows, block), lambda j: (0, j))
    shapes = [((rows, units), unit_spec), ((rows, units), unit_spec)]
    if sums:
        shapes += [((rows // sums, width), whole((rows // sums, width)))] * sums
    shapes += [(sources[0].shape, block_of(sources[0], block))] * emits
    return pl.pallas_call(
        functools.partial(forward_kernel, mix, counts, len(inputs), len(waits), sums, emits),
        grid=(units // block,),
        in_specs=[pl.BlockSpec(memory_space=pltpu.SMEM)]
        + [whole(piece.shape) for piece in inputs]
        + [block_of(part, block, parts) for part in flat]
        + [ANY] * len(waits),
        out_specs=[spec for _, spec in shapes],
        out_shape=[jax.ShapeDtypeStruct(shape, bf16) for shape, _ in shapes],
        scratch_shapes=[pltpu.VMEM((rows, width), f32)] * bool(sums) + [pltpu.VMEM((rows, width), bf16)],
        compiler_params=pltpu.CompilerParams(vmem_limit_bytes=56 << 20),
        cost_estimate=LIGHT,
    )(flag, *inputs, *flat, *waits)


def only(flag, weights):
    return weights


def pushed(flag, weights, first, second):
    return weights - 0.5 * learn_rate * (first + second)


def halved(flag, found, weights, sent):
    return 0.5 * (weights + jnp.where(flag == 0, sent, found))


def backward_kernel(update, taken, pieces, given, by_core, flag, weights, slope, hidden, *refs):
    states, refs = regrouped(refs, taken)
    error_count, input_count = pieces
    errors, inputs = refs[:error_count], refs[error_count : error_count + input_count]
    error, error_t, rows, inputs_t = refs[-4:]
    refs = refs[error_count + input_count : -4]
    results, _ = regrouped(refs[len(refs) - sum(given) :], given)
    error, rows = joined(errors, error), joined(inputs, rows)

    @pl.when(pl.program_id(0) == 0)
    def _():
        error_t[...] = error[...].T
        inputs_t[...] = rows[...].T

    back = jnp.dot(error[...], weights[0].astype(bf16), preferred_element_type=f32) * slope[...].astype(f32)
    for k, (left, right) in enumerate(((inputs_t[...], back.astype(bf16)), (error_t[...], hidden[...]))):
        grad = jnp.dot(left, right, preferred_element_type=f32)
        values = update(grad, *[loaded(state, k) for state in states])
        for result, apart, value in zip(results, by_core, values):
            if type(result) is not tuple:
                result[k] = value.astype(result.dtype)
                continue
            if apart:
                mine, *others = result

                @pl.when(flag[0] == k)
                def _():
                    mine[...] = value.astype(mine.dtype)

                @pl.when(flag[0] != k)
                def _():
                    size = others[0].shape[0]
                    for i, piece in enumerate(others):
                        piece[...] = value[i * size : (i + 1) * size].astype(piece.dtype)

                continue
            each = len(result) // 2
            for i, piece in enumerate(result[k * each : (k + 1) * each]):
                size = piece.shape[0]
                piece[...] = value[i * size : (i + 1) * size].astype(piece.dtype)


def backward(flag, errors, weights, slope, hidden, inputs, states, update, kinds, waits=()):
    rows, width = hidden.shape[0], weights.shape[1]
    units = weights.shape[2]
    block = min(units, 512)
    counts, flat = flattened(states)
    kinds = [kind if type(kind) is tuple else (kind, 1) for kind in kinds]
    by_core = [count == "core" for _, count in kinds]
    kinds = [(kind, 3 if apart else count) for (kind, count), apart in zip(kinds, by_core)]
    shapes = []
    for (kind, count), apart in zip(kinds, by_core):
        if apart:
            parts = [(width, units), (width // 2, units), (width // 2, units)]
        else:
            parts = [weights.shape if count == 1 else (2 * width // count, units)] * count
        shapes += [jax.ShapeDtypeStruct(part, kind) for part in parts]
    results = pl.pallas_call(
        functools.partial(
            backward_kernel, update, counts, (len(errors), len(inputs)), [count for _, count in kinds], by_core
        ),
        grid=(units // block,),
        in_specs=[
            pl.BlockSpec(memory_space=pltpu.SMEM),
            pl.BlockSpec((1, width, block), lambda j: (1, 0, j)),
            pl.BlockSpec((rows, block), lambda j: (0, j)),
            pl.BlockSpec((rows, block), lambda j: (0, j)),
        ]
        + [block_of(part, block) for part in flat]
        + [whole(piece.shape) for piece in (*errors, *inputs)]
        + [ANY] * len(waits),
        out_specs=[block_of(shape, block) for shape in shapes],
        out_shape=shapes,
        scratch_shapes=[pltpu.VMEM((rows, width), bf16), pltpu.VMEM((width, rows), bf16)] * 2,
        compiler_params=pltpu.CompilerParams(vmem_limit_bytes=56 << 20),
        cost_estimate=LIGHT,
    )(flag, weights, slope, hidden, *flat, *errors, *inputs, *waits)
    return regrouped(results, [count for _, count in kinds])[0]


def first_update(grad, moment):
    moment = inner_beta * moment + grad
    return (moment, moment)


def first_beside(grad, moment, own_moment, weights):
    moment = inner_beta * moment + grad
    return (moment, weights - 0.5 * learn_rate * (own_moment + moment))


def second_update(grad, moment, weights):
    moment_new = inner_beta * moment + grad
    return (moment_new, weights - learn_rate * moment_new, moment + (1.0 + inner_beta) * moment_new)


def second_beside(grad, moment, weights):
    return (weights - learn_rate * (inner_beta * moment + grad),)


def third_update(grad, moment, known):
    return (inner_beta * moment + grad, known + grad)


def rounded(value):
    return lax.reduce_precision(value, 8, 7).astype(bf16)


def added(left, right):
    return rounded(left.astype(f32) + right.astype(f32))


def nothing(*refs):
    pass


def tied(waits, block):
    return pl.pallas_call(
        nothing,
        in_specs=[ANY] * (1 + len(waits)),
        out_specs=ANY,
        out_shape=jax.ShapeDtypeStruct(block.shape, block.dtype),
        input_output_aliases={0: 0},
        cost_estimate=LIGHT,
    )(block, *waits)


def finish_kernel(replicas, flag, slow, anchor, own, theirs, *refs):
    anchor_new, slow_new, token = refs[-3:]
    for k in range(2):
        total = jnp.where(flag[0] == k, own[...].astype(f32), theirs[...].astype(f32))
        value = slow_beta * slow[k] + total / replicas
        slow_new[k] = value
        anchor_new[k] = anchor[k] - learn_rate * value
    token[...] = jnp.zeros_like(token)


def finish(flag, replicas, slow, anchor, own, theirs, position, before):
    size, units = own.shape
    steps = 2
    rows = pl.BlockSpec((2, size // steps, units), lambda j: (0, position * steps + j, 0))
    part = pl.BlockSpec((size // steps, units), lambda j: (j, 0))
    shape = jax.ShapeDtypeStruct(slow.shape, f32)
    return pl.pallas_call(
        functools.partial(finish_kernel, replicas),
        grid=(steps,),
        in_specs=[pl.BlockSpec(memory_space=pltpu.SMEM), rows, rows, part, part] + [ANY] * len(before),
        out_specs=[rows, rows, whole((8, 128))],
        out_shape=[shape, shape, jax.ShapeDtypeStruct((8, 128), bf16)],
        input_output_aliases={5 + k: k for k in range(len(before))},
        compiler_params=pltpu.CompilerParams(vmem_limit_bytes=60 << 20),
        cost_estimate=LIGHT,
    )(flag, slow, anchor, own, theirs, *before)


def slow_step(flag, mine, others, slow, anchor):
    axis, cores = "replica", 2
    index = lax.axis_index(axis)
    replicas = lax.axis_size(axis)
    chip = index // cores
    length = replicas // cores
    half = length // 2
    rows = mine.shape[0]
    size = rows // chunks

    def moved(part, hops):
        return lax.ppermute(part, axis, [(cores * a + c, cores * b + c) for a, b in hops for c in range(cores)])

    def at(places):
        return functools.reduce(jnp.logical_or, [chip == place for place in places])

    stages = [(True, [(s, s + 1), (length - 1 - s, length - 2 - s)]) for s in range(half - 1)]
    if half:
        stages.append((True, [(half - 1, half), (half, half - 1)]))
    stages += [(False, [(s + 1, s), (length - 2 - s, length - 1 - s)]) for s in reversed(range(half - 1))]

    pair_rows = rows // 2
    pairs = [swapped(part, axis, 1) for part in others]
    blocks = []
    for c in range(chunks):
        p, start = divmod(c * size, pair_rows)
        blocks.append(added(mine[c * size : (c + 1) * size], pairs[p][start : start + size]))
    arrived, made, results, tokens = {}, {}, [], []
    final = len(stages) - 1
    for tick in range(chunks + len(stages)):
        for s in reversed(range(len(stages) + 1)):
            c = tick - s
            if not 0 <= c < chunks:
                continue
            block = blocks[c]
            if s:
                adds, hops = stages[s - 1]
                fresh = added(block, arrived[s - 1, c]) if adds else arrived[s - 1, c]
                block = jnp.where(at([b for _, b in hops]), fresh, block)
                if s > final and c:
                    block = tied([tokens[c - 1]], block)
            if s == 0 and c >= 3 and (2, c - 3) in made:
                block = tied([made[2, c - 3]], block)
            blocks[c] = made[s, c] = block
            if s < len(stages):
                arrived[s, c] = moved(block, stages[s][1])
            else:
                theirs = swapped(block, axis, 1)
                *results, token = finish(flag, replicas, slow, anchor, block, theirs, c, results)
                tokens.append(token)
    return results


def body(tokens, targets, row_ids, anchor, momentum, slow):
    row_count = tokens.shape[0]
    scale = 1.0 / row_count
    tensors = lax.axis_size("tensor")
    share_rows = row_count // tensors
    order = lax.axis_index("tensor") ^ jnp.arange(tensors)
    picks_all = row_ids[0].reshape(INNER, tensors, share_rows)[:, order].reshape(INNER, row_count)

    replicas = lax.axis_size("replica")
    flag = (lax.axis_index("replica") % 2).astype(jnp.int32).reshape(1)

    def gathered(own):
        return [own] + [swapped(own, "tensor", m) for m in range(1, tensors)]

    def error_share(partials, step):
        wanted = targets.at[picks_all[step, :share_rows]].get(mode="promise_in_bounds")
        share = partials[0].astype(f32)
        for m in range(1, tensors):
            share = share + swapped(partials[m], "tensor", m).astype(f32)
        return ((share - wanted.astype(f32)) * scale).astype(bf16)

    def sent(block, distance, which=(0, 1)):
        route = [((i - distance) % replicas, i) for i in range(replicas) if i % 2 in which]
        return lax.ppermute(block, "replica", route)

    def picked(step, count):
        return tokens.at[picks_all[step, :count]].get(mode="promise_in_bounds")

    near_share = sent(picked(0, share_rows), 1)
    narrow = tied([near_share], momentum[0].astype(bf16))
    moment_near = sent(narrow, 1)

    inputs = [picked(0, row_count)]
    hidden, slope, *partials = forward(flag, inputs, [anchor], only, tensors, emits=False, waits=[narrow])
    error = jnp.concatenate(gathered(error_share(partials, 0)))
    error_near = sent(error, 1)
    inputs_next = picked(1, row_count)
    moment, moment_bf = backward(
        flag,
        [error],
        anchor,
        slope,
        hidden,
        inputs,
        [momentum[0]],
        first_update,
        [f32, bf16],
        waits=[inputs_next],
    )
    inputs_near = gathered(near_share)
    hidden_near, slope_near = forward(flag, inputs_near, [anchor], only, 0, emits=False, waits=[moment])
    moment_far = sent(tied([error_near, hidden_near], moment_bf), 2, (0,))
    moment_near, weights = backward(
        flag,
        [error_near],
        anchor,
        slope_near,
        hidden_near,
        inputs_near,
        [moment_near, moment, anchor],
        first_beside,
        [(bf16, 2), bf16],
    )

    inputs = [tied([moment_near[0]], inputs_next)]
    inputs_far = sent(inputs[0], 2, (1,))
    hidden, slope, *partials = forward(flag, inputs, [weights], only, tensors, emits=False)
    error = jnp.concatenate(gathered(error_share(partials, 1)))
    error_far = sent(error, 2, (1,))
    moment, weights, known = backward(
        flag,
        [error],
        weights,
        slope,
        hidden,
        inputs,
        [moment, weights],
        second_update,
        [f32, bf16, bf16],
        waits=[moment_far],
    )
    weights = tied([error_far[:16], inputs_far[:16]], weights)
    weights_sent = sent(weights, 2, (0,))
    moment_two = tuple(sent(tied([weights], part), 1, (1,)) for part in moment_near)
    moment_three = tuple(sent(tied([weights], moment_far[k]), 1, (1,)) for k in range(2))
    hidden, slope, weights_far = forward(flag, [inputs_far], [anchor, moment_two, moment_three], pushed, 0)
    (weights_found,) = backward(
        flag, [error_far], weights_far, slope, hidden, [inputs_far], [moment_two, weights_far], second_beside, [bf16]
    )

    inputs = [picked(2, row_count)]
    hidden, slope, *rest = forward(flag, inputs, [weights_found, weights, weights_sent], halved, tensors)
    errors = gathered(error_share(rest[:tensors], 2))
    moment, total = backward(
        flag, errors, rest[tensors], slope, hidden, inputs, [moment, known], third_update, [f32, (bf16, "core")]
    )
    anchor_new, slow_new = slow_step(flag, total[0], total[1:], slow, anchor)
    return (anchor_new, slow_new, moment[None])


def solution(mesh):
    return jax.shard_map(
        body,
        mesh=mesh,
        in_specs=(
            P("replica", None),
            P("replica", None),
            P("replica", None, None),
            P(None, None, "tensor"),
            P("replica", None, None, "tensor"),
            P(None, None, "tensor"),
        ),
        out_specs=(
            P(None, None, "tensor"),
            P(None, None, "tensor"),
            P("replica", None, None, "tensor"),
        ),
        check_vma=False,
    )
```

```python
import functools

import jax
import jax.numpy as jnp
from jax import lax
from jax.experimental import pallas as pl
from jax.experimental.pallas import tpu as pltpu
from jax.sharding import PartitionSpec as P

INNER = 3


learn_rate = 0.02
inner_beta = 0.9
slow_beta = 0.5
chunks = 4
bf16, f32 = jnp.bfloat16, jnp.float32
ANY = pl.BlockSpec(memory_space=pl.ANY)
LIGHT = pl.CostEstimate(flops=1, bytes_accessed=1, transcendentals=0)


def swapped(block, axis, mask):
    return lax.ppermute(block, axis, [(i, i ^ mask) for i in range(lax.axis_size(axis))])


def gelu_pair(pre):
    coeff = 0.7978845608028654
    square = pre * pre
    tanh_val = jnp.tanh(coeff * (pre + 0.044715 * square * pre))
    half = 0.5 * (1.0 + tanh_val)
    slope = half + 0.5 * pre * (1.0 - tanh_val * tanh_val) * coeff * (1.0 + 3.0 * 0.044715 * square)
    return (pre * half, slope)


def whole(shape):
    return pl.BlockSpec(shape, lambda j: (0,) * len(shape))


def loaded(state, k):
    if type(state) is not tuple:
        return state[k].astype(f32)
    each = len(state) // 2
    return jnp.concatenate([piece[...].astype(f32) for piece in state[k * each : (k + 1) * each]], axis=0)


def regrouped(refs, counts):
    refs, states = list(refs), []
    for count in counts:
        states.append(tuple(refs[:count]) if count > 1 else refs[0])
        del refs[:count]
    return states, refs


def flattened(states):
    flat = [state if type(state) is tuple else (state,) for state in states]
    return [len(state) for state in flat], [part for state in flat for part in state]


def block_of(part, block, parts=2):
    if part.ndim == 2:
        return pl.BlockSpec((part.shape[0], block), lambda j: (0, j))
    return pl.BlockSpec((parts, part.shape[1], block), lambda j: (0, 0, j))


def joined(pieces, place):
    if len(pieces) == 1:
        return pieces[0]

    @pl.when(pl.program_id(0) == 0)
    def _():
        size = pieces[0].shape[0]
        for b, piece in enumerate(pieces):
            place[b * size : (b + 1) * size] = piece[...]

    return place


def forward_kernel(mix, taken, pieces, waits, sums, emits, flag, *refs):
    rows, refs = refs[:pieces], refs[pieces:]
    sources, refs = regrouped(refs, taken)
    refs = refs[waits:]
    hidden, slope = refs[:2]
    inputs = joined(rows, refs[-1])
    block = [mix(flag[0], *[loaded(source, k) for source in sources]).astype(bf16) for k in range(2 if sums or emits else 1)]
    if emits:
        for k in range(2):
            refs[2 + sums][k] = block[k]
    j = pl.program_id(0)
    value, slope_val = gelu_pair(jnp.dot(inputs[...], block[0], preferred_element_type=f32))
    value = value.astype(bf16)
    hidden[...] = value
    slope[...] = slope_val.astype(bf16)
    if sums:
        partials, total = refs[2 : 2 + sums], refs[-2]
        out = lax.dot_general(value, block[1], (((1,), (1,)), ((), ())), preferred_element_type=f32)

        @pl.when(j == 0)
        def _():
            total[...] = out

        @pl.when(j > 0)
        def _():
            total[...] += out

        @pl.when(j == pl.num_programs(0) - 1)
        def _():
            size = partials[0].shape[0]
            for b, partial in enumerate(partials):
                partial[...] = total[b * size : (b + 1) * size].astype(bf16)


def forward(flag, inputs, sources, mix, sums, emits=True, waits=()):
    count, width = inputs[0].shape
    rows = count * len(inputs)
    units = sources[0].shape[2]
    block = min(units, 512)
    parts = 2 if sums or emits else 1
    counts, flat = flattened(sources)
    unit_spec = pl.BlockSpec((rows, block), lambda j: (0, j))
    shapes = [((rows, units), unit_spec), ((rows, units), unit_spec)]
    if sums:
        shapes += [((rows // sums, width), whole((rows // sums, width)))] * sums
    shapes += [(sources[0].shape, block_of(sources[0], block))] * emits
    return pl.pallas_call(
        functools.partial(forward_kernel, mix, counts, len(inputs), len(waits), sums, emits),
        grid=(units // block,),
        in_specs=[pl.BlockSpec(memory_space=pltpu.SMEM)]
        + [whole(piece.shape) for piece in inputs]
        + [block_of(part, block, parts) for part in flat]
        + [ANY] * len(waits),
        out_specs=[spec for _, spec in shapes],
        out_shape=[jax.ShapeDtypeStruct(shape, bf16) for shape, _ in shapes],
        scratch_shapes=[pltpu.VMEM((rows, width), f32)] * bool(sums) + [pltpu.VMEM((rows, width), bf16)],
        compiler_params=pltpu.CompilerParams(vmem_limit_bytes=56 << 20),
        cost_estimate=LIGHT,
    )(flag, *inputs, *flat, *waits)


def only(flag, weights):
    return weights


def pushed(flag, weights, first, second):
    return weights - 0.5 * learn_rate * (first + second)


def halved(flag, found, weights, sent):
    return 0.5 * (weights + jnp.where(flag == 0, sent, found))


def backward_kernel(update, taken, pieces, given, by_core, flag, weights, slope, hidden, *refs):
    states, refs = regrouped(refs, taken)
    error_count, input_count = pieces
    errors, inputs = refs[:error_count], refs[error_count : error_count + input_count]
    error, error_t, rows, inputs_t = refs[-4:]
    refs = refs[error_count + input_count : -4]
    results, _ = regrouped(refs[len(refs) - sum(given) :], given)
    error, rows = joined(errors, error), joined(inputs, rows)

    @pl.when(pl.program_id(0) == 0)
    def _():
        error_t[...] = error[...].T
        inputs_t[...] = rows[...].T

    back = jnp.dot(error[...], weights[0].astype(bf16), preferred_element_type=f32) * slope[...].astype(f32)
    for k, (left, right) in enumerate(((inputs_t[...], back.astype(bf16)), (error_t[...], hidden[...]))):
        grad = jnp.dot(left, right, preferred_element_type=f32)
        values = update(grad, *[loaded(state, k) for state in states])
        for result, apart, value in zip(results, by_core, values):
            if type(result) is not tuple:
                result[k] = value.astype(result.dtype)
                continue
            if apart:
                mine, *others = result

                @pl.when(flag[0] == k)
                def _():
                    mine[...] = value.astype(mine.dtype)

                @pl.when(flag[0] != k)
                def _():
                    size = others[0].shape[0]
                    for i, piece in enumerate(others):
                        piece[...] = value[i * size : (i + 1) * size].astype(piece.dtype)

                continue
            each = len(result) // 2
            for i, piece in enumerate(result[k * each : (k + 1) * each]):
                size = piece.shape[0]
                piece[...] = value[i * size : (i + 1) * size].astype(piece.dtype)


def backward(flag, errors, weights, slope, hidden, inputs, states, update, kinds, waits=()):
    rows, width = hidden.shape[0], weights.shape[1]
    units = weights.shape[2]
    block = min(units, 512)
    counts, flat = flattened(states)
    kinds = [kind if type(kind) is tuple else (kind, 1) for kind in kinds]
    by_core = [count == "core" for _, count in kinds]
    kinds = [(kind, 3 if apart else count) for (kind, count), apart in zip(kinds, by_core)]
    shapes = []
    for (kind, count), apart in zip(kinds, by_core):
        if apart:
            parts = [(width, units), (width // 2, units), (width // 2, units)]
        else:
            parts = [weights.shape if count == 1 else (2 * width // count, units)] * count
        shapes += [jax.ShapeDtypeStruct(part, kind) for part in parts]
    results = pl.pallas_call(
        functools.partial(
            backward_kernel, update, counts, (len(errors), len(inputs)), [count for _, count in kinds], by_core
        ),
        grid=(units // block,),
        in_specs=[
            pl.BlockSpec(memory_space=pltpu.SMEM),
            pl.BlockSpec((1, width, block), lambda j: (1, 0, j)),
            pl.BlockSpec((rows, block), lambda j: (0, j)),
            pl.BlockSpec((rows, block), lambda j: (0, j)),
        ]
        + [block_of(part, block) for part in flat]
        + [whole(piece.shape) for piece in (*errors, *inputs)]
        + [ANY] * len(waits),
        out_specs=[block_of(shape, block) for shape in shapes],
        out_shape=shapes,
        scratch_shapes=[pltpu.VMEM((rows, width), bf16), pltpu.VMEM((width, rows), bf16)] * 2,
        compiler_params=pltpu.CompilerParams(vmem_limit_bytes=56 << 20),
        cost_estimate=LIGHT,
    )(flag, weights, slope, hidden, *flat, *errors, *inputs, *waits)
    return regrouped(results, [count for _, count in kinds])[0]


def first_update(grad, moment):
    moment = inner_beta * moment + grad
    return (moment, moment)


def first_beside(grad, moment, own_moment, weights):
    moment = inner_beta * moment + grad
    return (moment, weights - 0.5 * learn_rate * (own_moment + moment))


def second_update(grad, moment, weights):
    moment_new = inner_beta * moment + grad
    return (moment_new, weights - learn_rate * moment_new, moment + (1.0 + inner_beta) * moment_new)


def second_beside(grad, moment, weights):
    return (weights - learn_rate * (inner_beta * moment + grad),)


def third_update(grad, moment, known):
    return (inner_beta * moment + grad, known + grad)


def rounded(value):
    return lax.reduce_precision(value, 8, 7).astype(bf16)


def added(left, right):
    return rounded(left.astype(f32) + right.astype(f32))


def nothing(*refs):
    pass


def tied(waits, block):
    return pl.pallas_call(
        nothing,
        in_specs=[ANY] * (1 + len(waits)),
        out_specs=ANY,
        out_shape=jax.ShapeDtypeStruct(block.shape, block.dtype),
        input_output_aliases={0: 0},
        cost_estimate=LIGHT,
    )(block, *waits)


def join_kernel(count, *refs):
    size = refs[0].shape[0]
    for b, piece in enumerate(refs[:count]):
        refs[-1][b * size : (b + 1) * size] = piece[...]


def join(pieces, waits):
    size, width = pieces[0].shape
    shape = (size * len(pieces), width)
    return pl.pallas_call(
        functools.partial(join_kernel, len(pieces)),
        grid=(1,),
        in_specs=[whole(piece.shape) for piece in pieces] + [ANY] * len(waits),
        out_specs=whole(shape),
        out_shape=jax.ShapeDtypeStruct(shape, pieces[0].dtype),
        cost_estimate=LIGHT,
    )(*pieces, *waits)


def finish_kernel(replicas, flag, slow, anchor, own, theirs, *refs):
    anchor_new, slow_new, token = refs[-3:]
    for k in range(2):
        total = jnp.where(flag[0] == k, own[...].astype(f32), theirs[...].astype(f32))
        value = slow_beta * slow[k] + total / replicas
        slow_new[k] = value
        anchor_new[k] = anchor[k] - learn_rate * value
    token[...] = jnp.zeros_like(token)


def finish(flag, replicas, slow, anchor, own, theirs, position, before):
    size, units = own.shape
    steps = 2
    rows = pl.BlockSpec((2, size // steps, units), lambda j: (0, position * steps + j, 0))
    part = pl.BlockSpec((size // steps, units), lambda j: (j, 0))
    shape = jax.ShapeDtypeStruct(slow.shape, f32)
    return pl.pallas_call(
        functools.partial(finish_kernel, replicas),
        grid=(steps,),
        in_specs=[pl.BlockSpec(memory_space=pltpu.SMEM), rows, rows, part, part] + [ANY] * len(before),
        out_specs=[rows, rows, whole((8, 128))],
        out_shape=[shape, shape, jax.ShapeDtypeStruct((8, 128), bf16)],
        input_output_aliases={5 + k: k for k in range(len(before))},
        compiler_params=pltpu.CompilerParams(vmem_limit_bytes=60 << 20),
        cost_estimate=LIGHT,
    )(flag, slow, anchor, own, theirs, *before)


def slow_step(flag, mine, others, slow, anchor):
    axis, cores = "replica", 2
    index = lax.axis_index(axis)
    replicas = lax.axis_size(axis)
    chip = index // cores
    length = replicas // cores
    half = length // 2
    rows = mine.shape[0]
    size = rows // chunks

    def moved(part, hops):
        return lax.ppermute(part, axis, [(cores * a + c, cores * b + c) for a, b in hops for c in range(cores)])

    def at(places):
        return functools.reduce(jnp.logical_or, [chip == place for place in places])

    stages = [(True, [(s, s + 1), (length - 1 - s, length - 2 - s)]) for s in range(half - 1)]
    if half:
        stages.append((True, [(half - 1, half), (half, half - 1)]))
    stages += [(False, [(s + 1, s), (length - 2 - s, length - 1 - s)]) for s in reversed(range(half - 1))]

    pair_rows = rows // 2
    pairs = [swapped(part, axis, 1) for part in others]
    blocks = []
    for c in range(chunks):
        p, start = divmod(c * size, pair_rows)
        blocks.append(added(mine[c * size : (c + 1) * size], pairs[p][start : start + size]))
    arrived, made, results, tokens = {}, {}, [], []
    final = len(stages) - 1
    for tick in range(chunks + len(stages)):
        for s in reversed(range(len(stages) + 1)):
            c = tick - s
            if not 0 <= c < chunks:
                continue
            block = blocks[c]
            if s:
                adds, hops = stages[s - 1]
                fresh = added(block, arrived[s - 1, c]) if adds else arrived[s - 1, c]
                block = jnp.where(at([b for _, b in hops]), fresh, block)
                if s > final and 0 < c < chunks - 1:
                    block = tied([tokens[c - 1]], block)
            if s == 0 and c >= 3 and (2, c - 3) in made:
                block = tied([made[2, c - 3]], block)
            blocks[c] = made[s, c] = block
            if s < len(stages):
                arrived[s, c] = moved(block, stages[s][1])
            else:
                theirs = swapped(block, axis, 1)
                *results, token = finish(flag, replicas, slow, anchor, block, theirs, c, results)
                tokens.append(token)
    return results


def body(tokens, targets, row_ids, anchor, momentum, slow):
    row_count = tokens.shape[0]
    scale = 1.0 / row_count
    tensors = lax.axis_size("tensor")
    share_rows = row_count // tensors
    order = lax.axis_index("tensor") ^ jnp.arange(tensors)
    picks_all = row_ids[0].reshape(INNER, tensors, share_rows)[:, order].reshape(INNER, row_count)

    replicas = lax.axis_size("replica")
    flag = (lax.axis_index("replica") % 2).astype(jnp.int32).reshape(1)

    def gathered(own):
        return [own] + [swapped(own, "tensor", m) for m in range(1, tensors)]

    def error_share(partials, step):
        wanted = targets.at[picks_all[step, :share_rows]].get(mode="promise_in_bounds")
        share = partials[0].astype(f32)
        for m in range(1, tensors):
            share = share + swapped(partials[m], "tensor", m).astype(f32)
        return ((share - wanted.astype(f32)) * scale).astype(bf16)

    def sent(block, distance, which=(0, 1)):
        route = [((i - distance) % replicas, i) for i in range(replicas) if i % 2 in which]
        return lax.ppermute(block, "replica", route)

    def picked(step, count):
        return tokens.at[picks_all[step, :count]].get(mode="promise_in_bounds")

    near_share = sent(picked(0, share_rows), 1)
    narrow = tied([near_share], momentum[0].astype(bf16))
    moment_near = sent(narrow, 1)

    inputs = [picked(0, row_count)]
    hidden, slope, *partials = forward(flag, inputs, [anchor], only, tensors, emits=False, waits=[narrow])
    inputs_next = picked(1, row_count)
    error = join(gathered(error_share(partials, 0)), [inputs_next])
    error_near = sent(error, 1)
    moment, moment_bf = backward(
        flag,
        [error],
        anchor,
        slope,
        hidden,
        inputs,
        [momentum[0]],
        first_update,
        [f32, (bf16, 2)],
    )
    inputs_near = gathered(near_share)
    hidden_near, slope_near = forward(flag, inputs_near, [anchor], only, 0, emits=False, waits=[moment])
    moment_far = [sent(tied([error_near, hidden_near], part), 2, (0,)) for part in moment_bf]
    moment_near, weights = backward(
        flag,
        [error_near],
        anchor,
        slope_near,
        hidden_near,
        inputs_near,
        [moment_near, moment, anchor],
        first_beside,
        [(bf16, 2), bf16],
    )

    inputs = [tied([moment_near[0]], inputs_next)]
    inputs_far = sent(inputs[0], 2, (1,))
    hidden, slope, *partials = forward(flag, inputs, [weights], only, tensors, emits=False)
    error = jnp.concatenate(gathered(error_share(partials, 1)))
    error_far = sent(error, 2, (1,))
    moment, weights, known = backward(
        flag,
        [error],
        weights,
        slope,
        hidden,
        inputs,
        [moment, weights],
        second_update,
        [f32, bf16, bf16],
        waits=moment_far,
    )
    weights = tied([error_far[:16], inputs_far[:16]], weights)
    weights_sent = sent(weights, 2, (0,))
    moment_two = tuple(sent(tied([weights], part), 1, (1,)) for part in moment_near)
    moment_three = tuple(sent(tied([weights], part), 1, (1,)) for part in moment_far)
    hidden, slope, weights_far = forward(flag, [inputs_far], [anchor, moment_two, moment_three], pushed, 0)
    (weights_found,) = backward(
        flag, [error_far], weights_far, slope, hidden, [inputs_far], [moment_two, weights_far], second_beside, [bf16]
    )

    inputs = [picked(2, row_count)]
    hidden, slope, *rest = forward(flag, inputs, [weights_found, weights, weights_sent], halved, tensors)
    errors = gathered(error_share(rest[:tensors], 2))
    moment, total = backward(
        flag, errors, rest[tensors], slope, hidden, inputs, [moment, known], third_update, [f32, (bf16, "core")]
    )
    anchor_new, slow_new = slow_step(flag, total[0], total[1:], slow, anchor)
    return (anchor_new, slow_new, moment[None])


def solution(mesh):
    return jax.shard_map(
        body,
        mesh=mesh,
        in_specs=(
            P("replica", None),
            P("replica", None),
            P("replica", None, None),
            P(None, None, "tensor"),
            P("replica", None, None, "tensor"),
            P(None, None, "tensor"),
        ),
        out_specs=(
            P(None, None, "tensor"),
            P(None, None, "tensor"),
            P("replica", None, None, "tensor"),
        ),
        check_vma=False,
    )
```

```python
import functools

import jax
import jax.numpy as jnp
from jax import lax
from jax.experimental import pallas as pl
from jax.experimental.pallas import tpu as pltpu
from jax.sharding import PartitionSpec as P

INNER = 3


learn_rate = 0.02
inner_beta = 0.9
slow_beta = 0.5
chunks = 4
bf16, f32 = jnp.bfloat16, jnp.float32
ANY = pl.BlockSpec(memory_space=pl.ANY)
LIGHT = pl.CostEstimate(flops=1, bytes_accessed=1, transcendentals=0)


def swapped(block, axis, mask):
    return lax.ppermute(block, axis, [(i, i ^ mask) for i in range(lax.axis_size(axis))])


def gelu_pair(pre):
    coeff = 0.7978845608028654
    square = pre * pre
    tanh_val = jnp.tanh(coeff * (pre + 0.044715 * square * pre))
    half = 0.5 * (1.0 + tanh_val)
    slope = half + 0.5 * pre * (1.0 - tanh_val * tanh_val) * coeff * (1.0 + 3.0 * 0.044715 * square)
    return (pre * half, slope)


def whole(shape):
    return pl.BlockSpec(shape, lambda j: (0,) * len(shape))


def loaded(state, k):
    if type(state) is not tuple:
        return state[k].astype(f32)
    each = len(state) // 2
    return jnp.concatenate([piece[...].astype(f32) for piece in state[k * each : (k + 1) * each]], axis=0)


def regrouped(refs, counts):
    refs, states = list(refs), []
    for count in counts:
        states.append(tuple(refs[:count]) if count > 1 else refs[0])
        del refs[:count]
    return states, refs


def flattened(states):
    flat = [state if type(state) is tuple else (state,) for state in states]
    return [len(state) for state in flat], [part for state in flat for part in state]


def block_of(part, block, parts=2):
    if part.ndim == 2:
        return pl.BlockSpec((part.shape[0], block), lambda j: (0, j))
    return pl.BlockSpec((parts, part.shape[1], block), lambda j: (0, 0, j))


def joined(pieces, place):
    if len(pieces) == 1:
        return pieces[0]

    @pl.when(pl.program_id(0) == 0)
    def _():
        size = pieces[0].shape[0]
        for b, piece in enumerate(pieces):
            place[b * size : (b + 1) * size] = piece[...]

    return place


def forward_kernel(mix, taken, pieces, waits, sums, emits, flag, *refs):
    rows, refs = refs[:pieces], refs[pieces:]
    sources, refs = regrouped(refs, taken)
    refs = refs[waits:]
    hidden, slope = refs[:2]
    inputs = joined(rows, refs[-1])
    block = [mix(flag[0], *[loaded(source, k) for source in sources]).astype(bf16) for k in range(2 if sums or emits else 1)]
    if emits:
        for k in range(2):
            refs[2 + sums][k] = block[k]
    j = pl.program_id(0)
    value, slope_val = gelu_pair(jnp.dot(inputs[...], block[0], preferred_element_type=f32))
    value = value.astype(bf16)
    hidden[...] = value
    slope[...] = slope_val.astype(bf16)
    if sums:
        partials, total = refs[2 : 2 + sums], refs[-2]
        out = lax.dot_general(value, block[1], (((1,), (1,)), ((), ())), preferred_element_type=f32)

        @pl.when(j == 0)
        def _():
            total[...] = out

        @pl.when(j > 0)
        def _():
            total[...] += out

        @pl.when(j == pl.num_programs(0) - 1)
        def _():
            size = partials[0].shape[0]
            for b, partial in enumerate(partials):
                partial[...] = total[b * size : (b + 1) * size].astype(bf16)


def forward(flag, inputs, sources, mix, sums, emits=True, waits=()):
    count, width = inputs[0].shape
    rows = count * len(inputs)
    units = sources[0].shape[2]
    block = min(units, 512)
    parts = 2 if sums or emits else 1
    counts, flat = flattened(sources)
    unit_spec = pl.BlockSpec((rows, block), lambda j: (0, j))
    shapes = [((rows, units), unit_spec), ((rows, units), unit_spec)]
    if sums:
        shapes += [((rows // sums, width), whole((rows // sums, width)))] * sums
    shapes += [(sources[0].shape, block_of(sources[0], block))] * emits
    return pl.pallas_call(
        functools.partial(forward_kernel, mix, counts, len(inputs), len(waits), sums, emits),
        grid=(units // block,),
        in_specs=[pl.BlockSpec(memory_space=pltpu.SMEM)]
        + [whole(piece.shape) for piece in inputs]
        + [block_of(part, block, parts) for part in flat]
        + [ANY] * len(waits),
        out_specs=[spec for _, spec in shapes],
        out_shape=[jax.ShapeDtypeStruct(shape, bf16) for shape, _ in shapes],
        scratch_shapes=[pltpu.VMEM((rows, width), f32)] * bool(sums) + [pltpu.VMEM((rows, width), bf16)],
        compiler_params=pltpu.CompilerParams(vmem_limit_bytes=56 << 20),
        cost_estimate=LIGHT,
    )(flag, *inputs, *flat, *waits)


def only(flag, weights):
    return weights


def pushed(flag, weights, first, second):
    return weights - 0.5 * learn_rate * (first + second)


def halved(flag, known, sent):
    return known + 0.5 * sent


def backward_kernel(update, taken, pieces, given, by_core, flag, weights, slope, hidden, *refs):
    states, refs = regrouped(refs, taken)
    error_count, input_count = pieces
    errors, inputs = refs[:error_count], refs[error_count : error_count + input_count]
    error, error_t, rows, inputs_t = refs[-4:]
    refs = refs[error_count + input_count : -4]
    results, _ = regrouped(refs[len(refs) - sum(given) :], given)
    error, rows = joined(errors, error), joined(inputs, rows)

    @pl.when(pl.program_id(0) == 0)
    def _():
        error_t[...] = error[...].T
        inputs_t[...] = rows[...].T

    back = jnp.dot(error[...], weights[0].astype(bf16), preferred_element_type=f32) * slope[...].astype(f32)
    for k, (left, right) in enumerate(((inputs_t[...], back.astype(bf16)), (error_t[...], hidden[...]))):
        grad = jnp.dot(left, right, preferred_element_type=f32)
        values = update(flag[0], grad, *[loaded(state, k) for state in states])
        for result, apart, value in zip(results, by_core, values):
            if type(result) is not tuple:
                result[k] = value.astype(result.dtype)
                continue
            if apart:
                for place, piece in enumerate(result):

                    @pl.when((flag[0] == k) == (place == 0))
                    def _():
                        piece[...] = value.astype(piece.dtype)

                continue
            each = len(result) // 2
            for i, piece in enumerate(result[k * each : (k + 1) * each]):
                size = piece.shape[0]
                piece[...] = value[i * size : (i + 1) * size].astype(piece.dtype)


def backward(flag, errors, weights, slope, hidden, inputs, states, update, kinds, waits=()):
    rows, width = hidden.shape[0], weights.shape[1]
    units = weights.shape[2]
    block = min(units, 512)
    counts, flat = flattened(states)
    kinds = [kind if type(kind) is tuple else (kind, 1) for kind in kinds]
    by_core = [count == "core" for _, count in kinds]
    kinds = [(kind, 2 if apart else count) for (kind, count), apart in zip(kinds, by_core)]
    shapes = []
    for kind, count in kinds:
        shape = weights.shape if count == 1 else (2 * width // count, units)
        shapes += [jax.ShapeDtypeStruct(shape, kind)] * count
    results = pl.pallas_call(
        functools.partial(
            backward_kernel, update, counts, (len(errors), len(inputs)), [count for _, count in kinds], by_core
        ),
        grid=(units // block,),
        in_specs=[
            pl.BlockSpec(memory_space=pltpu.SMEM),
            pl.BlockSpec((1, width, block), lambda j: (1, 0, j)),
            pl.BlockSpec((rows, block), lambda j: (0, j)),
            pl.BlockSpec((rows, block), lambda j: (0, j)),
        ]
        + [block_of(part, block) for part in flat]
        + [whole(piece.shape) for piece in (*errors, *inputs)]
        + [ANY] * len(waits),
        out_specs=[block_of(shape, block) for shape in shapes],
        out_shape=shapes,
        scratch_shapes=[pltpu.VMEM((rows, width), bf16), pltpu.VMEM((width, rows), bf16)] * 2,
        compiler_params=pltpu.CompilerParams(vmem_limit_bytes=56 << 20),
        cost_estimate=LIGHT,
    )(flag, weights, slope, hidden, *flat, *errors, *inputs, *waits)
    return regrouped(results, [count for _, count in kinds])[0]


def first_update(core, grad, moment):
    moment = inner_beta * moment + grad
    return (moment, moment)


def first_beside(core, grad, moment, own_moment, weights):
    moment = inner_beta * moment + grad
    return (moment, weights - 0.5 * learn_rate * (own_moment + moment))


def second_update(core, grad, moment, weights):
    moment_new = inner_beta * moment + grad
    return (moment_new, weights - learn_rate * moment_new, moment + (1.0 + inner_beta) * moment_new)


def second_beside(core, grad, moment, weights, own):
    found = weights - learn_rate * (inner_beta * moment + grad)
    return (0.5 * jnp.where(core == 0, own, own + found),)


def third_update(core, grad, moment, known):
    return (inner_beta * moment + grad, known + grad)


def rounded(value):
    return lax.reduce_precision(value, 8, 7).astype(bf16)


def added(left, right):
    return rounded(left.astype(f32) + right.astype(f32))


def nothing(*refs):
    pass


def tied(waits, block):
    return pl.pallas_call(
        nothing,
        in_specs=[ANY] * (1 + len(waits)),
        out_specs=ANY,
        out_shape=jax.ShapeDtypeStruct(block.shape, block.dtype),
        input_output_aliases={0: 0},
        cost_estimate=LIGHT,
    )(block, *waits)


def finish_kernel(replicas, flag, slow, anchor, own, theirs, *refs):
    anchor_new, slow_new, token = refs[-3:]
    for k in range(2):
        total = jnp.where(flag[0] == k, own[...].astype(f32), theirs[...].astype(f32))
        value = slow_beta * slow[k] + total / replicas
        slow_new[k] = value
        anchor_new[k] = anchor[k] - learn_rate * value
    token[...] = jnp.zeros_like(token)


def finish(flag, replicas, slow, anchor, own, theirs, position, before):
    size, units = own.shape
    steps = 2
    rows = pl.BlockSpec((2, size // steps, units), lambda j: (0, position * steps + j, 0))
    part = pl.BlockSpec((size // steps, units), lambda j: (j, 0))
    shape = jax.ShapeDtypeStruct(slow.shape, f32)
    return pl.pallas_call(
        functools.partial(finish_kernel, replicas),
        grid=(steps,),
        in_specs=[pl.BlockSpec(memory_space=pltpu.SMEM), rows, rows, part, part] + [ANY] * len(before),
        out_specs=[rows, rows, whole((8, 128))],
        out_shape=[shape, shape, jax.ShapeDtypeStruct((8, 128), bf16)],
        input_output_aliases={5 + k: k for k in range(len(before))},
        compiler_params=pltpu.CompilerParams(vmem_limit_bytes=60 << 20),
        cost_estimate=LIGHT,
    )(flag, slow, anchor, own, theirs, *before)


def slow_step(flag, mine, other, slow, anchor):
    axis, cores = "replica", 2
    index = lax.axis_index(axis)
    replicas = lax.axis_size(axis)
    chip = index // cores
    length = replicas // cores
    half = length // 2
    rows = mine.shape[0]
    size = rows // chunks

    def moved(part, hops):
        return lax.ppermute(part, axis, [(cores * a + c, cores * b + c) for a, b in hops for c in range(cores)])

    def at(places):
        return functools.reduce(jnp.logical_or, [chip == place for place in places])

    stages = [(True, [(s, s + 1), (length - 1 - s, length - 2 - s)]) for s in range(half - 1)]
    if half:
        stages.append((True, [(half - 1, half), (half, half - 1)]))
    stages += [(False, [(s + 1, s), (length - 2 - s, length - 1 - s)]) for s in reversed(range(half - 1))]

    pair_rows = rows // 2
    pairs = [swapped(other[p * pair_rows : (p + 1) * pair_rows], axis, 1) for p in range(2)]
    blocks = []
    for c in range(chunks):
        p, start = divmod(c * size, pair_rows)
        blocks.append(added(mine[c * size : (c + 1) * size], pairs[p][start : start + size]))
    arrived, made, results, tokens = {}, {}, [], []
    final = len(stages) - 1
    for tick in range(chunks + len(stages)):
        for s in reversed(range(len(stages) + 1)):
            c = tick - s
            if not 0 <= c < chunks:
                continue
            block = blocks[c]
            if s:
                adds, hops = stages[s - 1]
                fresh = added(block, arrived[s - 1, c]) if adds else arrived[s - 1, c]
                block = jnp.where(at([b for _, b in hops]), fresh, block)
                if s > final and 0 < c < chunks - 1:
                    block = tied([tokens[c - 1]], block)
            if s == 0 and c >= 3 and (2, c - 3) in made:
                block = tied([made[2, c - 3]], block)
            blocks[c] = made[s, c] = block
            if s < len(stages):
                arrived[s, c] = moved(block, stages[s][1])
            else:
                theirs = swapped(block, axis, 1)
                *results, token = finish(flag, replicas, slow, anchor, block, theirs, c, results)
                tokens.append(token)
    return results


def body(tokens, targets, row_ids, anchor, momentum, slow):
    row_count = tokens.shape[0]
    scale = 1.0 / row_count
    tensors = lax.axis_size("tensor")
    share_rows = row_count // tensors
    order = lax.axis_index("tensor") ^ jnp.arange(tensors)
    picks_all = row_ids[0].reshape(INNER, tensors, share_rows)[:, order].reshape(INNER, row_count)

    replicas = lax.axis_size("replica")
    flag = (lax.axis_index("replica") % 2).astype(jnp.int32).reshape(1)

    def gathered(own):
        return [own] + [swapped(own, "tensor", m) for m in range(1, tensors)]

    def error_share(partials, step):
        wanted = targets.at[picks_all[step, :share_rows]].get(mode="promise_in_bounds")
        share = partials[0].astype(f32)
        for m in range(1, tensors):
            share = share + swapped(partials[m], "tensor", m).astype(f32)
        return ((share - wanted.astype(f32)) * scale).astype(bf16)

    def sent(block, distance, which=(0, 1)):
        route = [((i - distance) % replicas, i) for i in range(replicas) if i % 2 in which]
        return lax.ppermute(block, "replica", route)

    def picked(step, count):
        return tokens.at[picks_all[step, :count]].get(mode="promise_in_bounds")

    near_share = sent(picked(0, share_rows), 1)
    narrow = tied([near_share], momentum[0].astype(bf16))
    moment_near = sent(narrow, 1)

    inputs = [picked(0, row_count)]
    hidden, slope, *partials = forward(flag, inputs, [anchor], only, tensors, emits=False, waits=[narrow])
    inputs_next = picked(1, row_count)
    own_error = jnp.where(flag[0] < 2, error_share(partials, 0), inputs_next[:share_rows])
    error = jnp.concatenate(gathered(own_error))
    error_near = sent(error, 1)
    moment, moment_bf = backward(
        flag,
        [error],
        anchor,
        slope,
        hidden,
        inputs,
        [momentum[0]],
        first_update,
        [f32, (bf16, 2)],
    )
    inputs_near = gathered(near_share)
    hidden_near, slope_near = forward(flag, inputs_near, [anchor], only, 0, emits=False, waits=[moment])
    moment_far = [sent(tied([error_near, hidden_near], part), 2, (0,)) for part in moment_bf]
    moment_near, weights = backward(
        flag,
        [error_near],
        anchor,
        slope_near,
        hidden_near,
        inputs_near,
        [moment_near, moment, anchor],
        first_beside,
        [(bf16, 2), bf16],
    )

    inputs = [tied([moment_near[0]], inputs_next)]
    inputs_far = sent(inputs[0], 2, (1,))
    hidden, slope, *partials = forward(flag, inputs, [weights], only, tensors, emits=False)
    error = jnp.concatenate(gathered(error_share(partials, 1)))
    error_far = sent(error, 2, (1,))
    moment, weights, known = backward(
        flag,
        [error],
        weights,
        slope,
        hidden,
        inputs,
        [moment, weights],
        second_update,
        [f32, bf16, bf16],
        waits=moment_far,
    )
    weights = tied([error_far, inputs_far], weights)
    weights_sent = sent(weights, 2, (0,))
    moment_two = tuple(sent(tied([weights], part), 1, (1,)) for part in moment_near)
    moment_three = tuple(sent(tied([weights], part), 1, (1,)) for part in moment_far)
    hidden, slope, weights_far = forward(flag, [inputs_far], [anchor, moment_two, moment_three], pushed, 0)
    (weights_known,) = backward(
        flag,
        [error_far],
        weights_far,
        slope,
        hidden,
        [inputs_far],
        [moment_two, weights_far, weights],
        second_beside,
        [bf16],
    )

    inputs = [picked(2, row_count)]
    hidden, slope, *rest = forward(flag, inputs, [weights_known, weights_sent], halved, tensors)
    errors = gathered(error_share(rest[:tensors], 2))
    moment, total = backward(
        flag, errors, rest[tensors], slope, hidden, inputs, [moment, known], third_update, [f32, (bf16, "core")]
    )
    anchor_new, slow_new = slow_step(flag, *total, slow, anchor)
    return (anchor_new, slow_new, moment[None])


def solution(mesh):
    return jax.shard_map(
        body,
        mesh=mesh,
        in_specs=(
            P("replica", None),
            P("replica", None),
            P("replica", None, None),
            P(None, None, "tensor"),
            P("replica", None, None, "tensor"),
            P(None, None, "tensor"),
        ),
        out_specs=(
            P(None, None, "tensor"),
            P(None, None, "tensor"),
            P("replica", None, None, "tensor"),
        ),
        check_vma=False,
    )
```

```python
import functools

import jax
import jax.numpy as jnp
from jax import lax
from jax.experimental import pallas as pl
from jax.experimental.pallas import tpu as pltpu
from jax.sharding import PartitionSpec as P

INNER = 3


learn_rate = 0.02
inner_beta = 0.9
slow_beta = 0.5
chunks = 4
bf16, f32 = jnp.bfloat16, jnp.float32
ANY = pl.BlockSpec(memory_space=pl.ANY)
LIGHT = pl.CostEstimate(flops=1, bytes_accessed=1, transcendentals=0)


def swapped(block, axis, mask):
    return lax.ppermute(block, axis, [(i, i ^ mask) for i in range(lax.axis_size(axis))])


def gelu_pair(pre):
    coeff = 0.7978845608028654
    square = pre * pre
    tanh_val = jnp.tanh(coeff * (pre + 0.044715 * square * pre))
    half = 0.5 * (1.0 + tanh_val)
    slope = half + 0.5 * pre * (1.0 - tanh_val * tanh_val) * coeff * (1.0 + 3.0 * 0.044715 * square)
    return (pre * half, slope)


def whole(shape):
    return pl.BlockSpec(shape, lambda j: (0,) * len(shape))


def loaded(state, k):
    if type(state) is not tuple:
        return state[k].astype(f32)
    each = len(state) // 2
    return jnp.concatenate([piece[...].astype(f32) for piece in state[k * each : (k + 1) * each]], axis=0)


def regrouped(refs, counts):
    refs, states = list(refs), []
    for count in counts:
        states.append(tuple(refs[:count]) if count > 1 else refs[0])
        del refs[:count]
    return states, refs


def flattened(states):
    flat = [state if type(state) is tuple else (state,) for state in states]
    return [len(state) for state in flat], [part for state in flat for part in state]


def block_of(part, block, parts=2):
    if part.ndim == 2:
        return pl.BlockSpec((part.shape[0], block), lambda j: (0, j))
    return pl.BlockSpec((parts, part.shape[1], block), lambda j: (0, 0, j))


def joined(pieces, place):
    if len(pieces) == 1:
        return pieces[0]

    @pl.when(pl.program_id(0) == 0)
    def _():
        size = pieces[0].shape[0]
        for b, piece in enumerate(pieces):
            place[b * size : (b + 1) * size] = piece[...]

    return place


def forward_kernel(mix, taken, pieces, waits, sums, emits, flag, *refs):
    rows, refs = refs[:pieces], refs[pieces:]
    sources, refs = regrouped(refs, taken)
    refs = refs[waits:]
    hidden, slope = refs[:2]
    inputs = joined(rows, refs[-1])
    block = [mix(flag[0], *[loaded(source, k) for source in sources]).astype(bf16) for k in range(2 if sums or emits else 1)]
    if emits:
        for k in range(2):
            refs[2 + sums][k] = block[k]
    j = pl.program_id(0)
    value, slope_val = gelu_pair(jnp.dot(inputs[...], block[0], preferred_element_type=f32))
    value = value.astype(bf16)
    hidden[...] = value
    slope[...] = slope_val.astype(bf16)
    if sums:
        partials, total = refs[2 : 2 + sums], refs[-2]
        out = lax.dot_general(value, block[1], (((1,), (1,)), ((), ())), preferred_element_type=f32)

        @pl.when(j == 0)
        def _():
            total[...] = out

        @pl.when(j > 0)
        def _():
            total[...] += out

        @pl.when(j == pl.num_programs(0) - 1)
        def _():
            size = partials[0].shape[0]
            for b, partial in enumerate(partials):
                partial[...] = total[b * size : (b + 1) * size].astype(bf16)


def forward(flag, inputs, sources, mix, sums, emits=True, waits=()):
    count, width = inputs[0].shape
    rows = count * len(inputs)
    units = sources[0].shape[2]
    block = min(units, 512)
    parts = 2 if sums or emits else 1
    counts, flat = flattened(sources)
    unit_spec = pl.BlockSpec((rows, block), lambda j: (0, j))
    shapes = [((rows, units), unit_spec), ((rows, units), unit_spec)]
    if sums:
        shapes += [((rows // sums, width), whole((rows // sums, width)))] * sums
    shapes += [(sources[0].shape, block_of(sources[0], block))] * emits
    return pl.pallas_call(
        functools.partial(forward_kernel, mix, counts, len(inputs), len(waits), sums, emits),
        grid=(units // block,),
        in_specs=[pl.BlockSpec(memory_space=pltpu.SMEM)]
        + [whole(piece.shape) for piece in inputs]
        + [block_of(part, block, parts) for part in flat]
        + [ANY] * len(waits),
        out_specs=[spec for _, spec in shapes],
        out_shape=[jax.ShapeDtypeStruct(shape, bf16) for shape, _ in shapes],
        scratch_shapes=[pltpu.VMEM((rows, width), f32)] * bool(sums) + [pltpu.VMEM((rows, width), bf16)],
        compiler_params=pltpu.CompilerParams(vmem_limit_bytes=56 << 20),
        cost_estimate=LIGHT,
    )(flag, *inputs, *flat, *waits)


def only(flag, weights):
    return weights


def pushed(flag, weights, first, second):
    return weights - 0.5 * learn_rate * (first + second)


def halved(flag, known, sent):
    return known + 0.5 * sent


def backward_kernel(update, taken, pieces, given, by_core, flag, weights, slope, hidden, *refs):
    states, refs = regrouped(refs, taken)
    error_count, input_count = pieces
    errors, inputs = refs[:error_count], refs[error_count : error_count + input_count]
    error, error_t, rows, inputs_t = refs[-4:]
    refs = refs[error_count + input_count : -4]
    results, _ = regrouped(refs[len(refs) - sum(given) :], given)
    error, rows = joined(errors, error), joined(inputs, rows)

    @pl.when(pl.program_id(0) == 0)
    def _():
        error_t[...] = error[...].T
        inputs_t[...] = rows[...].T

    back = jnp.dot(error[...], weights[0].astype(bf16), preferred_element_type=f32) * slope[...].astype(f32)
    for k, (left, right) in enumerate(((inputs_t[...], back.astype(bf16)), (error_t[...], hidden[...]))):
        grad = jnp.dot(left, right, preferred_element_type=f32)
        values = update(flag[0], grad, *[loaded(state, k) for state in states])
        for result, apart, value in zip(results, by_core, values):
            if type(result) is not tuple:
                result[k] = value.astype(result.dtype)
                continue
            if apart:
                for place, piece in enumerate(result):

                    @pl.when((flag[0] == k) == (place == 0))
                    def _():
                        piece[...] = value.astype(piece.dtype)

                continue
            each = len(result) // 2
            for i, piece in enumerate(result[k * each : (k + 1) * each]):
                size = piece.shape[0]
                piece[...] = value[i * size : (i + 1) * size].astype(piece.dtype)


def backward(flag, errors, weights, slope, hidden, inputs, states, update, kinds, waits=()):
    rows, width = hidden.shape[0], weights.shape[1]
    units = weights.shape[2]
    block = min(units, 512)
    counts, flat = flattened(states)
    kinds = [kind if type(kind) is tuple else (kind, 1) for kind in kinds]
    by_core = [count == "core" for _, count in kinds]
    kinds = [(kind, 2 if apart else count) for (kind, count), apart in zip(kinds, by_core)]
    shapes = []
    for kind, count in kinds:
        shape = weights.shape if count == 1 else (2 * width // count, units)
        shapes += [jax.ShapeDtypeStruct(shape, kind)] * count
    results = pl.pallas_call(
        functools.partial(
            backward_kernel, update, counts, (len(errors), len(inputs)), [count for _, count in kinds], by_core
        ),
        grid=(units // block,),
        in_specs=[
            pl.BlockSpec(memory_space=pltpu.SMEM),
            pl.BlockSpec((1, width, block), lambda j: (1, 0, j)),
            pl.BlockSpec((rows, block), lambda j: (0, j)),
            pl.BlockSpec((rows, block), lambda j: (0, j)),
        ]
        + [block_of(part, block) for part in flat]
        + [whole(piece.shape) for piece in (*errors, *inputs)]
        + [ANY] * len(waits),
        out_specs=[block_of(shape, block) for shape in shapes],
        out_shape=shapes,
        scratch_shapes=[pltpu.VMEM((rows, width), bf16), pltpu.VMEM((width, rows), bf16)] * 2,
        compiler_params=pltpu.CompilerParams(vmem_limit_bytes=56 << 20),
        cost_estimate=LIGHT,
    )(flag, weights, slope, hidden, *flat, *errors, *inputs, *waits)
    return regrouped(results, [count for _, count in kinds])[0]


def first_update(core, grad, moment):
    moment = inner_beta * moment + grad
    return (moment, moment)


def first_beside(core, grad, moment, own_moment, weights):
    moment = inner_beta * moment + grad
    return (moment, weights - 0.5 * learn_rate * (own_moment + moment))


def second_update(core, grad, moment, weights):
    moment_new = inner_beta * moment + grad
    return (moment_new, weights - learn_rate * moment_new, moment + (1.0 + inner_beta) * moment_new)


def second_beside(core, grad, moment, weights, own):
    found = weights - learn_rate * (inner_beta * moment + grad)
    return (0.5 * jnp.where(core == 0, own, own + found),)


def third_update(core, grad, moment, known):
    return (inner_beta * moment + grad, known + grad)


def rounded(value):
    return lax.reduce_precision(value, 8, 7).astype(bf16)


def added(left, right):
    return rounded(left.astype(f32) + right.astype(f32))


def nothing(*refs):
    pass


def tied(waits, block):
    return pl.pallas_call(
        nothing,
        in_specs=[ANY] * (1 + len(waits)),
        out_specs=ANY,
        out_shape=jax.ShapeDtypeStruct(block.shape, block.dtype),
        input_output_aliases={0: 0},
        cost_estimate=LIGHT,
    )(block, *waits)


def finish_kernel(replicas, flag, slow, anchor, own, theirs, *refs):
    anchor_new, slow_new, token = refs[-3:]
    for k in range(2):
        total = jnp.where(flag[0] == k, own[...].astype(f32), theirs[...].astype(f32))
        value = slow_beta * slow[k] + total / replicas
        slow_new[k] = value
        anchor_new[k] = anchor[k] - learn_rate * value
    token[...] = jnp.zeros_like(token)


def finish(flag, replicas, slow, anchor, own, theirs, position, before):
    size, units = own.shape
    steps = 2
    rows = pl.BlockSpec((2, size // steps, units), lambda j: (0, position * steps + j, 0))
    part = pl.BlockSpec((size // steps, units), lambda j: (j, 0))
    shape = jax.ShapeDtypeStruct(slow.shape, f32)
    return pl.pallas_call(
        functools.partial(finish_kernel, replicas),
        grid=(steps,),
        in_specs=[pl.BlockSpec(memory_space=pltpu.SMEM), rows, rows, part, part] + [ANY] * len(before),
        out_specs=[rows, rows, whole((8, 128))],
        out_shape=[shape, shape, jax.ShapeDtypeStruct((8, 128), bf16)],
        input_output_aliases={5 + k: k for k in range(len(before))},
        compiler_params=pltpu.CompilerParams(vmem_limit_bytes=60 << 20),
        cost_estimate=LIGHT,
    )(flag, slow, anchor, own, theirs, *before)


def slow_step(flag, mine, other, slow, anchor):
    axis, cores = "replica", 2
    index = lax.axis_index(axis)
    replicas = lax.axis_size(axis)
    chip = index // cores
    length = replicas // cores
    half = length // 2
    rows = mine.shape[0]
    size = rows // chunks

    def moved(part, hops):
        return lax.ppermute(part, axis, [(cores * a + c, cores * b + c) for a, b in hops for c in range(cores)])

    def at(places):
        return functools.reduce(jnp.logical_or, [chip == place for place in places])

    stages = [(True, [(s, s + 1), (length - 1 - s, length - 2 - s)]) for s in range(half - 1)]
    if half:
        stages.append((True, [(half - 1, half), (half, half - 1)]))
    stages += [(False, [(s + 1, s), (length - 2 - s, length - 1 - s)]) for s in reversed(range(half - 1))]

    pair_rows = rows // 2
    pairs = [swapped(other[p * pair_rows : (p + 1) * pair_rows], axis, 1) for p in range(2)]
    blocks = []
    for c in range(chunks):
        p, start = divmod(c * size, pair_rows)
        blocks.append(added(mine[c * size : (c + 1) * size], pairs[p][start : start + size]))
    arrived, made, results, tokens = {}, {}, [], []
    final = len(stages) - 1
    for tick in range(chunks + len(stages)):
        for s in reversed(range(len(stages) + 1)):
            c = tick - s
            if not 0 <= c < chunks:
                continue
            block = blocks[c]
            if s:
                adds, hops = stages[s - 1]
                fresh = added(block, arrived[s - 1, c]) if adds else arrived[s - 1, c]
                block = jnp.where(at([b for _, b in hops]), fresh, block)
                if s > final and 0 < c < chunks - 1:
                    block = tied([tokens[c - 1]], block)
            if s == 0 and c >= 3 and (2, c - 3) in made:
                block = tied([made[2, c - 3]], block)
            blocks[c] = made[s, c] = block
            if s < len(stages):
                arrived[s, c] = moved(block, stages[s][1])
            else:
                theirs = swapped(block, axis, 1)
                *results, token = finish(flag, replicas, slow, anchor, block, theirs, c, results)
                tokens.append(token)
    return results


def body(tokens, targets, row_ids, anchor, momentum, slow):
    row_count = tokens.shape[0]
    scale = 1.0 / row_count
    tensors = lax.axis_size("tensor")
    share_rows = row_count // tensors
    order = lax.axis_index("tensor") ^ jnp.arange(tensors)
    picks_all = row_ids[0].reshape(INNER, tensors, share_rows)[:, order].reshape(INNER, row_count)

    replicas = lax.axis_size("replica")
    flag = (lax.axis_index("replica") % 2).astype(jnp.int32).reshape(1)

    def gathered(own):
        return [own] + [swapped(own, "tensor", m) for m in range(1, tensors)]

    def error_share(partials, step):
        wanted = targets.at[picks_all[step, :share_rows]].get(mode="promise_in_bounds")
        share = partials[0].astype(f32)
        for m in range(1, tensors):
            share = share + swapped(partials[m], "tensor", m).astype(f32)
        return ((share - wanted.astype(f32)) * scale).astype(bf16)

    def sent(block, distance, which=(0, 1)):
        route = [((i - distance) % replicas, i) for i in range(replicas) if i % 2 in which]
        return lax.ppermute(block, "replica", route)

    def picked(step, count):
        return tokens.at[picks_all[step, :count]].get(mode="promise_in_bounds")

    near_share = sent(picked(0, share_rows), 1)
    narrow = tied([near_share], momentum[0].astype(bf16))
    moment_near = sent(narrow, 1)
    inputs_near = gathered(near_share)

    inputs = [picked(0, row_count)]
    hidden, slope, *partials = forward(flag, inputs, [anchor], only, tensors, emits=False, waits=[narrow])
    partials[1] = tied(inputs_near[1:], partials[1])
    hidden_near, slope_near = forward(flag, inputs_near, [anchor], only, 0, emits=False)
    inputs_next = picked(1, row_count)
    own_error = jnp.where(flag[0] < 2, error_share(partials, 0), inputs_next[:share_rows] + hidden_near[:1, :1])
    error = jnp.concatenate(gathered(own_error))
    error_near = sent(error, 1)
    moment, moment_bf = backward(
        flag,
        [error],
        anchor,
        slope,
        hidden,
        inputs,
        [momentum[0]],
        first_update,
        [f32, (bf16, 2)],
    )
    moment_far = [sent(tied([error_near, hidden_near], part), 2, (0,)) for part in moment_bf]
    moment_near, weights = backward(
        flag,
        [error_near],
        anchor,
        slope_near,
        hidden_near,
        inputs_near,
        [moment_near, moment, anchor],
        first_beside,
        [(bf16, 2), bf16],
    )

    inputs = [tied([moment_near[0]], inputs_next)]
    inputs_far = sent(inputs[0], 2, (1,))
    hidden, slope, *partials = forward(flag, inputs, [weights], only, tensors, emits=False)
    error = jnp.concatenate(gathered(error_share(partials, 1)))
    error_far = sent(error, 2, (1,))
    moment, weights, known = backward(
        flag,
        [error],
        weights,
        slope,
        hidden,
        inputs,
        [moment, weights],
        second_update,
        [f32, bf16, bf16],
        waits=moment_far,
    )
    weights = tied([error_far, inputs_far], weights)
    weights_sent = sent(weights, 2, (0,))
    moment_two = tuple(sent(tied([weights], part), 1, (1,)) for part in moment_near)
    moment_three = tuple(sent(tied([weights], part), 1, (1,)) for part in moment_far)
    hidden, slope, weights_far = forward(flag, [inputs_far], [anchor, moment_two, moment_three], pushed, 0)
    (weights_known,) = backward(
        flag,
        [error_far],
        weights_far,
        slope,
        hidden,
        [inputs_far],
        [moment_two, weights_far, weights],
        second_beside,
        [bf16],
    )

    inputs = [picked(2, row_count)]
    hidden, slope, *rest = forward(flag, inputs, [weights_known, weights_sent], halved, tensors)
    errors = gathered(error_share(rest[:tensors], 2))
    moment, total = backward(
        flag, errors, rest[tensors], slope, hidden, inputs, [moment, known], third_update, [f32, (bf16, "core")]
    )
    anchor_new, slow_new = slow_step(flag, *total, slow, anchor)
    return (anchor_new, slow_new, moment[None])


def solution(mesh):
    return jax.shard_map(
        body,
        mesh=mesh,
        in_specs=(
            P("replica", None),
            P("replica", None),
            P("replica", None, None),
            P(None, None, "tensor"),
            P("replica", None, None, "tensor"),
            P(None, None, "tensor"),
        ),
        out_specs=(
            P(None, None, "tensor"),
            P(None, None, "tensor"),
            P("replica", None, None, "tensor"),
        ),
        check_vma=False,
    )
```

```python
import functools

import jax
import jax.numpy as jnp
from jax import lax
from jax.experimental import pallas as pl
from jax.experimental.pallas import tpu as pltpu
from jax.sharding import PartitionSpec as P

INNER = 3


learn_rate = 0.02
inner_beta = 0.9
slow_beta = 0.5
chunks = 4
bf16, f32 = jnp.bfloat16, jnp.float32
ANY = pl.BlockSpec(memory_space=pl.ANY)
LIGHT = pl.CostEstimate(flops=1, bytes_accessed=1, transcendentals=0)


def swapped(block, axis, mask):
    return lax.ppermute(block, axis, [(i, i ^ mask) for i in range(lax.axis_size(axis))])


def gelu_pair(pre):
    coeff = 0.7978845608028654
    square = pre * pre
    tanh_val = jnp.tanh(coeff * (pre + 0.044715 * square * pre))
    half = 0.5 * (1.0 + tanh_val)
    slope = half + 0.5 * pre * (1.0 - tanh_val * tanh_val) * coeff * (1.0 + 3.0 * 0.044715 * square)
    return (pre * half, slope)


def whole(shape):
    return pl.BlockSpec(shape, lambda j: (0,) * len(shape))


def loaded(state, k):
    if type(state) is not tuple:
        return state[k].astype(f32)
    each = len(state) // 2
    return jnp.concatenate([piece[...].astype(f32) for piece in state[k * each : (k + 1) * each]], axis=0)


def regrouped(refs, counts):
    refs, states = list(refs), []
    for count in counts:
        states.append(tuple(refs[:count]) if count > 1 else refs[0])
        del refs[:count]
    return states, refs


def flattened(states):
    flat = [state if type(state) is tuple else (state,) for state in states]
    return [len(state) for state in flat], [part for state in flat for part in state]


def block_of(part, block, parts=2):
    if part.ndim == 2:
        return pl.BlockSpec((part.shape[0], block), lambda j: (0, j))
    return pl.BlockSpec((parts, part.shape[1], block), lambda j: (0, 0, j))


def joined(pieces, place):
    if len(pieces) == 1:
        return pieces[0]

    @pl.when(pl.program_id(0) == 0)
    def _():
        size = pieces[0].shape[0]
        for b, piece in enumerate(pieces):
            place[b * size : (b + 1) * size] = piece[...]

    return place


def forward_kernel(mix, taken, pieces, waits, sums, emits, flag, *refs):
    rows, refs = refs[:pieces], refs[pieces:]
    sources, refs = regrouped(refs, taken)
    refs = refs[waits:]
    hidden, slope = refs[:2]
    inputs = joined(rows, refs[-1])
    block = [mix(flag[0], *[loaded(source, k) for source in sources]).astype(bf16) for k in range(2 if sums or emits else 1)]
    if emits:
        for k in range(2):
            refs[2 + sums][k] = block[k]
    j = pl.program_id(0)
    value, slope_val = gelu_pair(jnp.dot(inputs[...], block[0], preferred_element_type=f32))
    value = value.astype(bf16)
    hidden[...] = value
    slope[...] = slope_val.astype(bf16)
    if sums:
        partials, total = refs[2 : 2 + sums], refs[-2]
        out = lax.dot_general(value, block[1], (((1,), (1,)), ((), ())), preferred_element_type=f32)

        @pl.when(j == 0)
        def _():
            total[...] = out

        @pl.when(j > 0)
        def _():
            total[...] += out

        @pl.when(j == pl.num_programs(0) - 1)
        def _():
            size = partials[0].shape[0]
            for b, partial in enumerate(partials):
                partial[...] = total[b * size : (b + 1) * size].astype(bf16)


def forward(flag, inputs, sources, mix, sums, emits=True, waits=()):
    count, width = inputs[0].shape
    rows = count * len(inputs)
    units = sources[0].shape[2]
    block = min(units, 512)
    parts = 2 if sums or emits else 1
    counts, flat = flattened(sources)
    unit_spec = pl.BlockSpec((rows, block), lambda j: (0, j))
    shapes = [((rows, units), unit_spec), ((rows, units), unit_spec)]
    if sums:
        shapes += [((rows // sums, width), whole((rows // sums, width)))] * sums
    shapes += [(sources[0].shape, block_of(sources[0], block))] * emits
    return pl.pallas_call(
        functools.partial(forward_kernel, mix, counts, len(inputs), len(waits), sums, emits),
        grid=(units // block,),
        in_specs=[pl.BlockSpec(memory_space=pltpu.SMEM)]
        + [whole(piece.shape) for piece in inputs]
        + [block_of(part, block, parts) for part in flat]
        + [ANY] * len(waits),
        out_specs=[spec for _, spec in shapes],
        out_shape=[jax.ShapeDtypeStruct(shape, bf16) for shape, _ in shapes],
        scratch_shapes=[pltpu.VMEM((rows, width), f32)] * bool(sums) + [pltpu.VMEM((rows, width), bf16)],
        compiler_params=pltpu.CompilerParams(vmem_limit_bytes=56 << 20),
        cost_estimate=LIGHT,
    )(flag, *inputs, *flat, *waits)


def only(flag, weights):
    return weights


def pushed(flag, weights, first, second):
    return weights - 0.5 * learn_rate * (first + second)


def halved(flag, known, sent):
    return known + 0.5 * sent


def backward_kernel(update, taken, pieces, given, by_core, flag, weights, slope, hidden, *refs):
    states, refs = regrouped(refs, taken)
    error_count, input_count = pieces
    errors, inputs = refs[:error_count], refs[error_count : error_count + input_count]
    error, error_t, rows, inputs_t = refs[-4:]
    refs = refs[error_count + input_count : -4]
    results, _ = regrouped(refs[len(refs) - sum(given) :], given)
    error, rows = joined(errors, error), joined(inputs, rows)

    @pl.when(pl.program_id(0) == 0)
    def _():
        error_t[...] = error[...].T
        inputs_t[...] = rows[...].T

    back = jnp.dot(error[...], weights[0].astype(bf16), preferred_element_type=f32) * slope[...].astype(f32)
    for k, (left, right) in enumerate(((inputs_t[...], back.astype(bf16)), (error_t[...], hidden[...]))):
        grad = jnp.dot(left, right, preferred_element_type=f32)
        values = update(flag[0], grad, *[loaded(state, k) for state in states])
        for result, apart, value in zip(results, by_core, values):
            if type(result) is not tuple:
                result[k] = value.astype(result.dtype)
                continue
            if apart:
                for place, piece in enumerate(result):

                    @pl.when((flag[0] == k) == (place == 0))
                    def _():
                        piece[...] = value.astype(piece.dtype)

                continue
            each = len(result) // 2
            for i, piece in enumerate(result[k * each : (k + 1) * each]):
                size = piece.shape[0]
                piece[...] = value[i * size : (i + 1) * size].astype(piece.dtype)


def backward(flag, errors, weights, slope, hidden, inputs, states, update, kinds, waits=()):
    rows, width = hidden.shape[0], weights.shape[1]
    units = weights.shape[2]
    block = min(units, 512)
    counts, flat = flattened(states)
    kinds = [kind if type(kind) is tuple else (kind, 1) for kind in kinds]
    by_core = [count == "core" for _, count in kinds]
    kinds = [(kind, 2 if apart else count) for (kind, count), apart in zip(kinds, by_core)]
    shapes = []
    for kind, count in kinds:
        shape = weights.shape if count == 1 else (2 * width // count, units)
        shapes += [jax.ShapeDtypeStruct(shape, kind)] * count
    results = pl.pallas_call(
        functools.partial(
            backward_kernel, update, counts, (len(errors), len(inputs)), [count for _, count in kinds], by_core
        ),
        grid=(units // block,),
        in_specs=[
            pl.BlockSpec(memory_space=pltpu.SMEM),
            pl.BlockSpec((1, width, block), lambda j: (1, 0, j)),
            pl.BlockSpec((rows, block), lambda j: (0, j)),
            pl.BlockSpec((rows, block), lambda j: (0, j)),
        ]
        + [block_of(part, block) for part in flat]
        + [whole(piece.shape) for piece in (*errors, *inputs)]
        + [ANY] * len(waits),
        out_specs=[block_of(shape, block) for shape in shapes],
        out_shape=shapes,
        scratch_shapes=[pltpu.VMEM((rows, width), bf16), pltpu.VMEM((width, rows), bf16)] * 2,
        compiler_params=pltpu.CompilerParams(vmem_limit_bytes=56 << 20),
        cost_estimate=LIGHT,
    )(flag, weights, slope, hidden, *flat, *errors, *inputs, *waits)
    return regrouped(results, [count for _, count in kinds])[0]


def first_update(core, grad, moment):
    moment = inner_beta * moment + grad
    return (moment, moment)


def first_beside(core, grad, moment, own_moment, weights):
    moment = inner_beta * moment + grad
    return (moment, weights - 0.5 * learn_rate * (own_moment + moment))


def second_update(core, grad, moment, weights):
    moment_new = inner_beta * moment + grad
    return (moment_new, weights - learn_rate * moment_new, moment + (1.0 + inner_beta) * moment_new)


def second_beside(core, grad, moment, weights, own):
    found = weights - learn_rate * (inner_beta * moment + grad)
    return (0.5 * jnp.where(core == 0, own, own + found),)


def third_update(core, grad, moment, known):
    return (inner_beta * moment + grad, known + grad)


def rounded(value):
    return lax.reduce_precision(value, 8, 7).astype(bf16)


def added(left, right):
    return rounded(left.astype(f32) + right.astype(f32))


def nothing(*refs):
    pass


def tied(waits, block):
    return pl.pallas_call(
        nothing,
        in_specs=[ANY] * (1 + len(waits)),
        out_specs=ANY,
        out_shape=jax.ShapeDtypeStruct(block.shape, block.dtype),
        input_output_aliases={0: 0},
        cost_estimate=LIGHT,
    )(block, *waits)


def finish_kernel(replicas, flag, slow, anchor, own, theirs, *refs):
    anchor_new, slow_new, token = refs[-3:]
    for k in range(2):
        total = jnp.where(flag[0] == k, own[...].astype(f32), theirs[...].astype(f32))
        value = slow_beta * slow[k] + total / replicas
        slow_new[k] = value
        anchor_new[k] = anchor[k] - learn_rate * value
    token[...] = jnp.zeros_like(token)


def finish(flag, replicas, slow, anchor, own, theirs, position, before):
    size, units = own.shape
    steps = 2
    rows = pl.BlockSpec((2, size // steps, units), lambda j: (0, position * steps + j, 0))
    part = pl.BlockSpec((size // steps, units), lambda j: (j, 0))
    shape = jax.ShapeDtypeStruct(slow.shape, f32)
    return pl.pallas_call(
        functools.partial(finish_kernel, replicas),
        grid=(steps,),
        in_specs=[pl.BlockSpec(memory_space=pltpu.SMEM), rows, rows, part, part] + [ANY] * len(before),
        out_specs=[rows, rows, whole((8, 128))],
        out_shape=[shape, shape, jax.ShapeDtypeStruct((8, 128), bf16)],
        input_output_aliases={5 + k: k for k in range(len(before))},
        compiler_params=pltpu.CompilerParams(vmem_limit_bytes=60 << 20),
        cost_estimate=LIGHT,
    )(flag, slow, anchor, own, theirs, *before)


def slow_step(flag, mine, other, slow, anchor):
    axis, cores = "replica", 2
    index = lax.axis_index(axis)
    replicas = lax.axis_size(axis)
    chip = index // cores
    length = replicas // cores
    half = length // 2
    rows = mine.shape[0]
    size = rows // chunks

    def moved(part, hops):
        return lax.ppermute(part, axis, [(cores * a + c, cores * b + c) for a, b in hops for c in range(cores)])

    def at(places):
        return functools.reduce(jnp.logical_or, [chip == place for place in places])

    stages = [(True, [(s, s + 1), (length - 1 - s, length - 2 - s)]) for s in range(half - 1)]
    if half:
        stages.append((True, [(half - 1, half), (half, half - 1)]))
    stages += [(False, [(s + 1, s), (length - 2 - s, length - 1 - s)]) for s in reversed(range(half - 1))]

    pair_rows = rows // 2
    pairs = [swapped(other[p * pair_rows : (p + 1) * pair_rows], axis, 1) for p in range(2)]
    blocks = []
    for c in range(chunks):
        p, start = divmod(c * size, pair_rows)
        blocks.append(added(mine[c * size : (c + 1) * size], pairs[p][start : start + size]))
    arrived, made, results, tokens = {}, {}, [], []
    final = len(stages) - 1
    for tick in range(chunks + len(stages)):
        for s in reversed(range(len(stages) + 1)):
            c = tick - s
            if not 0 <= c < chunks:
                continue
            block = blocks[c]
            if s:
                adds, hops = stages[s - 1]
                fresh = added(block, arrived[s - 1, c]) if adds else arrived[s - 1, c]
                block = jnp.where(at([b for _, b in hops]), fresh, block)
                if s > final and 0 < c < chunks - 1:
                    block = tied([tokens[c - 1]], block)
            if s == 0 and c >= 3 and (2, c - 3) in made:
                block = tied([made[2, c - 3]], block)
            blocks[c] = made[s, c] = block
            if s < len(stages):
                arrived[s, c] = moved(block, stages[s][1])
            else:
                theirs = swapped(block, axis, 1)
                *results, token = finish(flag, replicas, slow, anchor, block, theirs, c, results)
                tokens.append(token)
    return results


def body(tokens, targets, row_ids, anchor, momentum, slow):
    row_count = tokens.shape[0]
    scale = 1.0 / row_count
    tensors = lax.axis_size("tensor")
    share_rows = row_count // tensors
    order = lax.axis_index("tensor") ^ jnp.arange(tensors)
    picks_all = row_ids[0].reshape(INNER, tensors, share_rows)[:, order].reshape(INNER, row_count)

    replicas = lax.axis_size("replica")
    flag = (lax.axis_index("replica") % 2).astype(jnp.int32).reshape(1)

    def gathered(own):
        return [own] + [swapped(own, "tensor", m) for m in range(1, tensors)]

    def error_share(partials, step):
        wanted = targets.at[picks_all[step, :share_rows]].get(mode="promise_in_bounds")
        share = partials[0].astype(f32)
        for m in range(1, tensors):
            share = share + swapped(partials[m], "tensor", m).astype(f32)
        return ((share - wanted.astype(f32)) * scale).astype(bf16)

    def sent(block, distance, which=(0, 1)):
        route = [((i - distance) % replicas, i) for i in range(replicas) if i % 2 in which]
        return lax.ppermute(block, "replica", route)

    def picked(step, count):
        return tokens.at[picks_all[step, :count]].get(mode="promise_in_bounds")

    near_share = sent(picked(0, share_rows), 1)
    narrow = tied([near_share], momentum[0].astype(bf16))
    moment_near = sent(narrow, 1)
    inputs_near = gathered(near_share)

    inputs = [picked(0, row_count)]
    hidden, slope, *partials = forward(flag, inputs, [anchor], only, tensors, emits=False, waits=[narrow])
    partials[1] = tied(inputs_near[1:], partials[1])
    hidden_near, slope_near = forward(flag, inputs_near, [anchor], only, 0, emits=False)
    inputs_next = picked(1, row_count)
    own_error = jnp.where(flag[0] < 2, error_share(partials, 0), inputs_next[:share_rows] + hidden_near[:1, :1])
    error = jnp.concatenate(gathered(own_error))
    error_near = sent(error, 1)
    moment, moment_bf = backward(
        flag,
        [error],
        anchor,
        slope,
        hidden,
        inputs,
        [momentum[0]],
        first_update,
        [f32, (bf16, 2)],
    )
    moment_far = [sent(tied([error_near, hidden_near], part), 2, (0,)) for part in moment_bf]
    moment_near, weights = backward(
        flag,
        [error_near],
        anchor,
        slope_near,
        hidden_near,
        inputs_near,
        [moment_near, moment, anchor],
        first_beside,
        [(bf16, 2), bf16],
    )

    inputs = [tied([moment_near[0]], inputs_next)]
    inputs_far = sent(inputs[0], 2, (1,))
    hidden, slope, *partials = forward(flag, inputs, [weights], only, tensors, emits=False)
    error = jnp.concatenate(gathered(error_share(partials, 1)))
    error_far = sent(error, 2, (1,))
    moment, weights, known = backward(
        flag,
        [error],
        weights,
        slope,
        hidden,
        inputs,
        [moment, weights],
        second_update,
        [f32, bf16, bf16],
    )
    weights = tied([error_far, inputs_far, *moment_far], weights)
    weights_sent = sent(weights, 2, (0,))
    moment_two = tuple(sent(tied([weights], part), 1, (1,)) for part in moment_near)
    moment_three = tuple(sent(tied([weights], part), 1, (1,)) for part in moment_far)
    hidden, slope, weights_far = forward(flag, [inputs_far], [anchor, moment_two, moment_three], pushed, 0)
    (weights_known,) = backward(
        flag,
        [error_far],
        weights_far,
        slope,
        hidden,
        [inputs_far],
        [moment_two, weights_far, weights],
        second_beside,
        [bf16],
    )

    inputs = [picked(2, row_count)]
    hidden, slope, *rest = forward(flag, inputs, [weights_known, weights_sent], halved, tensors)
    errors = gathered(error_share(rest[:tensors], 2))
    moment, total = backward(
        flag, errors, rest[tensors], slope, hidden, inputs, [moment, known], third_update, [f32, (bf16, "core")]
    )
    anchor_new, slow_new = slow_step(flag, *total, slow, anchor)
    return (anchor_new, slow_new, moment[None])


def solution(mesh):
    return jax.shard_map(
        body,
        mesh=mesh,
        in_specs=(
            P("replica", None),
            P("replica", None),
            P("replica", None, None),
            P(None, None, "tensor"),
            P("replica", None, None, "tensor"),
            P(None, None, "tensor"),
        ),
        out_specs=(
            P(None, None, "tensor"),
            P(None, None, "tensor"),
            P("replica", None, None, "tensor"),
        ),
        check_vma=False,
    )
```
